32 devices in a mesh: items: 4 (over y, x), lat: 8 (over z, core).
Axes of the slice: x: 2, y: 2, z: 4, core: 2. Of those that a mesh axis runs over, the one named last changes fastest.
Arguments:
- latents: float32 [4, 8, 512, 1024], P('items', None, 'lat'), may hold values from -6 to 6
- pixels: bfloat16 [4, 6144, 261], P('items', 'lat'), may hold values from -6 to 6
- lengths: int32 [4, 8], P('items'), may hold values from 1 to 5376, as said below
- out_grad: float32 [4, 8, 512, 1024], P('items', None, 'lat'), may hold values from -6 to 6
- latent_gain: float32 [1024], replicated, may hold values from 0.1 to 1.9
- latent_shift: float32 [1024], replicated, may hold values from -1.5 to 1.5
- pixel_gain: float32 [261], replicated, may hold values from 0.1 to 1.9
- pixel_shift: float32 [261], replicated, may hold values from -1.5 to 1.5
- query_weight: bfloat16 [1024, 1024], replicated, may hold values from -0.4375 to 0.4375
- key_weight: bfloat16 [261, 1024], replicated, may hold values from -0.375 to 0.375
- value_weight: bfloat16 [261, 1024], replicated, may hold values from -0.375 to 0.375
- out_weight: bfloat16 [1024, 1024], replicated, may hold values from -0.75 to 0.75
- cross_gain: float32 [1024], replicated, may hold values from 0.1 to 1.9
- cross_shift: float32 [1024], replicated, may hold values from -1.5 to 1.5
- cross_up: bfloat16 [1024, 1024], replicated, may hold values from -0.1875 to 0.1875
- cross_down: bfloat16 [1024, 1024], replicated, may hold values from -0.1875 to 0.1875
- self_gain: float32 [1024], replicated, may hold values from 0.1 to 1.9
- self_shift: float32 [1024], replicated, may hold values from -1.5 to 1.5
- self_packed: bfloat16 [1024, 3072], replicated, may hold values from -0.25 to 0.25
- self_out: bfloat16 [1024, 1024], replicated, may hold values from -0.5 to 0.5
- final_gain: float32 [1024], replicated, may hold values from 0.1 to 1.9
- final_shift: float32 [1024], replicated, may hold values from -1.5 to 1.5
- latent_up: bfloat16 [1024, 1024], replicated, may hold values from -0.1875 to 0.1875
- latent_down: bfloat16 [1024, 1024], replicated, may hold values from -0.1875 to 0.1875
Outputs:
- result: float32 [4, 8, 512, 1024], P('items', None, 'lat')
- grad_latents: float32 [4, 8, 512, 1024], P('items', None, 'lat')
- grad_pixels: float32 [4, 6144, 261], P('items', 'lat')
- grad_latent_gain: float32 [1024], P('lat')
- grad_latent_shift: float32 [1024], P('lat')
- grad_pixel_gain: float32 [261], replicated
- grad_pixel_shift: float32 [261], replicated
- grad_query_weight: float32 [1024, 1024], P('lat')
- grad_key_weight: float32 [261, 1024], P(None, 'lat')
- grad_value_weight: float32 [261, 1024], P(None, 'lat')
- grad_out_weight: float32 [1024, 1024], P('lat')
- grad_cross_gain: float32 [1024], P('lat')
- grad_cross_shift: float32 [1024], P('lat')
- grad_cross_up: float32 [1024, 1024], P('lat')
- grad_cross_down: float32 [1024, 1024], P('lat')
- grad_self_gain: float32 [1024], P('lat')
- grad_self_shift: float32 [1024], P('lat')
- grad_self_packed: float32 [1024, 3072], P('lat')
- grad_self_out: float32 [1024, 1024], P('lat')
- grad_final_gain: float32 [1024], P('lat')
- grad_final_shift: float32 [1024], P('lat')
- grad_latent_up: float32 [1024, 1024], P('lat')
- grad_latent_down: float32 [1024, 1024], P('lat')
The draws below stay inside these ranges and needn't reach their ends.
Inputs may be any that keep to these rules, and one draw needn't show every extreme that they name: In each group the 8 images lie one after another in its 6144 pixel rows, so their lengths sum to 6144. Exactly one image of each group, never the first or the last, is 5376 rows long; it starts within the group's first 768 rows and ends within its last 768 rows. The other images together hold 768 rows.
All inputs are finite; a program needn't handle non-finite values.
Results may differ from the reference program's by a relative error of at most 0.02615.
The reference program's roundings to bfloat16 on the way count: a program that leaves them out, or rounds other values in their place, can miss the bound.
Values may be sent and summed in bfloat16 or wider, within the bound.
No kernel may reach another device: no remote copies, remote signals or barrier semaphores. Data moves between devices by JAX's collectives and lax.ppermute only.
A program may use at most 384 MiB of HBM per device.

```python
import math
import jax
import jax.numpy as jnp
from jax import lax

D = 1024
CIN = 261
LATENTS = 512
HEADS = 8
HEAD = 128
HID = 1024
IPG = 8
PIX_DEV = 768
GROUPS = 4
PIX_GROUP = 6144
MOST = 5376


def draw_lengths(key, part):
    key = jax.random.fold_in(key, 11)

    def one_group(group_index):
        group_key = jax.random.fold_in(key, group_index)
        cut_key, place_key = jax.random.split(group_key)
        chosen = jax.random.permutation(cut_key, PIX_DEV - 1)[:IPG - 2].astype(jnp.int32) + 1
        cuts = jnp.sort(chosen)
        edges = jnp.concatenate([jnp.zeros((1,), jnp.int32), cuts, jnp.full((1,), PIX_DEV, jnp.int32)])
        others = edges[1:] - edges[:-1]
        place = jax.random.randint(place_key, (), 1, IPG - 1).astype(jnp.int32)
        slots = jnp.arange(IPG, dtype=jnp.int32)
        before = others[jnp.clip(slots, 0, IPG - 2)]
        after = others[jnp.clip(slots - 1, 0, IPG - 2)]
        longest = jnp.full((IPG,), MOST, jnp.int32)
        return jnp.where(slots < place, before, jnp.where(slots == place, longest, after)).astype(jnp.int32)
    return jax.vmap(one_group)(jnp.arange(GROUPS, dtype=jnp.int32))


def steps_of(stream_key, shape, cuts, least, top_value):
    loudness, own = 1.0, jax.random.fold_in(stream_key, 6)
    for axis_at, shards_of in cuts:
        draws = jnp.exp(jax.random.uniform(jax.random.fold_in(own, axis_at), (shards_of,), jnp.float32, least / len(cuts), top_value / len(cuts)))
        loudness = loudness * jnp.repeat(draws, shape[axis_at] // shards_of).reshape([-1 if axis == axis_at else 1 for axis in range(len(shape))])
    return loudness


def noise(own_key, dims, deviation, most, shards=(), kind=jnp.bfloat16):
    entries = jax.random.normal(own_key, dims, jnp.float32) * deviation
    if len(shards) > 0:
        entries = steps_of(own_key, dims, shards, -0.22, 0.18) * entries
    return jnp.clip(entries, min=-most, max=most).astype(kind)


def setup_inputs(seed: int = 0) -> dict:
    keys = jax.random.split(jax.random.key(seed), 25)
    return {
        "latents": noise(keys[0], (GROUPS, IPG, LATENTS, D), 1.0, 6.0, ((0, 4), (2, 8)), jnp.float32),
        "pixels": noise(keys[1], (GROUPS, PIX_GROUP, CIN), 1.0, 6.0, ((0, 4), (1, 8))),
        "lengths": draw_lengths(jax.random.fold_in(keys[24], 71), 0),
        "out_grad": noise(keys[3], (GROUPS, IPG, LATENTS, D), 1.0, 6.0, ((0, 4), (2, 8)), jnp.float32),
        "latent_gain": jnp.clip(1.0 + 0.18 * jax.random.normal(keys[4], (D,), jnp.float32), 0.1, 1.9),
        "latent_shift": noise(keys[5], (D,), 0.3, 1.5, (), jnp.float32),
        "pixel_gain": jnp.clip(1.0 + 0.18 * jax.random.normal(keys[6], (CIN,), jnp.float32), 0.1, 1.9),
        "pixel_shift": noise(keys[7], (CIN,), 0.3, 1.5, (), jnp.float32),
        "query_weight": noise(keys[8], (D, D), (D // 6) ** -0.5, 0.4375),
        "key_weight": noise(keys[9], (CIN, D), CIN ** -0.5, 0.375),
        "value_weight": noise(keys[10], (CIN, D), CIN ** -0.5, 0.375),
        "out_weight": noise(keys[11], (D, D), (D // 16) ** -0.5, 0.75),
        "cross_gain": jnp.clip(1.0 + 0.18 * jax.random.normal(keys[12], (D,), jnp.float32), 0.1, 1.9),
        "cross_shift": noise(keys[13], (D,), 0.3, 1.5, (), jnp.float32),
        "cross_up": noise(keys[14], (D, HID), D ** -0.5, 0.1875),
        "cross_down": noise(keys[15], (HID, D), HID ** -0.5, 0.1875),
        "self_gain": jnp.clip(1.0 + 0.18 * jax.random.normal(keys[16], (D,), jnp.float32), 0.1, 1.9),
        "self_shift": noise(keys[17], (D,), 0.3, 1.5, (), jnp.float32),
        "self_packed": noise(keys[18], (D, 3 * D), (D // 2) ** -0.5, 0.25),
        "self_out": noise(keys[19], (D, D), (D // 8) ** -0.5, 0.5),
        "final_gain": jnp.clip(1.0 + 0.18 * jax.random.normal(keys[20], (D,), jnp.float32), 0.1, 1.9),
        "final_shift": noise(keys[21], (D,), 0.3, 1.5, (), jnp.float32),
        "latent_up": noise(keys[22], (D, HID), D ** -0.5, 0.1875),
        "latent_down": noise(keys[23], (HID, D), HID ** -0.5, 0.1875),
    }


@jax.custom_vjp
def low(v):
    return lax.optimization_barrier(v.astype(jnp.bfloat16)).astype(jnp.float32)

@jax.custom_vjp
def low_back(v):
    return v

def low_keep(v):
    return (low(v), None)

def low_pass(kept, grad):
    return (grad,)

def back_keep(v):
    return (v, None)

def back_low(kept, grad):
    return (low(grad),)
low.defvjp(low_keep, low_pass)
low_back.defvjp(back_keep, back_low)

def rounded_both(value):
    return low(low_back(value))

def layer_norm(values, gain_vec, shift_vec):
    centre = values - lax.optimization_barrier(jnp.mean(values, axis=-1, keepdims=True))
    spread = lax.optimization_barrier(jnp.mean(centre * centre, axis=-1, keepdims=True))
    return centre * lax.rsqrt(spread + 1e-05) * gain_vec + shift_vec

def matmul(left, right):
    return jnp.dot(left, right, precision=lax.Precision.HIGHEST)

def reference(latents, pixels, lengths, out_grad, latent_gain, latent_shift, pixel_gain, pixel_shift, query_weight, key_weight, value_weight, out_weight, cross_gain, cross_shift, cross_up, cross_down, self_gain, self_shift, self_packed, self_out, final_gain, final_shift, latent_up, latent_down):
    groups = latents.shape[0]
    starts = (jnp.cumsum(lengths, axis=1) - lengths).astype(jnp.int32).reshape(-1)
    item_spans = lengths.astype(jnp.int32).reshape(-1)
    group_of_item = (jnp.arange(groups * IPG, dtype=jnp.int32) // IPG).astype(jnp.int32)
    score_scale = 1.0 / math.sqrt(D)
    head_scale = 1.0 / math.sqrt(HEAD)

    def forward(latent_rows, pixel_rows, latent_gain, latent_shift, pixel_gain, pixel_shift, query_weight, key_weight, value_weight, out_weight, cross_gain, cross_shift, cross_up, cross_down, self_gain, self_shift, self_packed, self_out, final_gain, final_shift, latent_up, latent_down):
        residual = latent_rows.reshape(-1, D)
        normed = low(layer_norm(residual, latent_gain, latent_shift))
        queries = rounded_both(matmul(normed, query_weight)).reshape(groups * IPG, LATENTS, D)
        pix_normed = low(layer_norm(pixel_rows, pixel_gain, pixel_shift)).reshape(-1, CIN)
        pixel_keys = rounded_both(matmul(pix_normed, key_weight)).reshape(groups, PIX_GROUP, D)
        pixel_values = rounded_both(matmul(pix_normed, value_weight)).reshape(groups, PIX_GROUP, D)

        def cross_item(operands):
            query_block, group_index, item_start, item_span = operands
            window_start = jnp.minimum(item_start, PIX_GROUP - MOST).astype(jnp.int32)
            zero_index = jnp.zeros((), jnp.int32)
            key_block = lax.dynamic_slice(pixel_keys, (group_index, window_start, zero_index), (1, MOST, D))[0]
            value_block = lax.dynamic_slice(pixel_values, (group_index, window_start, zero_index), (1, MOST, D))[0]
            places = window_start + jnp.arange(MOST, dtype=jnp.int32)
            inside = (places >= item_start) & (places < item_start + item_span)
            scores = low_back(matmul(query_block, key_block.T) * score_scale)
            masked = jnp.where(inside[None, :], scores, -1e+30)
            row_peak = lax.optimization_barrier(jnp.max(masked, axis=-1, keepdims=True))
            weights = jnp.exp(masked - row_peak)
            weights = weights / lax.optimization_barrier(jnp.sum(weights, axis=-1, keepdims=True))
            return matmul(low(weights), value_block)
        cross_mixed = lax.map(jax.checkpoint(cross_item), (queries, group_of_item, starts, item_spans))
        cross_mixed = rounded_both(cross_mixed).reshape(-1, D)
        first_sum = residual + low_back(matmul(cross_mixed, out_weight))
        cross_normed = low(layer_norm(first_sum, cross_gain, cross_shift))
        cross_hidden = low_back(matmul(cross_normed, cross_up))
        cross_active = low(jax.nn.gelu(cross_hidden))
        second_sum = first_sum + low_back(matmul(cross_active, cross_down))
        self_normed = low(layer_norm(second_sum, self_gain, self_shift))
        packed = rounded_both(matmul(self_normed, self_packed)).reshape(groups * IPG, LATENTS, 3, HEADS, HEAD)

        def self_item(item_block):
            scores = low_back(jnp.einsum('qhd,khd->hqk', item_block[:, 0], item_block[:, 1], precision=lax.Precision.HIGHEST) * head_scale)
            row_peak = lax.optimization_barrier(jnp.max(scores, axis=-1, keepdims=True))
            weights = jnp.exp(scores - row_peak)
            weights = weights / lax.optimization_barrier(jnp.sum(weights, axis=-1, keepdims=True))
            return jnp.einsum('hqk,khd->qhd', low(weights), item_block[:, 2], precision=lax.Precision.HIGHEST)
        self_mixed = lax.map(jax.checkpoint(self_item), packed)
        self_mixed = rounded_both(self_mixed).reshape(-1, D)
        third_sum = second_sum + low_back(matmul(self_mixed, self_out))
        final_normed = low(layer_norm(third_sum, final_gain, final_shift))
        final_hidden = low_back(matmul(final_normed, latent_up))
        final_active = low(jax.nn.gelu(final_hidden))
        result = third_sum + low_back(matmul(final_active, latent_down))
        return result.reshape(groups, IPG, LATENTS, D)
    arguments = (latents.astype(jnp.float32), pixels.astype(jnp.float32), latent_gain, latent_shift, pixel_gain, pixel_shift, query_weight.astype(jnp.float32), key_weight.astype(jnp.float32), value_weight.astype(jnp.float32), out_weight.astype(jnp.float32), cross_gain, cross_shift, cross_up.astype(jnp.float32), cross_down.astype(jnp.float32), self_gain, self_shift, self_packed.astype(jnp.float32), self_out.astype(jnp.float32), final_gain, final_shift, latent_up.astype(jnp.float32), latent_down.astype(jnp.float32))
    result, pullback = jax.vjp(forward, *arguments)
    gradients = pullback(out_grad.astype(jnp.float32))
    return (result, gradients[0], gradients[1], gradients[2], gradients[3], gradients[4], gradients[5], gradients[6], gradients[7], gradients[8], gradients[9], gradients[10], gradients[11], gradients[12], gradients[13], gradients[14], gradients[15], gradients[16], gradients[17], gradients[18], gradients[19], gradients[20], gradients[21])
```

```python
import math

import jax
import jax.numpy as jnp
from jax import lax
from jax.sharding import PartitionSpec as P

HEADS = 8
HEAD = 128
BF = jnp.bfloat16
F32 = jnp.float32


def norm_parts(values, axis=-1):
    centre = values - jnp.mean(values, axis=axis, keepdims=True)
    spread = jnp.mean(centre * centre, axis=axis, keepdims=True)
    inv = lax.rsqrt(spread + 1e-05)
    return centre * inv, inv


def layer_norm(values, gain, shift):
    hat, unused = norm_parts(values)
    return hat * gain + shift


def norm_back(values, gain, upstream):
    hat, inv = norm_parts(values)
    scaled = upstream * gain
    back = inv * (
        scaled
        - jnp.mean(scaled, axis=-1, keepdims=True)
        - hat * jnp.mean(scaled * hat, axis=-1, keepdims=True)
    )
    return back, jnp.sum(upstream * hat, axis=0), jnp.sum(upstream, axis=0)


def gelu_back(hidden, upstream):
    unused, pullback = jax.vjp(jax.nn.gelu, hidden)
    return pullback(upstream)[0]


def dot(left, right):
    return jnp.dot(left, right, preferred_element_type=F32)


def dot_tn(left, right):
    return lax.dot_general(left, right, (((0,), (0,)), ((), ())), preferred_element_type=F32)


def dot_nt(left, right):
    return lax.dot_general(left, right, (((1,), (1,)), ((), ())), preferred_element_type=F32)


def softmax(scores):
    raised = jnp.exp(scores - jnp.max(scores, axis=-1, keepdims=True))
    return raised / jnp.sum(raised, axis=-1, keepdims=True)


def on_device(
    latents,
    pixels,
    lengths,
    out_grad,
    latent_gain,
    latent_shift,
    pixel_gain,
    pixel_shift,
    query_weight,
    key_weight,
    value_weight,
    out_weight,
    cross_gain,
    cross_shift,
    cross_up,
    cross_down,
    self_gain,
    self_shift,
    self_packed,
    self_out,
    final_gain,
    final_shift,
    latent_up,
    latent_down,
):
    items = latents.shape[1]
    lat_rows = latents.shape[2]
    width = latents.shape[3]
    pix_rows = pixels.shape[1]
    cin = pixels.shape[2]
    ways = lax.axis_size("lat")
    groups = lax.axis_size("items")
    sub = ways // items
    rows = items * lat_rows
    piece = lat_rows // sub
    score_scale = 1.0 / math.sqrt(width)
    head_scale = 1.0 / math.sqrt(HEAD)
    lat_index = lax.axis_index("lat")
    core = lat_index % 2

    spans = lengths[0]
    starts = jnp.cumsum(spans) - spans
    largest = jnp.argmax(spans).astype(jnp.int32)
    places = jnp.arange(pix_rows * ways, dtype=jnp.int32)
    owner = jnp.sum((places[:, None] >= starts[None, :]).astype(jnp.int32), axis=1) - 1

    pix = pixels[0].T.astype(F32)
    pix_hat, pix_inv = norm_parts(pix, 0)
    pn = (pix_hat * pixel_gain[:, None] + pixel_shift[:, None]).astype(BF)
    pn_all = lax.all_gather(pn, "lat", axis=0, tiled=False)
    whole = pn_all.transpose(1, 0, 2).reshape(cin, ways * pix_rows)
    edge = jnp.concatenate([pn_all[0], pn_all[ways - 1]], axis=1)
    edge_owner = jnp.concatenate([owner[:pix_rows], owner[-pix_rows:]])

    to_pixels = (dot_nt(query_weight, key_weight) * score_scale).astype(BF)
    from_pixels = dot(value_weight, out_weight).astype(BF)

    residual = latents.reshape(rows, width)
    upstream = out_grad.reshape(rows, width)
    normed = layer_norm(residual, latent_gain, latent_shift).astype(BF)
    asks = dot(normed, to_pixels).astype(BF)
    row_item = jnp.arange(rows, dtype=jnp.int32) // lat_rows

    small_mask = (edge_owner[None, :] == row_item[:, None]) & (row_item != largest)[:, None]
    small_scores = jnp.where(small_mask, dot(asks, edge), -1e30)
    small_weights = jnp.where(small_mask, softmax(small_scores), 0.0)
    large_asks = lax.dynamic_slice_in_dim(asks, largest * lat_rows, lat_rows, 0)
    large_scores = jnp.where((owner == largest)[None, :], dot(large_asks, whole), -1e30)
    large_weights = softmax(large_scores)
    small_low = small_weights.astype(BF)
    large_low = large_weights.astype(BF)
    mixed = lax.dynamic_update_slice_in_dim(
        dot_nt(small_low, edge), dot_nt(large_low, whole), largest * lat_rows, 0
    )
    mixed_low = mixed.astype(BF)
    first_sum = residual + dot(mixed_low, from_pixels)
    cross_normed = layer_norm(first_sum, cross_gain, cross_shift).astype(BF)
    cross_hidden = dot(cross_normed, cross_up)
    cross_active = jax.nn.gelu(cross_hidden).astype(BF)
    second_sum = first_sum + dot(cross_active, cross_down)

    def to_items(values):
        moved = lax.all_to_all(
            values.astype(BF).reshape(ways, piece, width), "lat", split_axis=0, concat_axis=0, tiled=True
        )
        return moved.reshape(rows, width)

    def from_items(values):
        moved = lax.all_to_all(
            values.astype(BF).reshape(ways, piece, width), "lat", split_axis=0, concat_axis=0, tiled=True
        )
        return moved.reshape(rows, width).astype(F32)

    second = to_items(second_sum).astype(F32)
    grad_low = to_items(upstream)
    self_normed = layer_norm(second, self_gain, self_shift).astype(BF)
    packed = dot(self_normed, self_packed).astype(BF)
    queries = packed[:, :width].reshape(rows, HEADS, HEAD)
    pairs = packed[:, width:]
    if sub > 1:
        same_item = [[i * sub + s for s in range(sub)] for i in range(items)]
        pairs = lax.all_gather(pairs, "lat", axis=0, tiled=True, axis_index_groups=same_item)
    keys = pairs[:, :width].reshape(-1, HEADS, HEAD)
    values = pairs[:, width:].reshape(-1, HEADS, HEAD)
    self_weights = softmax(
        jnp.einsum("qhd,khd->hqk", queries, keys, preferred_element_type=F32) * head_scale
    )
    self_low = self_weights.astype(BF)
    self_mixed = (
        jnp.einsum("hqk,khd->qhd", self_low, values, preferred_element_type=F32)
        .astype(BF)
        .reshape(rows, width)
    )
    self_add = dot(self_mixed, self_out)
    third = second + self_add
    final_normed = layer_norm(third, final_gain, final_shift).astype(BF)
    final_hidden = dot(final_normed, latent_up)
    final_active = jax.nn.gelu(final_hidden).astype(BF)
    result = second_sum + from_items(self_add + dot(final_active, latent_down))

    grad_latent_down = dot_tn(final_active, grad_low)
    grad_final_hidden = gelu_back(final_hidden, dot_nt(grad_low, latent_down)).astype(BF)
    grad_latent_up = dot_tn(final_normed, grad_final_hidden)
    back_third, grad_final_gain, grad_final_shift = norm_back(
        third, final_gain, dot_nt(grad_final_hidden, latent_up)
    )
    grad_third_low = (grad_low.astype(F32) + back_third).astype(BF)
    grad_self_out = dot_tn(self_mixed, grad_third_low)
    grad_mixed = dot_nt(grad_third_low, self_out).astype(BF).reshape(rows, HEADS, HEAD)
    grad_weights = jnp.einsum("qhd,khd->hqk", grad_mixed, values, preferred_element_type=F32)
    grad_values = jnp.einsum("hqk,qhd->khd", self_low, grad_mixed, preferred_element_type=F32)
    spread = self_weights * (
        grad_weights - jnp.sum(self_weights * grad_weights, axis=-1, keepdims=True)
    )
    spread_low = (spread * head_scale).astype(BF)
    grad_queries = jnp.einsum("hqk,khd->qhd", spread_low, keys, preferred_element_type=F32)
    grad_keys = jnp.einsum("hqk,qhd->khd", spread_low, queries, preferred_element_type=F32)
    grad_pairs = jnp.concatenate(
        [grad_keys.reshape(-1, width), grad_values.reshape(-1, width)], axis=1
    ).astype(BF)
    if sub > 1:
        grad_pairs = lax.psum_scatter(
            grad_pairs, "lat", scatter_dimension=0, tiled=True, axis_index_groups=same_item
        )
    grad_packed = jnp.concatenate([grad_queries.reshape(rows, width).astype(BF), grad_pairs], axis=1)
    grad_self_packed = dot_tn(self_normed, grad_packed)
    back_second, grad_self_gain, grad_self_shift = norm_back(
        second, self_gain, dot_nt(grad_packed, self_packed)
    )
    grad_second = upstream + from_items(back_third + back_second)

    grad_second_low = grad_second.astype(BF)
    grad_cross_down = dot_tn(cross_active, grad_second_low)
    grad_cross_hidden = gelu_back(cross_hidden, dot_nt(grad_second_low, cross_down)).astype(BF)
    grad_cross_up = dot_tn(cross_normed, grad_cross_hidden)
    back_first, grad_cross_gain, grad_cross_shift = norm_back(
        first_sum, cross_gain, dot_nt(grad_cross_hidden, cross_up)
    )
    grad_first = grad_second + back_first
    grad_first_low = grad_first.astype(BF)
    grad_mixed_low = dot_nt(grad_first_low, from_pixels).astype(BF)
    value_core = dot_tn(mixed_low, grad_first_low)
    deltas = jnp.sum(grad_mixed_low.astype(F32) * mixed, axis=-1, keepdims=True)
    large_grad = lax.dynamic_slice_in_dim(grad_mixed_low, largest * lat_rows, lat_rows, 0)
    large_deltas = lax.dynamic_slice_in_dim(deltas, largest * lat_rows, lat_rows, 0)
    small_spread = (small_weights * (dot(grad_mixed_low, edge) - deltas)).astype(BF)
    large_spread = (large_weights * (dot(large_grad, whole) - large_deltas)).astype(BF)
    moves = lax.dynamic_update_slice_in_dim(
        dot_nt(small_spread, edge), dot_nt(large_spread, whole), largest * lat_rows, 0
    ).astype(BF)
    small_pix = dot_tn(asks, small_spread) + dot_tn(grad_mixed_low, small_low)
    large_pix = dot_tn(large_asks, large_spread) + dot_tn(large_grad, large_low)
    large_pix = large_pix.reshape(cin, ways, pix_rows).transpose(1, 0, 2)
    parts_pix = large_pix.at[0].add(small_pix[:, :pix_rows]).at[ways - 1].add(small_pix[:, pix_rows:])
    grad_pn = lax.psum_scatter(
        parts_pix.astype(BF), "lat", scatter_dimension=0, tiled=False
    ).astype(F32)
    grad_pixel_gain = jnp.sum(grad_pn * pix_hat, axis=1)
    grad_pixel_shift = jnp.sum(grad_pn, axis=1)
    scaled = grad_pn * pixel_gain[:, None]
    grad_pixels = pix_inv * (
        scaled
        - jnp.mean(scaled, axis=0, keepdims=True)
        - pix_hat * jnp.mean(scaled * pix_hat, axis=0, keepdims=True)
    )
    query_core = dot_tn(normed, moves)
    back_zero, grad_latent_gain, grad_latent_shift = norm_back(
        residual, latent_gain, dot_nt(moves, to_pixels)
    )
    grad_latents = grad_first + back_zero

    half = ways // 2
    swap = [(i, i ^ 1) for i in range(ways)]
    same_core = [list(range(0, ways, 2)), list(range(1, ways, 2))]

    def reduce_weights(*grads):
        whole_grad = jnp.concatenate([grad.astype(BF) for grad in grads], axis=1)
        columns = whole_grad.shape[1]
        blocks = whole_grad.reshape(half, 2, width // ways, columns)
        mine = lax.dynamic_index_in_dim(blocks, core, 1, keepdims=False)
        other = lax.dynamic_index_in_dim(blocks, 1 - core, 1, keepdims=False)
        got = lax.ppermute(other, "lat", swap)
        both = (mine.astype(F32) + got.astype(F32)).astype(BF)
        both = both.reshape(half, groups, width // ways // groups, columns)
        over_items = lax.psum_scatter(both, "items", scatter_dimension=1, tiled=False)
        over_chips = lax.psum_scatter(
            over_items, "lat", scatter_dimension=0, tiled=False, axis_index_groups=same_core
        )
        return lax.all_gather(over_chips, "items", axis=0, tiled=True).astype(F32)

    first_three = reduce_weights(grad_latent_down, grad_latent_up, grad_self_out)
    grad_latent_down, grad_latent_up, grad_self_out = jnp.split(first_three, 3, axis=1)
    grad_self_packed = reduce_weights(grad_self_packed)
    grad_cross_down, grad_cross_up = jnp.split(
        reduce_weights(grad_cross_down, grad_cross_up), 2, axis=1
    )

    everywhere = ("items", "lat")
    value_core = lax.psum(value_core.astype(BF), everywhere)
    query_core = lax.psum(query_core.astype(BF), everywhere)
    block = width // ways
    low_at = lat_index * block
    query_rows = lax.dynamic_slice_in_dim(query_core, low_at, block, 0)
    grad_query_weight = dot(query_rows, key_weight) * score_scale
    grad_key_weight = (
        dot_tn(query_core, lax.dynamic_slice_in_dim(query_weight, low_at, block, 1)) * score_scale
    )
    grad_value_weight = dot_nt(value_core, lax.dynamic_slice_in_dim(out_weight, low_at, block, 0))
    grad_out_weight = dot_tn(lax.dynamic_slice_in_dim(value_weight, low_at, block, 1), value_core)

    vectors = jnp.concatenate(
        [
            grad_latent_gain,
            grad_latent_shift,
            grad_cross_gain,
            grad_cross_shift,
            grad_self_gain,
            grad_self_shift,
            grad_final_gain,
            grad_final_shift,
            grad_pixel_gain,
            grad_pixel_shift,
        ]
    )
    vectors = jnp.sum(lax.all_gather(vectors, "lat"), axis=0)
    vectors = jnp.sum(lax.all_gather(vectors, "items"), axis=0)
    gains = lax.dynamic_slice_in_dim(vectors[: 8 * width].reshape(8, width), low_at, block, 1)
    grad_pixel_gain = vectors[8 * width : 8 * width + cin]
    grad_pixel_shift = vectors[8 * width + cin :]
    shape = (1, items, lat_rows, width)
    return (
        result.reshape(shape),
        grad_latents.reshape(shape),
        grad_pixels.T[None],
        gains[0],
        gains[1],
        grad_pixel_gain,
        grad_pixel_shift,
        grad_query_weight,
        grad_key_weight,
        grad_value_weight,
        grad_out_weight,
        gains[2],
        gains[3],
        grad_cross_up,
        grad_cross_down,
        gains[4],
        gains[5],
        grad_self_packed,
        grad_self_out,
        gains[6],
        gains[7],
        grad_latent_up,
        grad_latent_down,
    )


def solution(mesh):
    rows = P("items", None, "lat", None)
    in_specs = (rows, P("items", "lat", None), P("items", None), rows) + (P(),) * 20
    lane = P("lat")
    tall = P("lat", None)
    wide = P(None, "lat")
    out_specs = (
        rows,
        rows,
        P("items", "lat", None),
        lane,
        lane,
        P(),
        P(),
        tall,
        wide,
        wide,
        tall,
        lane,
        lane,
        tall,
        tall,
        lane,
        lane,
        tall,
        tall,
        lane,
        lane,
        tall,
        tall,
    )
    return jax.shard_map(
        on_device, mesh=mesh, in_specs=in_specs, out_specs=out_specs, check_vma=False
    )
```

```python
import math

import jax
import jax.numpy as jnp
from jax import lax
from jax.experimental import pallas as pl
from jax.experimental.pallas import tpu as pltpu
from jax.sharding import PartitionSpec as P

HEADS = 8
HEAD = 128
X_FIRST = (1, 3, 0, 2)
Y_FIRST = (2, 3, 0, 1)
BF = jnp.bfloat16
F32 = jnp.float32


def norm_parts(values, axis=-1):
    centre = values - jnp.mean(values, axis=axis, keepdims=True)
    spread = jnp.mean(centre * centre, axis=axis, keepdims=True)
    inv = lax.rsqrt(spread + 1e-05)
    return centre * inv, inv


def layer_norm(values, gain, shift):
    hat, unused = norm_parts(values)
    return hat * gain + shift


def norm_back(values, gain, upstream):
    hat, inv = norm_parts(values)
    scaled = upstream * gain
    back = inv * (
        scaled
        - jnp.mean(scaled, axis=-1, keepdims=True)
        - hat * jnp.mean(scaled * hat, axis=-1, keepdims=True)
    )
    return back, jnp.sum(upstream * hat, axis=0), jnp.sum(upstream, axis=0)


def gelu_back(hidden, upstream):
    unused, pullback = jax.vjp(jax.nn.gelu, hidden)
    return pullback(upstream)[0]


def dot(left, right):
    return jnp.dot(left, right, preferred_element_type=F32)


def dot_tn(left, right):
    return lax.dot_general(left, right, (((0,), (0,)), ((), ())), preferred_element_type=F32)


def dot_nt(left, right):
    return lax.dot_general(left, right, (((1,), (1,)), ((), ())), preferred_element_type=F32)


def softmax(scores):
    raised = jnp.exp(scores - jnp.max(scores, axis=-1, keepdims=True))
    return raised / jnp.sum(raised, axis=-1, keepdims=True)


def attend_kernel(query, key, value, out, kept):
    scores = dot_nt(query[...], key[...]) * (1.0 / math.sqrt(HEAD))
    raised = jnp.exp(scores - jnp.max(scores, axis=-1, keepdims=True))
    weights = (raised * (1.0 / jnp.sum(raised, axis=-1, keepdims=True))).astype(BF)
    kept[0] = weights
    out[...] = dot(weights, value[...]).astype(BF)


def attend(queries, pairs, rows, whole_rows):
    column = lambda at: pl.BlockSpec((whole_rows, HEAD), lambda h: (0, h + at))
    own = pl.BlockSpec((rows, HEAD), lambda h: (0, h))
    return pl.pallas_call(
        attend_kernel,
        grid=(HEADS,),
        in_specs=[own, column(0), column(HEADS)],
        out_specs=[own, pl.BlockSpec((1, rows, whole_rows), lambda h: (h, 0, 0))],
        out_shape=[
            jax.ShapeDtypeStruct((rows, HEADS * HEAD), BF),
            jax.ShapeDtypeStruct((HEADS, rows, whole_rows), BF),
        ],
        compiler_params=pltpu.CompilerParams(vmem_limit_bytes=40 << 20),
        name="attend",
    )(queries, pairs, pairs)


def attend_back_kernel(grad, weights_ref, query, key, value, grad_query, grad_pair):
    at = pl.multiple_of(pl.program_id(0) * HEAD, HEAD)
    also = pl.multiple_of(pl.program_id(0) * HEAD + HEADS * HEAD, HEAD)
    weights_low = weights_ref[0]
    weights = weights_low.astype(F32)
    upstream = grad[...]
    grad_weights = dot_nt(upstream, value[...])
    grad_pair[:, pl.ds(also, HEAD)] = dot_tn(weights_low, upstream).astype(BF)
    inner = jnp.sum(weights * grad_weights, axis=-1, keepdims=True)
    spread = (weights * (grad_weights - inner)).astype(BF)
    scale = 1.0 / math.sqrt(HEAD)
    grad_query[...] = (dot(spread, key[...]) * scale).astype(BF)
    grad_pair[:, pl.ds(at, HEAD)] = (dot_tn(spread, query[...]) * scale).astype(BF)


def attend_back(grad, weights, queries, pairs, rows, whole_rows):
    column = lambda at: pl.BlockSpec((whole_rows, HEAD), lambda h: (0, h + at))
    own = pl.BlockSpec((rows, HEAD), lambda h: (0, h))
    return pl.pallas_call(
        attend_back_kernel,
        grid=(HEADS,),
        in_specs=[
            own,
            pl.BlockSpec((1, rows, whole_rows), lambda h: (h, 0, 0)),
            own,
            column(0),
            column(HEADS),
        ],
        out_specs=[own, pl.BlockSpec((whole_rows, 2 * HEADS * HEAD), lambda h: (0, 0))],
        out_shape=[
            jax.ShapeDtypeStruct((rows, HEADS * HEAD), BF),
            jax.ShapeDtypeStruct((whole_rows, 2 * HEADS * HEAD), BF),
        ],
        compiler_params=pltpu.CompilerParams(vmem_limit_bytes=40 << 20),
        name="attend_back",
    )(grad, weights, queries, pairs, pairs)


def half_columns(left, half, blocks):
    step = left.shape[1] // (2 * blocks)
    return jnp.concatenate(
        [left[:, pl.ds(pl.multiple_of((2 * z + half) * step, step), step)] for z in range(blocks)], axis=1
    ).T


def half_kernel(count, blocks, place, *refs):
    lefts, rights, added = refs[:count], refs[count : 2 * count], refs[2 * count]
    sent, kept, turned = refs[2 * count + 1 :]
    step = pl.program_id(0)

    @pl.when(step == 0)
    def start():
        for at, left in enumerate(lefts):
            turned[at] = half_columns(left, place[0], blocks)

    at = 0
    for index, right in enumerate(rights):
        size = right.shape[1]
        value = dot(turned[index], right[...]) + added[0, :, at : at + size].astype(F32)
        value = value.astype(BF)

        @pl.when(step < 2)
        def send():
            sent[0, :, at : at + size] = value

        @pl.when(step >= 2)
        def keep():
            kept[0, :, at : at + size] = value

        at += size


def half_plain(pairs, half, item, order, ways):
    blocks = ways // 2
    rows, width = pairs[0][0].shape
    groups = len(order)
    outs = []
    for left, right in pairs:
        columns = lax.dynamic_index_in_dim(
            left.reshape(rows, blocks, 2, width // ways), half, 2, keepdims=False
        ).reshape(rows, width // 2)
        value = dot_tn(columns, right).reshape(width // 2, groups, -1).transpose(1, 0, 2)
        outs.append(value)
    value = jnp.concatenate(outs, axis=2)
    return jnp.stack([lax.dynamic_index_in_dim(value, item ^ m, 0, keepdims=False) for m in order])


def half_grads(pairs, half, item, order, ways, added):
    rows, width = pairs[0][0].shape
    blocks, groups = ways // 2, len(order)
    total = sum(right.shape[1] for unused, right in pairs) // groups
    if (width // ways) % 128:
        value = (half_plain(pairs, half, item, order, ways) + added.astype(F32)).astype(BF)
        return value[:2], value[2:]
    return pl.pallas_call(
        lambda place, *refs: half_kernel(len(pairs), blocks, place, *refs),
        grid_spec=pltpu.PrefetchScalarGridSpec(
            num_scalar_prefetch=1,
            grid=(groups,),
            in_specs=[pl.BlockSpec((rows, width), lambda g, place: (0, 0)) for unused in pairs]
            + [
                pl.BlockSpec((rows, right.shape[1] // groups), lambda g, place: (0, place[1 + g]))
                for unused, right in pairs
            ]
            + [pl.BlockSpec((1, width // 2, total), lambda g, place: (g, 0, 0))],
            out_specs=[
                pl.BlockSpec((1, width // 2, total), lambda g, place: (jnp.minimum(g, 1), 0, 0)),
                pl.BlockSpec((1, width // 2, total), lambda g, place: (jnp.maximum(g - 2, 0), 0, 0)),
            ],
            scratch_shapes=[pltpu.VMEM((len(pairs), width // 2, rows), BF)],
        ),
        out_shape=[jax.ShapeDtypeStruct((2, width // 2, total), BF)] * 2,
        compiler_params=pltpu.CompilerParams(vmem_limit_bytes=40 << 20),
        name="half_grads",
    )(
        jnp.stack([half] + [item ^ m for m in order]).astype(jnp.int32),
        *[left for left, unused in pairs],
        *[right for unused, right in pairs],
        added,
    )


def last_kernel(
    place, moves, core_in, residual, grad_first, gain, core_value, out_w, normed, queries,
    vectors, pixel_sums, grad_latents, mine, other, stacked, rest,
):
    rows, width = residual.shape
    block = mine.shape[2] // 2
    chips = width // block // 2
    channels = moves.shape[1]
    stacked[...] = jnp.zeros(stacked.shape, F32)

    def back(part):
        grad_normed = dot_nt(moves[part, :], core_in[...])
        hat, inv = norm_parts(residual[part, :])
        stacked[0:1, :] += jnp.sum(grad_normed * hat, axis=0, keepdims=True)
        stacked[1:2, :] += jnp.sum(grad_normed, axis=0, keepdims=True)
        grad_latents[part, :] = grad_first[part, :] + norm_slope(hat, inv, gain[...], grad_normed)

    each_part(rows, back)
    stacked[8:16, :] = vectors[...]
    for at in range(2):
        line = jnp.broadcast_to(pixel_sums[at], (channels, 128)).T[0:1, :]
        line = jnp.concatenate([line, jnp.zeros((1, -channels % 128), F32)], axis=1)
        for k in range(line.shape[1] // 128):
            for j in range(width // block):
                stacked[2 + 3 * at + k : 3 + 3 * at + k, j * block : j * block + 128] = line[
                    :, k * 128 : (k + 1) * 128
                ]
    rest[0:channels, :] = dot_nt(core_value[...], out_w[...]).astype(BF)
    rest[channels : 2 * channels, :] = dot_tn(moves[...], normed[...]).astype(BF)
    rest[2 * channels : 3 * channels, :] = dot_tn(moves[...], queries[...]).astype(BF)
    rest[3 * channels :, :] = stacked[...].astype(BF)
    size = rest.shape[0] // 4
    for p, m in enumerate(Y_FIRST):
        lines = pl.ds(pl.multiple_of((place[1] ^ m) * size, 16), size)
        for out, core in ((mine, place[0]), (other, 1 - place[0])):
            for z in range(chips):
                lanes = pl.ds(pl.multiple_of((2 * z + core) * block, block), block)
                out[p, z // 2 * size : (z // 2 + 1) * size, z % 2 * block : (z % 2 + 1) * block] = rest[
                    lines, lanes
                ]


def small_lines(channels):
    return 3 * channels + 16


def last_block(
    core, item, ways, moves, core_in, residual, grad_first, gain, core_value, out_w, normed, queries,
    vectors, pixel_sums,
):
    rows, width = residual.shape
    channels = moves.shape[1]
    block, chips = width // ways, ways // 2
    total = small_lines(channels)
    if block % 128:
        grad_normed = dot_nt(moves, core_in)
        back, grad_gain, grad_shift = norm_back(residual, gain[0], grad_normed)
        sums = jnp.pad(pixel_sums.reshape(2, channels), ((0, 0), (0, -channels % block)))
        lines = sums.reshape(-1, 1, block)
        lines = jnp.broadcast_to(lines, (lines.shape[0], ways, block)).reshape(-1, width)
        stack = [
            dot_nt(core_value, out_w),
            dot_tn(moves, normed),
            dot_tn(moves, queries),
            grad_gain[None],
            grad_shift[None],
            lines,
            vectors,
        ]
        count = sum(value.shape[0] for value in stack)
        stack = jnp.concatenate(stack + [jnp.zeros((-count % 64, width), F32)]).astype(BF)
        size = stack.shape[0] // 4
        stack = stack.reshape(4, size, chips // 2, 2, 2, block)
        halves = []
        for half in (core, 1 - core):
            value = lax.dynamic_index_in_dim(stack, half, 4, keepdims=False)
            value = value.transpose(0, 2, 1, 3, 4).reshape(4, chips // 2 * size, 2 * block)
            halves.append(
                jnp.stack([lax.dynamic_index_in_dim(value, item ^ m, 0, keepdims=False) for m in Y_FIRST])
            )
        return grad_first + back, halves[0], halves[1]
    vmem = pl.BlockSpec(memory_space=pltpu.VMEM)
    half = jax.ShapeDtypeStruct((4, chips // 2 * (total // 4), 2 * block), BF)
    return pl.pallas_call(
        last_kernel,
        in_specs=[pl.BlockSpec(memory_space=pltpu.SMEM)] + [vmem] * 11,
        out_specs=[vmem] * 3,
        out_shape=[jax.ShapeDtypeStruct((rows, width), F32), half, half],
        scratch_shapes=[pltpu.VMEM((16, width), F32), pltpu.VMEM((total, width), BF)],
        compiler_params=pltpu.CompilerParams(vmem_limit_bytes=50 << 20),
        name="last_block",
    )(
        jnp.stack([core, item]).astype(jnp.int32), moves, core_in, residual, grad_first, gain, core_value,
        out_w, normed, queries, vectors, pixel_sums,
    )


GELU_A = 0.044715
GELU_C = math.sqrt(2.0 / math.pi)
PART = 256


def gelu_both(hidden):
    square = hidden * hidden
    bent = jnp.tanh(hidden * (GELU_C + (GELU_C * GELU_A) * square))
    half = 0.5 + 0.5 * bent
    slope = half + (0.5 * hidden) * (1.0 - bent * bent) * (GELU_C + (3.0 * GELU_C * GELU_A) * square)
    return hidden * half, slope


def norm_slope(hat, inv, gain, upstream):
    scaled = upstream * gain
    centre = jnp.mean(scaled, axis=-1, keepdims=True)
    along = jnp.mean(scaled * hat, axis=-1, keepdims=True)
    return inv * (scaled - centre - hat * along)


def each_part(rows, body):
    size = min(PART, rows)

    def step(r, carry):
        body(pl.ds(pl.multiple_of(r * size, size), size))
        return carry

    lax.fori_loop(0, rows // size, step, 0)


def each_head(body):
    def step(h, carry):
        body(h)
        return carry

    lax.fori_loop(0, HEADS, step, 0)


def write_halves(pairs, outs, item, order, blocks, turned):
    at = 0
    for left, right in pairs:
        size = right.shape[1] // len(order)
        for out, half in outs:
            turned[...] = half_columns(left, half, blocks)
            for p, m in enumerate(order):
                lanes = pl.ds(pl.multiple_of((item ^ m) * size, HEAD), size)
                out[p, :, at : at + size] = dot(turned[...], right[:, lanes]).astype(BF)
        at += size


def item_body(place, near, made, extra, need, flush):
    second, vectors, packed_w0, packed_w1, packed_w2, out_w, up_w, down_w, grad_low = near
    (
        self_normed, self_mixed, final_normed, final_active, result_add, grad_final_hidden, grad_third_low,
        second_add, grad_packed, sums, other_first, other_packed,
    ) = made
    packed, raised_low, inverse, mixed, back_third, grad_mixed, turned = extra
    packed_w = (packed_w0, packed_w1, packed_w2)
    rows, width = second.shape
    need(0, 1)
    sums[...] = jnp.zeros(sums.shape, F32)

    def normalize(part):
        hat, unused = norm_parts(second[part, :].astype(F32))
        self_normed[part, :] = (hat * vectors[0:1, :] + vectors[1:2, :]).astype(BF)

    each_part(rows, normalize)
    flush(0)
    for c in range(3):
        need(2 + c)

        def project(part):
            packed[part, c * width : (c + 1) * width] = dot(
                self_normed[part, :], packed_w[c][...]
            ).astype(BF)

        each_part(rows, project)

    def lanes(h, group):
        return pl.ds(pl.multiple_of(h * HEAD + group * width, HEAD), HEAD)

    scale = 1.0 / math.sqrt(HEAD)

    def attend_head(h):
        scores = dot_nt(packed[:, lanes(h, 0)], packed[:, lanes(h, 1)])
        peak = jnp.max(scores, axis=-1, keepdims=True)
        raised = jnp.exp2((scores - peak) * (scale * math.log2(math.e)))
        inv = 1.0 / jnp.sum(raised, axis=-1, keepdims=True)
        low = raised.astype(BF)
        raised_low[h] = low
        inverse[h] = inv
        mixed[:, lanes(h, 0)] = dot(low, packed[:, lanes(h, 2)]) * inv

    each_head(attend_head)
    need(5, 6, 7, 8)

    def middle(part):
        low = mixed[part, :].astype(BF)
        self_mixed[part, :] = low
        added = dot(low, out_w[...])
        hat, inv = norm_parts(second[part, :].astype(F32) + added)
        normed = (hat * vectors[2:3, :] + vectors[3:4, :]).astype(BF)
        final_normed[part, :] = normed
        active, slope = gelu_both(dot(normed, up_w[...]))
        active = active.astype(BF)
        final_active[part, :] = active
        result_add[part, :] = (added + dot(active, down_w[...])).astype(BF)
        upstream = grad_low[part, :]
        grad_hidden = (dot_nt(upstream, down_w[...]) * slope).astype(BF)
        grad_final_hidden[part, :] = grad_hidden
        grad_normed = dot_nt(grad_hidden, up_w[...])
        sums[2:3, :] += jnp.sum(grad_normed * hat, axis=0, keepdims=True)
        sums[3:4, :] += jnp.sum(grad_normed, axis=0, keepdims=True)
        back = norm_slope(hat, inv, vectors[2:3, :], grad_normed)
        back_third[part, :] = back
        third_low = (upstream.astype(F32) + back).astype(BF)
        grad_third_low[part, :] = third_low
        grad_mixed[part, :] = dot_nt(third_low, out_w[...]).astype(BF)

    each_part(rows, middle)
    flush(1, 2, 3, 4, 5, 6)

    def attend_back_head(h):
        upstream = grad_mixed[:, lanes(h, 0)]
        low = raised_low[h]
        inv = inverse[h]
        up32 = upstream.astype(F32)
        inner = jnp.sum(up32 * mixed[:, lanes(h, 0)], axis=-1, keepdims=True)
        grad_packed[:, lanes(h, 2)] = dot_tn(low, (up32 * inv).astype(BF)).astype(BF)
        grad_weights = dot_nt(upstream, packed[:, lanes(h, 2)])
        spread = (low.astype(F32) * ((grad_weights - inner) * (inv * scale))).astype(BF)
        grad_packed[:, lanes(h, 0)] = dot(spread, packed[:, lanes(h, 1)]).astype(BF)
        grad_packed[:, lanes(h, 1)] = dot_tn(spread, packed[:, lanes(h, 0)]).astype(BF)

    each_head(attend_back_head)
    flush(8)

    def last(part):
        hat, inv = norm_parts(second[part, :].astype(F32))
        grad_normed = dot_nt(grad_packed[part, :width], packed_w[0][...])
        for c in range(1, 3):
            grad_normed += dot_nt(grad_packed[part, c * width : (c + 1) * width], packed_w[c][...])
        sums[0:1, :] += jnp.sum(grad_normed * hat, axis=0, keepdims=True)
        sums[1:2, :] += jnp.sum(grad_normed, axis=0, keepdims=True)
        back = norm_slope(hat, inv, vectors[0:1, :], grad_normed)
        second_add[part, :] = (back_third[part, :] + back).astype(BF)

    each_part(rows, last)
    flush(7, 9)
    blocks = width // 2 // HEAD
    write_halves(
        ((final_active, grad_low), (final_normed, grad_final_hidden), (self_mixed, grad_third_low)),
        ((other_first, 1 - place[0]),), place[1], X_FIRST, blocks, turned,
    )
    flush(10)
    write_halves(
        ((self_normed, grad_packed),), ((other_packed, 1 - place[0]),), place[1], Y_FIRST, blocks, turned
    )


def item_block(place, groups, second, grad_low, vectors, self_packed, self_out, latent_up, latent_down):
    rows, width = second.shape
    low = jax.ShapeDtypeStruct((rows, width), BF)
    half = jax.ShapeDtypeStruct((groups, width // 2, 3 * width // groups), BF)
    packed_parts = [(self_packed, c * width, width) for c in range(3)]
    (
        self_normed, self_mixed, final_normed, final_active, result_add, grad_final_hidden, grad_third_low,
        second_add, grad_packed, sums, other_first, other_packed,
    ) = streamed(
        "item_block",
        item_body,
        place,
        [second, vectors, *packed_parts, self_out, latent_up, latent_down, grad_low],
        [low] * 8
        + [
            jax.ShapeDtypeStruct((rows, 3 * width), BF),
            jax.ShapeDtypeStruct((4, width), F32),
            half,
            half,
        ],
        [
            pltpu.VMEM((rows, 3 * width), BF),
            pltpu.VMEM((HEADS, rows, rows), BF),
            pltpu.VMEM((HEADS, rows, 1), F32),
            pltpu.VMEM((rows, width), F32),
            pltpu.VMEM((rows, width), F32),
            pltpu.VMEM((rows, width), BF),
            pltpu.VMEM((width // 2, rows), BF),
        ],
    )
    return (
        result_add, second_add, self_normed, grad_packed, self_mixed, grad_third_low,
        final_normed, final_active, grad_final_hidden, sums, other_first, other_packed,
    )


def streamed(name, body, place, ins, outs, scratch):
    cuts = [value[1:] if isinstance(value, tuple) else None for value in ins]
    ins = [value[0] if isinstance(value, tuple) else value for value in ins]
    shapes = [value.shape if cut is None else (value.shape[0], cut[1]) for value, cut in zip(ins, cuts)]
    anywhere = pl.BlockSpec(memory_space=pl.ANY)

    def kernel(place_ref, *refs):
        sources, refs = refs[: len(ins)], refs[len(ins) :]
        targets, refs = refs[: len(outs)], refs[len(outs) :]
        near, refs = refs[: len(ins)], refs[len(ins) :]
        made, refs = refs[: len(outs)], refs[len(outs) :]
        extra, (in_sems, out_sems) = refs[:-2], refs[-2:]
        sources = [ref if cut is None else ref.at[:, pl.ds(*cut)] for ref, cut in zip(sources, cuts)]
        loads = [pltpu.make_async_copy(a, b, in_sems.at[i]) for i, (a, b) in enumerate(zip(sources, near))]
        stores = [pltpu.make_async_copy(a, b, out_sems.at[i]) for i, (a, b) in enumerate(zip(made, targets))]
        left_in, left_out = list(range(len(ins))), list(range(len(outs)))
        for load in loads:
            load.start()

        def need(*which):
            for i in which:
                left_in.remove(i)
                loads[i].wait()

        def flush(*which):
            for i in which:
                left_out.remove(i)
                stores[i].start()

        body(place_ref, near, made, extra, need, flush)
        need(*list(left_in))
        flush(*list(left_out))
        for store in stores:
            store.wait()

    return pl.pallas_call(
        kernel,
        in_specs=[pl.BlockSpec(memory_space=pltpu.SMEM)] + [anywhere] * len(ins),
        out_specs=[anywhere] * len(outs),
        out_shape=list(outs),
        scratch_shapes=[pltpu.VMEM(shape, value.dtype) for shape, value in zip(shapes, ins)]
        + [pltpu.VMEM(value.shape, value.dtype) for value in outs]
        + list(scratch)
        + [pltpu.SemaphoreType.DMA((len(ins),)), pltpu.SemaphoreType.DMA((len(outs),))],
        compiler_params=pltpu.CompilerParams(vmem_limit_bytes=60 << 20),
        name=name,
    )(place, *ins)


def pixel_hat(values, cin):
    real = lax.broadcasted_iota(jnp.int32, (values.shape[0], 1), 0) < cin
    portion = 1.0 / cin.astype(F32)
    centre = jnp.where(real, values - jnp.sum(values, axis=0, keepdims=True) * portion, 0.0)
    return centre * lax.rsqrt(jnp.sum(centre * centre, axis=0, keepdims=True) * portion + 1e-05)


def each_block(count, body):
    def step(n, carry):
        body(n)
        return carry

    lax.fori_loop(0, count, step, 0)


def cross_body(place, near, made, extra, need, flush):
    asks, gain, shift, raw, owner, core_out, residual, vectors, up_w, down_w = near
    (
        normal, scores, kept, mixed, top, first_sum, cross_normed, slopes, cross_active, second_sum, second
    ) = made
    (heap,) = extra
    ways, channels, size = normal.shape
    rows = asks.shape[0]
    lat_rows = heap.shape[0]
    at = pl.multiple_of(place[2] * lat_rows, lat_rows)
    large = pl.ds(at, lat_rows)
    need(0, 1, 2, 3)
    columns = lax.broadcasted_iota(jnp.int32, (1, size), 1)
    top[...] = jnp.full(top.shape, -1e30, F32)

    def score(n):
        value = (pixel_hat(raw[n].astype(F32), place[3]) * gain[...] + shift[...]).astype(BF)
        normal[n] = value
        places = columns + n * size
        found = dot(asks[large, :], value)
        found = jnp.where((places >= place[0]) & (places < place[1]), found, -1e30)
        scores[n] = found
        top[...] = jnp.maximum(top[...], jnp.max(found, axis=1, keepdims=True))

    each_block(ways, score)
    flush(0, 1)
    need(4)
    edge = jnp.where(
        columns < place[0], normal[0].astype(F32), normal[ways - 1].astype(F32)
    ).astype(BF)
    row_item = lax.broadcasted_iota(jnp.int32, (rows, 1), 0) // lat_rows
    inside = (owner[...] == row_item) & (place[2] != row_item)
    found = jnp.where(inside, dot(asks[...], edge), -1e30)
    raised = jnp.exp(found - jnp.max(found, axis=1, keepdims=True))
    weights = raised * (1.0 / jnp.sum(raised, axis=1, keepdims=True))
    weights = jnp.where(inside, weights, 0.0).astype(BF)
    kept[...] = weights
    mixed[...] = dot_nt(weights, edge)
    heap[...] = jnp.zeros(heap.shape, F32)
    peak = top[...]

    def gather(n, carry):
        raised = jnp.exp(scores[n] - peak)
        heap[...] += dot_nt(raised.astype(BF), normal[n])
        return carry + jnp.sum(raised, axis=1, keepdims=True)

    whole = lax.fori_loop(0, ways, gather, jnp.zeros((lat_rows, 1), F32))
    mixed[large, :] = heap[...] * (1.0 / whole)
    top[...] = peak + jnp.log(whole)
    flush(2, 3, 4)
    need(5, 6, 7, 8, 9)

    def net(part):
        first = residual[part, :] + dot(mixed[part, :].astype(BF), core_out[...])
        first_sum[part, :] = first
        hat, unused = norm_parts(first)
        normed = (hat * vectors[0:1, :] + vectors[1:2, :]).astype(BF)
        cross_normed[part, :] = normed
        active, slope = gelu_both(dot(normed, up_w[...]))
        active = active.astype(BF)
        cross_active[part, :] = active
        slopes[part, :] = slope
        value = first + dot(active, down_w[...])
        second_sum[part, :] = value
        second[part, :] = value.astype(BF)

    each_part(rows, net)


def cross_back_body(place, near, made, extra, need, flush):
    (
        got, upstream, slopes, down_w, up_w, first_sum, vectors, core_out, normal, mixed, kept, asks, scores, top,
        raw, value_w, cross_active, cross_normed,
    ) = near
    grad_second_low, grad_cross_hidden, grad_first, grad_first_low, sums, moves, pix, pixel_sums = made[:8]
    core_value, cross_mixed, *halves = made[8:]
    grad, corner, heap, turned = extra
    ways, channels, size = normal.shape
    rows = asks.shape[0]
    lat_rows = heap.shape[0]
    at = pl.multiple_of(place[2] * lat_rows, lat_rows)
    large = pl.ds(at, lat_rows)
    sums[...] = jnp.zeros(sums.shape, F32)
    pixel_sums[...] = jnp.zeros(pixel_sums.shape, F32)
    need(0, 1, 2, 3, 4, 5, 6, 7)

    def net(part):
        grad_second = upstream[part, :] + got[part, :].astype(F32)
        low = grad_second.astype(BF)
        grad_second_low[part, :] = low
        grad_hidden = (dot_nt(low, down_w[...]) * slopes[part, :]).astype(BF)
        grad_cross_hidden[part, :] = grad_hidden
        grad_normed = dot_nt(grad_hidden, up_w[...])
        hat, inv = norm_parts(first_sum[part, :])
        sums[0:1, :] += jnp.sum(grad_normed * hat, axis=0, keepdims=True)
        sums[1:2, :] += jnp.sum(grad_normed, axis=0, keepdims=True)
        value = grad_second + norm_slope(hat, inv, vectors[0:1, :], grad_normed)
        grad_first[part, :] = value
        low = value.astype(BF)
        grad_first_low[part, :] = low
        grad[part, :] = dot_nt(low, core_out[...]).astype(BF)

    each_part(rows, net)
    flush(0, 1, 2, 3, 4)
    need(8, 9, 10, 11, 12, 13, 14)
    columns = lax.broadcasted_iota(jnp.int32, (1, size), 1)
    early = columns < place[0]
    edge = jnp.where(early, normal[0].astype(F32), normal[ways - 1].astype(F32)).astype(BF)
    deltas = jnp.sum(grad[...].astype(F32) * mixed[...], axis=1, keepdims=True)
    weights = kept[...]
    spread = (weights.astype(F32) * (dot(grad[...], edge) - deltas)).astype(BF)
    moves[...] = dot_nt(spread, edge).astype(BF)
    corner[...] = dot_tn(asks[...], spread) + dot_tn(grad[...], weights)
    heap[...] = jnp.zeros(heap.shape, F32)
    own = grad[large, :]
    own_asks = asks[large, :]
    deltas = jnp.sum(own.astype(F32) * mixed[large, :], axis=1, keepdims=True)
    level = top[...]

    def block(n):
        value = normal[n]
        weights = jnp.exp(scores[n] - level)
        spread = (weights * (dot(own, value) - deltas)).astype(BF)
        heap[...] += dot_nt(spread, value)
        part = dot_tn(own_asks, spread) + dot_tn(own, weights.astype(BF))
        use = ((n == 0) & early) | ((n == ways - 1) & jnp.logical_not(early))
        part = part + jnp.where(use, corner[...], 0.0)
        pix[n] = part.astype(BF)
        hat = pixel_hat(raw[n].astype(F32), place[3])
        pixel_sums[0] += jnp.sum(part * hat, axis=1, keepdims=True)
        pixel_sums[1] += jnp.sum(part, axis=1, keepdims=True)

    each_block(ways, block)
    moves[large, :] = heap[...].astype(BF)
    flush(5, 6, 7)
    need(15, 16, 17)
    mixed_low = mixed[...].astype(BF)
    cross_mixed[...] = dot(mixed_low, value_w[...]).astype(BF)
    core_value[...] = dot_tn(mixed_low, grad_first_low[...]).astype(BF)
    flush(8, 9)
    if halves:
        write_halves(
            ((cross_active, grad_second_low), (cross_normed, grad_cross_hidden)),
            ((halves[0], place[4]), (halves[1], 1 - place[4])), place[5], X_FIRST, ways // 2, turned,
        )
        write_halves(
            ((cross_mixed, grad_first_low),),
            ((halves[2], place[4]), (halves[3], 1 - place[4])), place[5], Y_FIRST, ways // 2, turned,
        )


def cross(place, raw_all, gain, shift, asks, owner, residual, core_out, vectors, up, down, lat_rows):
    ways, channels, size = raw_all.shape
    rows, width = residual.shape
    low = jax.ShapeDtypeStruct((rows, width), BF)
    wide = jax.ShapeDtypeStruct((rows, width), F32)
    (
        normal, scores, kept, mixed, top, first_sum, cross_normed, slopes, cross_active, second_sum, second
    ) = streamed(
        "cross",
        cross_body,
        place,
        [asks, gain, shift, raw_all, owner, core_out, residual, vectors, up, down],
        [
            jax.ShapeDtypeStruct((ways, channels, size), BF),
            jax.ShapeDtypeStruct((ways, lat_rows, size), F32),
            jax.ShapeDtypeStruct((rows, size), BF),
            jax.ShapeDtypeStruct((rows, channels), F32),
            jax.ShapeDtypeStruct((lat_rows, 1), F32),
            wide,
            low,
            wide,
            low,
            wide,
            low,
        ],
        [pltpu.VMEM((lat_rows, channels), F32)],
    )
    return mixed, kept, scores, top, normal, first_sum, second_sum, second, cross_normed, cross_active, slopes


def cross_back(
    place, got, upstream, first_sum, slopes, vectors, core_out, up, down,
    raw_all, normal, asks, mixed, kept, scores, top, cross_active, cross_normed, value_w, groups,
):
    ways, channels, size = raw_all.shape
    rows, width = upstream.shape
    lat_rows = top.shape[0]
    low = jax.ShapeDtypeStruct((rows, width), BF)
    halves = []
    if (width // ways) % 128 == 0:
        halves = [
            jax.ShapeDtypeStruct((groups, width // 2, count * width // groups), BF) for count in (2, 2, 1, 1)
        ]
    return streamed(
        "cross_back",
        cross_back_body,
        place,
        [
            got, upstream, slopes, down, up, first_sum, vectors, core_out, normal, mixed, kept, asks, scores, top,
            raw_all, value_w, cross_active, cross_normed,
        ],
        [
            low,
            low,
            jax.ShapeDtypeStruct((rows, width), F32),
            low,
            jax.ShapeDtypeStruct((2, width), F32),
            jax.ShapeDtypeStruct((rows, channels), BF),
            jax.ShapeDtypeStruct((ways, channels, size), BF),
            jax.ShapeDtypeStruct((2, channels, 1), F32),
            jax.ShapeDtypeStruct((channels, width), BF),
            low,
        ]
        + halves,
        [
            pltpu.VMEM((rows, channels), BF),
            pltpu.VMEM((channels, size), F32),
            pltpu.VMEM((lat_rows, channels), F32),
            pltpu.VMEM((width // 2, rows), BF),
        ],
    )


def on_device(
    latents,
    pixels,
    lengths,
    out_grad,
    latent_gain,
    latent_shift,
    pixel_gain,
    pixel_shift,
    query_weight,
    key_weight,
    value_weight,
    out_weight,
    cross_gain,
    cross_shift,
    cross_up,
    cross_down,
    self_gain,
    self_shift,
    self_packed,
    self_out,
    final_gain,
    final_shift,
    latent_up,
    latent_down,
):
    items = latents.shape[1]
    lat_rows = latents.shape[2]
    width = latents.shape[3]
    pix_rows = pixels.shape[1]
    cin = pixels.shape[2]
    ways = lax.axis_size("lat")
    groups = lax.axis_size("items")
    sub = ways // items
    rows = items * lat_rows
    piece = lat_rows // sub
    score_scale = 1.0 / math.sqrt(width)
    head_scale = 1.0 / math.sqrt(HEAD)
    lat_index = lax.axis_index("lat")
    core = lat_index % 2

    channels = -(-cin // 16) * 16
    pad = ((0, channels - cin), (0, 0))
    spans = lengths[0]
    starts = jnp.cumsum(spans) - spans
    largest = jnp.argmax(spans).astype(jnp.int32)
    large_start = starts[largest]
    place = jnp.stack(
        [
            large_start,
            large_start + spans[largest],
            largest,
            jnp.asarray(cin, jnp.int32),
            core,
            lax.axis_index("items"),
        ]
    ).astype(jnp.int32)
    edge_places = jnp.arange(pix_rows, dtype=jnp.int32)
    edge_places = jnp.where(edge_places < large_start, edge_places, edge_places + pix_rows * (ways - 1))
    owner = jnp.sum((edge_places[None, :] >= starts[:, None]).astype(jnp.int32), axis=0) - 1
    owner = owner[None, :]

    swap = [(i, i ^ 1) for i in range(ways)]
    same_core = [list(range(0, ways, 2)), list(range(1, ways, 2))]
    block = width // ways

    tie = lax.optimization_barrier

    chips = ways // 2
    chip = lat_index // 2
    item = lax.axis_index("items")

    def swap_items(part, m):
        return lax.ppermute(part, "items", [(i, i ^ m) for i in range(groups)])

    def near_chips(pieces):
        if chips != 4:
            whole = jnp.stack([pieces(j) for j in range(chips)])
            moved = lax.all_to_all(
                whole, "lat", split_axis=0, concat_axis=0, tiled=True, axis_index_groups=same_core
            )
            return [moved[j] for j in range(chips)]
        return [pieces(chip)] + [
            lax.ppermute(
                pieces(chip ^ m), "lat", [(i, ((i // 2) ^ m) * 2 + i % 2) for i in range(ways)]
            )
            for m in range(1, chips)
        ]

    def total(parts):
        value = parts[0].astype(F32)
        for part in parts[1:]:
            value = value + part.astype(F32)
        return value

    def add(left, right):
        return (left.astype(F32) + right.astype(F32)).astype(BF)

    def over_chips_whole(here):
        parts = lax.all_to_all(
            here, "lat", split_axis=0, concat_axis=0, tiled=True, axis_index_groups=same_core
        )
        return jnp.sum(parts.astype(F32), axis=0).astype(BF)

    def gather_items(part):
        return jnp.stack([part] + [swap_items(part, m) for m in range(1, groups)])

    def by_item(parts):
        return [lax.dynamic_index_in_dim(parts, item ^ j, 0, keepdims=False) for j in range(groups)]

    def weight_of(parts):
        return jnp.concatenate(by_item(parts), axis=1).astype(F32)

    pixels_low = jnp.pad(pixels[0].T, pad)
    raw_all = lax.all_gather(pixels_low, "lat", axis=0, tiled=False)
    gain_column = jnp.pad(pixel_gain[:, None], pad)
    shift_column = jnp.pad(pixel_shift[:, None], pad)
    key_pad = jnp.pad(key_weight, pad)
    value_pad = jnp.pad(value_weight, pad)

    to_pixels = (dot_nt(query_weight, key_pad) * score_scale).astype(BF)
    from_pixels = dot(value_pad, out_weight).astype(BF)

    residual = latents.reshape(rows, width)
    upstream = out_grad.reshape(rows, width)
    normed = layer_norm(residual, latent_gain, latent_shift).astype(BF)
    asks = dot(normed, to_pixels).astype(BF)
    latent_queries = dot(normed, query_weight).astype(BF)

    def reshare(values):
        moved = lax.all_to_all(
            values.reshape(ways, piece, width), "lat", split_axis=0, concat_axis=0, tiled=True
        )
        return moved.reshape(rows, width)

    (
        raw_all, value_pad, upstream_low, asks, latent_queries, from_pixels, to_pixels, gain_column, shift_column, place, owner
    ) = tie(
        (
            raw_all, value_pad, upstream.astype(BF), asks, latent_queries, from_pixels, to_pixels, gain_column, shift_column,
            place, owner,
        )
    )
    grad_low = reshare(upstream_low)
    cross_vectors = jnp.stack([cross_gain, cross_shift])
    (
        mixed, kept, scores, top, normal, first_sum, second_sum, second, cross_normed, cross_active, slopes
    ) = cross(
        place, raw_all, gain_column, shift_column, asks, owner, residual, from_pixels, cross_vectors,
        cross_up, cross_down, lat_rows,
    )
    second, grad_low = tie((second, grad_low))
    second = reshare(second)
    item_place = jnp.stack([core, item]).astype(jnp.int32)
    item_vectors = jnp.stack([self_gain, self_shift, final_gain, final_shift])
    if sub == 1:
        (
            result_add, second_add, self_normed, grad_packed, self_mixed, grad_third_low,
            final_normed, final_active, grad_final_hidden, item_sums, final_other, packed_other,
        ) = item_block(item_place, groups, second, grad_low, item_vectors, self_packed, self_out, latent_up, latent_down)
    else:
        whole_rows = rows * sub
        same_item = [[i * sub + s for s in range(sub)] for i in range(items)]
        second_wide = second.astype(F32)
        self_normed = layer_norm(second_wide, self_gain, self_shift).astype(BF)
        packed = dot(self_normed, self_packed).astype(BF)
        pairs = lax.all_gather(
            packed[:, width:], "lat", axis=0, tiled=True, axis_index_groups=same_item
        )
        self_mixed, self_low = attend(packed, pairs, rows, whole_rows)
        self_add = dot(self_mixed, self_out)
        third = second_wide + self_add
        final_normed = layer_norm(third, final_gain, final_shift).astype(BF)
        final_hidden = dot(final_normed, latent_up)
        final_active = jax.nn.gelu(final_hidden).astype(BF)
        result_add = (self_add + dot(final_active, latent_down)).astype(BF)
        grad_final_hidden = gelu_back(final_hidden, dot_nt(grad_low, latent_down)).astype(BF)
        back_third, grad_final_gain, grad_final_shift = norm_back(
            third, final_gain, dot_nt(grad_final_hidden, latent_up)
        )
        grad_third_low = (grad_low.astype(F32) + back_third).astype(BF)
        grad_mixed = dot_nt(grad_third_low, self_out).astype(BF)
        grad_queries, grad_pairs = attend_back(grad_mixed, self_low, packed, pairs, rows, whole_rows)
        grad_pairs = lax.psum_scatter(
            grad_pairs, "lat", scatter_dimension=0, tiled=True, axis_index_groups=same_item
        )
        grad_packed = jnp.concatenate([grad_queries, grad_pairs], axis=1)
        back_second, grad_self_gain, grad_self_shift = norm_back(
            second_wide, self_gain, dot_nt(grad_packed, self_packed)
        )
        second_add = (back_third + back_second).astype(BF)
        item_sums = jnp.stack([grad_self_gain, grad_self_shift, grad_final_gain, grad_final_shift])
    second_got = reshare(second_add)
    item_pairs = (
        (final_active, grad_low),
        (final_normed, grad_final_hidden),
        (self_mixed, grad_third_low),
        (self_normed, grad_packed),
    )
    final_pairs, packed_pairs = item_pairs[:3], item_pairs[3:]
    if sub > 1:
        final_other = half_plain(final_pairs, 1 - core, item, X_FIRST, ways).astype(BF)
        packed_other = half_plain(packed_pairs, 1 - core, item, Y_FIRST, ways).astype(BF)
    final_got = lax.ppermute(final_other, "lat", swap)
    packed_got = lax.ppermute(packed_other, "lat", swap)
    final_sent, final_kept = half_grads(final_pairs, core, item, X_FIRST, ways, final_got)
    packed_sent, packed_kept = half_grads(packed_pairs, core, item, Y_FIRST, ways, packed_got)
    second_got, final_sent, packed_sent, result_add = tie((second_got, final_sent, packed_sent, result_add))
    final_got = swap_items(final_sent, 1)
    packed_got = swap_items(packed_sent, 2)
    result_got = reshare(result_add)

    (
        grad_second_low, grad_cross_hidden, grad_first, grad_first_low, cross_sums, moves, parts_pix, pixel_sums,
        core_value, cross_mixed, *cross_halves,
    ) = cross_back(
        place, second_got, upstream, first_sum, slopes, cross_vectors, from_pixels, cross_up, cross_down,
        raw_all, normal, asks, mixed, kept, scores, top, cross_active, cross_normed, value_pad, groups,
    )
    if not cross_halves:
        cross_pairs = ((cross_active, grad_second_low), (cross_normed, grad_cross_hidden))
        cross_halves = [
            half_plain(pairs, half, item, order, ways).astype(BF)
            for pairs, order in ((cross_pairs, X_FIRST), (((cross_mixed, grad_first_low),), Y_FIRST))
            for half in (core, 1 - core)
        ]
    (
        parts_pix, moves, result_got, final_got, packed_got, core_value, grad_first, *cross_halves
    ) = tie((parts_pix, moves, result_got, final_got, packed_got, core_value, grad_first, *cross_halves))
    grad_pn = lax.psum_scatter(parts_pix, "lat", scatter_dimension=0, tiled=False)
    net_mine, net_other, out_mine, out_other = cross_halves
    net_got = lax.ppermute(net_other, "lat", swap)
    out_got = lax.ppermute(out_other, "lat", swap)
    final_two, packed_two, moves = tie(
        (add(final_kept[1], final_got[1]), add(packed_kept[1], packed_got[1]), moves)
    )
    final_two, packed_two = swap_items(final_two, 2), swap_items(packed_two, 1)
    grad_latents, small_mine, small_other = last_block(
        core, item, ways, moves, to_pixels, residual, grad_first, latent_gain[None], core_value, out_weight,
        normed, latent_queries, jnp.concatenate([cross_sums, item_sums, jnp.zeros((2, width), F32)]), pixel_sums,
    )
    small_got = lax.ppermute(small_other, "lat", swap)
    net_first, out_first = add(net_mine[:2], net_got[:2]), add(out_mine[:2], out_got[:2])
    final_two, packed_two, net_first, out_first, small_got, small_mine, grad_latents = tie(
        (final_two, packed_two, net_first, out_first, small_got, small_mine, grad_latents)
    )
    small_first = add(small_mine[:2], small_got[:2])
    first_got = [swap_items(net_first, 1), swap_items(out_first, 2), swap_items(small_first, 2)]
    item_here = jnp.concatenate(
        [
            total([final_kept[0], final_got[0], final_two]).astype(BF),
            total([packed_kept[0], packed_got[0], packed_two]).astype(BF),
        ],
        axis=1,
    )
    grad_pn, *first_got = tie((grad_pn, *first_got))
    item_part = over_chips_whole(item_here.reshape(chips, block, -1))
    flows = ((net_mine, net_got, 2), (out_mine, out_got, 1), (small_mine, small_got, 1))
    hops = [
        swap_items(total([mine[3], got[3], first[1]]).astype(BF), hop)
        for (mine, got, hop), first in zip(flows, first_got)
    ]
    net_here, out_here, small_here = [
        total([mine[2], got[2], first[0], last]).astype(BF)
        for (mine, got, hop), first, last in zip(flows, first_got, hops)
    ]
    lines = small_here.shape[0] // (chips // 2)
    pieces = jnp.stack(
        [
            jnp.concatenate(
                [
                    whole[z * block : (z + 1) * block, k * block : (k + 1) * block]
                    for whole in (net_here, out_here)
                    for k in range(whole.shape[1] // block)
                ]
                + [small_here[z // 2 * lines : (z // 2 + 1) * lines, z % 2 * block : (z % 2 + 1) * block]]
            )
            for z in range(chips)
        ]
    )
    rest = total(near_chips(lambda z: lax.dynamic_index_in_dim(pieces, z, 0, keepdims=False))).astype(BF)
    item_part, rest = tie((item_part, rest))
    rest_parts = gather_items(rest)
    item_parts = gather_items(item_part)
    quarter = width // groups
    grad_latent_down, grad_latent_up, grad_self_out = [
        weight_of(item_parts[:, :, at * quarter : (at + 1) * quarter]) for at in range(3)
    ]
    grad_self_packed = weight_of(item_parts[:, :, 3 * quarter :])
    tall = quarter // block * block
    grad_cross_down, grad_cross_up, grad_out_weight = [
        weight_of(
            rest_parts[:, at * tall : (at + 1) * tall]
            .reshape(groups, quarter // block, block, block)
            .transpose(0, 2, 1, 3)
            .reshape(groups, block, quarter)
        )
        for at in range(3)
    ]
    small = jnp.concatenate(by_item(rest_parts[:, 3 * tall :]), axis=0).astype(F32)
    result = second_sum + result_got.astype(F32)
    grad_pn = grad_pn.astype(F32)[:cin]
    pix_hat, pix_inv = norm_parts(pixels[0].T.astype(F32), 0)
    scaled = grad_pn * pixel_gain[:, None]
    grad_pixels = pix_inv * (
        scaled
        - jnp.mean(scaled, axis=0, keepdims=True)
        - pix_hat * jnp.mean(scaled * pix_hat, axis=0, keepdims=True)
    )
    grad_query_weight = dot_tn(small[channels : 2 * channels].astype(BF), key_pad) * score_scale
    grad_key_weight = small[2 * channels : 2 * channels + cin] * score_scale
    grad_value_weight = small[:cin]
    sums = small[3 * channels + 2 :]
    count = -(-channels // block)
    grad_pixel_gain = sums[:count].reshape(-1)[:cin]
    grad_pixel_shift = sums[count : 2 * count].reshape(-1)[:cin]
    gains = [small[3 * channels], small[3 * channels + 1]] + [sums[2 * count + at] for at in range(6)]
    shape = (1, items, lat_rows, width)
    return (
        result.reshape(shape),
        grad_latents.reshape(shape),
        grad_pixels.T[None],
        gains[0],
        gains[1],
        grad_pixel_gain,
        grad_pixel_shift,
        grad_query_weight,
        grad_key_weight,
        grad_value_weight,
        grad_out_weight,
        gains[2],
        gains[3],
        grad_cross_up,
        grad_cross_down,
        gains[4],
        gains[5],
        grad_self_packed,
        grad_self_out,
        gains[6],
        gains[7],
        grad_latent_up,
        grad_latent_down,
    )


def solution(mesh):
    rows = P("items", None, "lat", None)
    in_specs = (rows, P("items", "lat", None), P("items", None), rows) + (P(),) * 20
    lane = P("lat")
    tall = P("lat", None)
    wide = P(None, "lat")
    out_specs = (
        rows,
        rows,
        P("items", "lat", None),
        lane,
        lane,
        P(),
        P(),
        tall,
        wide,
        wide,
        tall,
        lane,
        lane,
        tall,
        tall,
        lane,
        lane,
        tall,
        tall,
        lane,
        lane,
        tall,
        tall,
    )
    return jax.shard_map(
        on_device, mesh=mesh, in_specs=in_specs, out_specs=out_specs, check_vma=False
    )
```

```python
import math

import jax
import jax.numpy as jnp
from jax import lax
from jax.experimental import pallas as pl
from jax.experimental.pallas import tpu as pltpu
from jax.sharding import PartitionSpec as P

HEADS = 8
HEAD = 128
X_FIRST = (1, 3, 0, 2)
Y_FIRST = (2, 3, 0, 1)
BF = jnp.bfloat16
F32 = jnp.float32


def norm_parts(values, axis=-1):
    centre = values - jnp.mean(values, axis=axis, keepdims=True)
    spread = jnp.mean(centre * centre, axis=axis, keepdims=True)
    inv = lax.rsqrt(spread + 1e-05)
    return centre * inv, inv


def layer_norm(values, gain, shift):
    hat, unused = norm_parts(values)
    return hat * gain + shift


def norm_back(values, gain, upstream):
    hat, inv = norm_parts(values)
    scaled = upstream * gain
    back = inv * (
        scaled
        - jnp.mean(scaled, axis=-1, keepdims=True)
        - hat * jnp.mean(scaled * hat, axis=-1, keepdims=True)
    )
    return back, jnp.sum(upstream * hat, axis=0), jnp.sum(upstream, axis=0)


def gelu_back(hidden, upstream):
    unused, pullback = jax.vjp(jax.nn.gelu, hidden)
    return pullback(upstream)[0]


def dot(left, right):
    return jnp.dot(left, right, preferred_element_type=F32)


def dot_tn(left, right):
    return lax.dot_general(left, right, (((0,), (0,)), ((), ())), preferred_element_type=F32)


def dot_nt(left, right):
    return lax.dot_general(left, right, (((1,), (1,)), ((), ())), preferred_element_type=F32)


def softmax(scores):
    raised = jnp.exp(scores - jnp.max(scores, axis=-1, keepdims=True))
    return raised / jnp.sum(raised, axis=-1, keepdims=True)


def attend_kernel(query, key, value, out, kept):
    scores = dot_nt(query[...], key[...]) * (1.0 / math.sqrt(HEAD))
    raised = jnp.exp(scores - jnp.max(scores, axis=-1, keepdims=True))
    weights = (raised * (1.0 / jnp.sum(raised, axis=-1, keepdims=True))).astype(BF)
    kept[0] = weights
    out[...] = dot(weights, value[...]).astype(BF)


def attend(queries, pairs, rows, whole_rows):
    column = lambda at: pl.BlockSpec((whole_rows, HEAD), lambda h: (0, h + at))
    own = pl.BlockSpec((rows, HEAD), lambda h: (0, h))
    return pl.pallas_call(
        attend_kernel,
        grid=(HEADS,),
        in_specs=[own, column(0), column(HEADS)],
        out_specs=[own, pl.BlockSpec((1, rows, whole_rows), lambda h: (h, 0, 0))],
        out_shape=[
            jax.ShapeDtypeStruct((rows, HEADS * HEAD), BF),
            jax.ShapeDtypeStruct((HEADS, rows, whole_rows), BF),
        ],
        compiler_params=pltpu.CompilerParams(vmem_limit_bytes=40 << 20),
        name="attend",
    )(queries, pairs, pairs)


def attend_back_kernel(grad, weights_ref, query, key, value, grad_query, grad_pair):
    at = pl.multiple_of(pl.program_id(0) * HEAD, HEAD)
    also = pl.multiple_of(pl.program_id(0) * HEAD + HEADS * HEAD, HEAD)
    weights_low = weights_ref[0]
    weights = weights_low.astype(F32)
    upstream = grad[...]
    grad_weights = dot_nt(upstream, value[...])
    grad_pair[:, pl.ds(also, HEAD)] = dot_tn(weights_low, upstream).astype(BF)
    inner = jnp.sum(weights * grad_weights, axis=-1, keepdims=True)
    spread = (weights * (grad_weights - inner)).astype(BF)
    scale = 1.0 / math.sqrt(HEAD)
    grad_query[...] = (dot(spread, key[...]) * scale).astype(BF)
    grad_pair[:, pl.ds(at, HEAD)] = (dot_tn(spread, query[...]) * scale).astype(BF)


def attend_back(grad, weights, queries, pairs, rows, whole_rows):
    column = lambda at: pl.BlockSpec((whole_rows, HEAD), lambda h: (0, h + at))
    own = pl.BlockSpec((rows, HEAD), lambda h: (0, h))
    return pl.pallas_call(
        attend_back_kernel,
        grid=(HEADS,),
        in_specs=[
            own,
            pl.BlockSpec((1, rows, whole_rows), lambda h: (h, 0, 0)),
            own,
            column(0),
            column(HEADS),
        ],
        out_specs=[own, pl.BlockSpec((whole_rows, 2 * HEADS * HEAD), lambda h: (0, 0))],
        out_shape=[
            jax.ShapeDtypeStruct((rows, HEADS * HEAD), BF),
            jax.ShapeDtypeStruct((whole_rows, 2 * HEADS * HEAD), BF),
        ],
        compiler_params=pltpu.CompilerParams(vmem_limit_bytes=40 << 20),
        name="attend_back",
    )(grad, weights, queries, pairs, pairs)


def half_columns(left, half, blocks):
    step = left.shape[1] // (2 * blocks)
    return jnp.concatenate(
        [left[:, pl.ds(pl.multiple_of((2 * z + half) * step, step), step)] for z in range(blocks)], axis=1
    ).T


def half_kernel(count, blocks, place, *refs):
    lefts, rights, added = refs[:count], refs[count : 2 * count], refs[2 * count]
    sent, kept, turned = refs[2 * count + 1 :]
    step = pl.program_id(0)

    @pl.when(step == 0)
    def start():
        for at, left in enumerate(lefts):
            turned[at] = half_columns(left, place[0], blocks)

    at = 0
    for index, right in enumerate(rights):
        size = right.shape[1]
        value = dot(turned[index], right[...]) + added[0, :, at : at + size].astype(F32)
        value = value.astype(BF)

        @pl.when(step < 2)
        def send():
            sent[0, :, at : at + size] = value

        @pl.when(step >= 2)
        def keep():
            kept[0, :, at : at + size] = value

        at += size


def half_plain(pairs, half, item, order, ways):
    blocks = ways // 2
    rows, width = pairs[0][0].shape
    groups = len(order)
    outs = []
    for left, right in pairs:
        columns = lax.dynamic_index_in_dim(
            left.reshape(rows, blocks, 2, width // ways), half, 2, keepdims=False
        ).reshape(rows, width // 2)
        value = dot_tn(columns, right).reshape(width // 2, groups, -1).transpose(1, 0, 2)
        outs.append(value)
    value = jnp.concatenate(outs, axis=2)
    return jnp.stack([lax.dynamic_index_in_dim(value, item ^ m, 0, keepdims=False) for m in order])


def half_grads(pairs, half, item, order, ways, added):
    rows, width = pairs[0][0].shape
    blocks, groups = ways // 2, len(order)
    total = sum(right.shape[1] for unused, right in pairs) // groups
    if (width // ways) % 128:
        value = (half_plain(pairs, half, item, order, ways) + added.astype(F32)).astype(BF)
        return value[:2], value[2:]
    return pl.pallas_call(
        lambda place, *refs: half_kernel(len(pairs), blocks, place, *refs),
        grid_spec=pltpu.PrefetchScalarGridSpec(
            num_scalar_prefetch=1,
            grid=(groups,),
            in_specs=[pl.BlockSpec((rows, width), lambda g, place: (0, 0)) for unused in pairs]
            + [
                pl.BlockSpec((rows, right.shape[1] // groups), lambda g, place: (0, place[1 + g]))
                for unused, right in pairs
            ]
            + [pl.BlockSpec((1, width // 2, total), lambda g, place: (g, 0, 0))],
            out_specs=[
                pl.BlockSpec((1, width // 2, total), lambda g, place: (jnp.minimum(g, 1), 0, 0)),
                pl.BlockSpec((1, width // 2, total), lambda g, place: (jnp.maximum(g - 2, 0), 0, 0)),
            ],
            scratch_shapes=[pltpu.VMEM((len(pairs), width // 2, rows), BF)],
        ),
        out_shape=[jax.ShapeDtypeStruct((2, width // 2, total), BF)] * 2,
        compiler_params=pltpu.CompilerParams(vmem_limit_bytes=40 << 20),
        name="half_grads",
    )(
        jnp.stack([half] + [item ^ m for m in order]).astype(jnp.int32),
        *[left for left, unused in pairs],
        *[right for unused, right in pairs],
        added,
    )


def small_parts(
    core, item, moves, core_in, residual, grad_first, gain, core_value, out_w, normed, queries,
    sums, item_sums, pixel_sums, grad_latents, mine, other, stacked, rest,
):
    rows, width = residual.shape
    block = mine.shape[2] // 2
    chips = width // block // 2
    channels = moves.shape[1]
    stacked[...] = jnp.zeros(stacked.shape, F32)

    def back(part):
        grad_normed = dot_nt(moves[part, :], core_in[...])
        hat, inv = norm_parts(residual[part, :])
        stacked[0:1, :] += jnp.sum(grad_normed * hat, axis=0, keepdims=True)
        stacked[1:2, :] += jnp.sum(grad_normed, axis=0, keepdims=True)
        grad_latents[part, :] = grad_first[part, :] + norm_slope(hat, inv, gain[...], grad_normed)

    each_part(rows, back)
    stacked[8:10, :] = sums[...]
    stacked[10:14, :] = item_sums[...]
    for at in range(2):
        line = jnp.broadcast_to(pixel_sums[at], (channels, 128)).T[0:1, :]
        line = jnp.concatenate([line, jnp.zeros((1, -channels % 128), F32)], axis=1)
        for k in range(line.shape[1] // 128):
            for j in range(width // block):
                stacked[2 + 3 * at + k : 3 + 3 * at + k, j * block : j * block + 128] = line[
                    :, k * 128 : (k + 1) * 128
                ]
    rest[0:channels, :] = dot_nt(core_value, out_w[...]).astype(BF)
    rest[channels : 2 * channels, :] = dot_tn(moves[...], normed[...]).astype(BF)
    rest[2 * channels : 3 * channels, :] = dot_tn(moves[...], queries[...]).astype(BF)
    rest[3 * channels :, :] = stacked[...].astype(BF)
    size = rest.shape[0] // 4
    for p, m in enumerate(Y_FIRST):
        lines = pl.ds(pl.multiple_of((item ^ m) * size, 16), size)
        for out, half in ((mine, core), (other, 1 - core)):
            for z in range(chips):
                lanes = pl.ds(pl.multiple_of((2 * z + half) * block, block), block)
                out[p, z // 2 * size : (z // 2 + 1) * size, z % 2 * block : (z % 2 + 1) * block] = rest[
                    lines, lanes
                ]


def small_lines(channels):
    return 3 * channels + 16


def last_block(
    core, item, ways, moves, core_in, residual, grad_first, gain, core_value, out_w, normed, queries,
    vectors, pixel_sums,
):
    rows, width = residual.shape
    channels = moves.shape[1]
    block, chips = width // ways, ways // 2
    grad_normed = dot_nt(moves, core_in)
    back, grad_gain, grad_shift = norm_back(residual, gain[0], grad_normed)
    sums = jnp.pad(pixel_sums.reshape(2, channels), ((0, 0), (0, -channels % block)))
    lines = sums.reshape(-1, 1, block)
    lines = jnp.broadcast_to(lines, (lines.shape[0], ways, block)).reshape(-1, width)
    stack = [
        dot_nt(core_value, out_w),
        dot_tn(moves, normed),
        dot_tn(moves, queries),
        grad_gain[None],
        grad_shift[None],
        lines,
        vectors,
    ]
    count = sum(value.shape[0] for value in stack)
    stack = jnp.concatenate(stack + [jnp.zeros((-count % 64, width), F32)]).astype(BF)
    size = stack.shape[0] // 4
    stack = stack.reshape(4, size, chips // 2, 2, 2, block)
    halves = []
    for half in (core, 1 - core):
        value = lax.dynamic_index_in_dim(stack, half, 4, keepdims=False)
        value = value.transpose(0, 2, 1, 3, 4).reshape(4, chips // 2 * size, 2 * block)
        halves.append(
            jnp.stack([lax.dynamic_index_in_dim(value, item ^ m, 0, keepdims=False) for m in Y_FIRST])
        )
    return grad_first + back, halves[0], halves[1]


GELU_A = 0.044715
GELU_C = math.sqrt(2.0 / math.pi)
PART = 256


def gelu_both(hidden):
    square = hidden * hidden
    bent = jnp.tanh(hidden * (GELU_C + (GELU_C * GELU_A) * square))
    half = 0.5 + 0.5 * bent
    slope = half + (0.5 * hidden) * (1.0 - bent * bent) * (GELU_C + (3.0 * GELU_C * GELU_A) * square)
    return hidden * half, slope


def norm_slope(hat, inv, gain, upstream):
    scaled = upstream * gain
    centre = jnp.mean(scaled, axis=-1, keepdims=True)
    along = jnp.mean(scaled * hat, axis=-1, keepdims=True)
    return inv * (scaled - centre - hat * along)


def each_part(rows, body):
    size = min(PART, rows)

    def step(r, carry):
        body(pl.ds(pl.multiple_of(r * size, size), size))
        return carry

    lax.fori_loop(0, rows // size, step, 0)


def each_head(body):
    def step(h, carry):
        body(h)
        return carry

    lax.fori_loop(0, HEADS, step, 0)


def write_halves(pairs, outs, item, order, blocks, turned):
    at = 0
    for left, right in pairs:
        size = right.shape[1] // len(order)
        for out, half in outs:
            turned[...] = half_columns(left, half, blocks)
            for p, m in enumerate(order):
                lanes = pl.ds(pl.multiple_of((item ^ m) * size, HEAD), size)
                out[p, :, at : at + size] = dot(turned[...], right[:, lanes]).astype(BF)
        at += size


def item_body(place, near, made, extra, need, flush):
    second, vectors, packed_w0, packed_w1, packed_w2, out_w, up_w, down_w, grad_low = near
    (
        self_normed, self_mixed, final_normed, final_active, result_add, grad_final_hidden, grad_third_low,
        second_add, grad_packed, sums, other_first, other_packed,
    ) = made
    packed, raised_low, inverse, mixed, back_third, grad_mixed, turned = extra
    packed_w = (packed_w0, packed_w1, packed_w2)
    rows, width = second.shape
    need(0, 1)
    sums[...] = jnp.zeros(sums.shape, F32)

    def normalize(part):
        hat, unused = norm_parts(second[part, :].astype(F32))
        self_normed[part, :] = (hat * vectors[0:1, :] + vectors[1:2, :]).astype(BF)

    each_part(rows, normalize)
    flush(0)
    for c in range(3):
        need(2 + c)

        def project(part):
            packed[part, c * width : (c + 1) * width] = dot(
                self_normed[part, :], packed_w[c][...]
            ).astype(BF)

        each_part(rows, project)

    def lanes(h, group):
        return pl.ds(pl.multiple_of(h * HEAD + group * width, HEAD), HEAD)

    scale = 1.0 / math.sqrt(HEAD)

    def attend_head(h):
        scores = dot_nt(packed[:, lanes(h, 0)], packed[:, lanes(h, 1)])
        peak = jnp.max(scores, axis=-1, keepdims=True)
        raised = jnp.exp2((scores - peak) * (scale * math.log2(math.e)))
        inv = 1.0 / jnp.sum(raised, axis=-1, keepdims=True)
        low = raised.astype(BF)
        raised_low[h] = low
        inverse[h] = inv
        mixed[:, lanes(h, 0)] = dot(low, packed[:, lanes(h, 2)]) * inv

    each_head(attend_head)
    need(5, 6, 7, 8)

    def middle(part):
        low = mixed[part, :].astype(BF)
        self_mixed[part, :] = low
        added = dot(low, out_w[...])
        hat, inv = norm_parts(second[part, :].astype(F32) + added)
        normed = (hat * vectors[2:3, :] + vectors[3:4, :]).astype(BF)
        final_normed[part, :] = normed
        active, slope = gelu_both(dot(normed, up_w[...]))
        active = active.astype(BF)
        final_active[part, :] = active
        result_add[part, :] = (added + dot(active, down_w[...])).astype(BF)
        upstream = grad_low[part, :]
        grad_hidden = (dot_nt(upstream, down_w[...]) * slope).astype(BF)
        grad_final_hidden[part, :] = grad_hidden
        grad_normed = dot_nt(grad_hidden, up_w[...])
        sums[2:3, :] += jnp.sum(grad_normed * hat, axis=0, keepdims=True)
        sums[3:4, :] += jnp.sum(grad_normed, axis=0, keepdims=True)
        back = norm_slope(hat, inv, vectors[2:3, :], grad_normed)
        back_third[part, :] = back
        third_low = (upstream.astype(F32) + back).astype(BF)
        grad_third_low[part, :] = third_low
        grad_mixed[part, :] = dot_nt(third_low, out_w[...]).astype(BF)

    each_part(rows, middle)
    flush(1, 2, 3, 4, 5, 6)

    def attend_back_head(h):
        upstream = grad_mixed[:, lanes(h, 0)]
        low = raised_low[h]
        inv = inverse[h]
        up32 = upstream.astype(F32)
        inner = jnp.sum(up32 * mixed[:, lanes(h, 0)], axis=-1, keepdims=True)
        grad_packed[:, lanes(h, 2)] = dot_tn(low, (up32 * inv).astype(BF)).astype(BF)
        grad_weights = dot_nt(upstream, packed[:, lanes(h, 2)])
        spread = (low.astype(F32) * ((grad_weights - inner) * (inv * scale))).astype(BF)
        grad_packed[:, lanes(h, 0)] = dot(spread, packed[:, lanes(h, 1)]).astype(BF)
        grad_packed[:, lanes(h, 1)] = dot_tn(spread, packed[:, lanes(h, 0)]).astype(BF)

    each_head(attend_back_head)
    flush(8)

    def last(part):
        hat, inv = norm_parts(second[part, :].astype(F32))
        grad_normed = dot_nt(grad_packed[part, :width], packed_w[0][...])
        for c in range(1, 3):
            grad_normed += dot_nt(grad_packed[part, c * width : (c + 1) * width], packed_w[c][...])
        sums[0:1, :] += jnp.sum(grad_normed * hat, axis=0, keepdims=True)
        sums[1:2, :] += jnp.sum(grad_normed, axis=0, keepdims=True)
        back = norm_slope(hat, inv, vectors[0:1, :], grad_normed)
        second_add[part, :] = (back_third[part, :] + back).astype(BF)

    each_part(rows, last)
    flush(7, 9)
    blocks = width // 2 // HEAD
    write_halves(
        ((final_active, grad_low), (final_normed, grad_final_hidden), (self_mixed, grad_third_low)),
        ((other_first, 1 - place[0]),), place[1], X_FIRST, blocks, turned,
    )
    flush(10)
    write_halves(
        ((self_normed, grad_packed),), ((other_packed, 1 - place[0]),), place[1], Y_FIRST, blocks, turned
    )


def item_block(place, groups, second, grad_low, vectors, self_packed, self_out, latent_up, latent_down):
    rows, width = second.shape
    low = jax.ShapeDtypeStruct((rows, width), BF)
    half = jax.ShapeDtypeStruct((groups, width // 2, 3 * width // groups), BF)
    packed_parts = [(self_packed, c * width, width) for c in range(3)]
    (
        self_normed, self_mixed, final_normed, final_active, result_add, grad_final_hidden, grad_third_low,
        second_add, grad_packed, sums, other_first, other_packed,
    ) = streamed(
        "item_block",
        item_body,
        place,
        [second, vectors, *packed_parts, self_out, latent_up, latent_down, grad_low],
        [low] * 8
        + [
            jax.ShapeDtypeStruct((rows, 3 * width), BF),
            jax.ShapeDtypeStruct((4, width), F32),
            half,
            half,
        ],
        [
            pltpu.VMEM((rows, 3 * width), BF),
            pltpu.VMEM((HEADS, rows, rows), BF),
            pltpu.VMEM((HEADS, rows, 1), F32),
            pltpu.VMEM((rows, width), F32),
            pltpu.VMEM((rows, width), F32),
            pltpu.VMEM((rows, width), BF),
            pltpu.VMEM((width // 2, rows), BF),
        ],
    )
    return (
        result_add, second_add, self_normed, grad_packed, self_mixed, grad_third_low,
        final_normed, final_active, grad_final_hidden, sums, other_first, other_packed,
    )


def streamed(name, body, place, ins, outs, scratch):
    cuts = [value[1:] if isinstance(value, tuple) else None for value in ins]
    ins = [value[0] if isinstance(value, tuple) else value for value in ins]
    shapes = [value.shape if cut is None else (value.shape[0], cut[1]) for value, cut in zip(ins, cuts)]
    anywhere = pl.BlockSpec(memory_space=pl.ANY)

    def kernel(place_ref, *refs):
        sources, refs = refs[: len(ins)], refs[len(ins) :]
        targets, refs = refs[: len(outs)], refs[len(outs) :]
        near, refs = refs[: len(ins)], refs[len(ins) :]
        made, refs = refs[: len(outs)], refs[len(outs) :]
        extra, (in_sems, out_sems) = refs[:-2], refs[-2:]
        sources = [ref if cut is None else ref.at[:, pl.ds(*cut)] for ref, cut in zip(sources, cuts)]
        loads = [pltpu.make_async_copy(a, b, in_sems.at[i]) for i, (a, b) in enumerate(zip(sources, near))]
        stores = [pltpu.make_async_copy(a, b, out_sems.at[i]) for i, (a, b) in enumerate(zip(made, targets))]
        left_in, left_out = list(range(len(ins))), list(range(len(outs)))
        for load in loads:
            load.start()

        def need(*which):
            for i in which:
                left_in.remove(i)
                loads[i].wait()

        def flush(*which):
            for i in which:
                left_out.remove(i)
                stores[i].start()

        body(place_ref, near, made, extra, need, flush)
        need(*list(left_in))
        flush(*list(left_out))
        for store in stores:
            store.wait()

    return pl.pallas_call(
        kernel,
        in_specs=[pl.BlockSpec(memory_space=pltpu.SMEM)] + [anywhere] * len(ins),
        out_specs=[anywhere] * len(outs),
        out_shape=list(outs),
        scratch_shapes=[pltpu.VMEM(shape, value.dtype) for shape, value in zip(shapes, ins)]
        + [pltpu.VMEM(value.shape, value.dtype) for value in outs]
        + list(scratch)
        + [pltpu.SemaphoreType.DMA((len(ins),)), pltpu.SemaphoreType.DMA((len(outs),))],
        compiler_params=pltpu.CompilerParams(vmem_limit_bytes=60 << 20),
        name=name,
    )(place, *ins)


def pixel_hat(values, cin):
    real = lax.broadcasted_iota(jnp.int32, (values.shape[0], 1), 0) < cin
    portion = 1.0 / cin.astype(F32)
    centre = jnp.where(real, values - jnp.sum(values, axis=0, keepdims=True) * portion, 0.0)
    return centre * lax.rsqrt(jnp.sum(centre * centre, axis=0, keepdims=True) * portion + 1e-05)


def each_block(count, body):
    def step(n, carry):
        body(n)
        return carry

    lax.fori_loop(0, count, step, 0)


def cross_body(place, near, made, extra, need, flush):
    asks, gain, shift, raw, owner, core_out, residual, vectors, up_w, down_w = near
    (
        normal, scores, kept, mixed, top, first_sum, cross_normed, slopes, cross_active, second_sum, second
    ) = made
    (heap,) = extra
    ways, channels, size = normal.shape
    rows = asks.shape[0]
    lat_rows = heap.shape[0]
    at = pl.multiple_of(place[2] * lat_rows, lat_rows)
    large = pl.ds(at, lat_rows)
    need(0, 1, 2, 3)
    columns = lax.broadcasted_iota(jnp.int32, (1, size), 1)
    top[...] = jnp.full(top.shape, -1e30, F32)

    def score(n):
        value = (pixel_hat(raw[n].astype(F32), place[3]) * gain[...] + shift[...]).astype(BF)
        normal[n] = value
        places = columns + n * size
        found = dot(asks[large, :], value)
        found = jnp.where((places >= place[0]) & (places < place[1]), found, -1e30)
        scores[n] = found
        top[...] = jnp.maximum(top[...], jnp.max(found, axis=1, keepdims=True))

    each_block(ways, score)
    flush(0, 1)
    need(4)
    edge = jnp.where(
        columns < place[0], normal[0].astype(F32), normal[ways - 1].astype(F32)
    ).astype(BF)
    row_item = lax.broadcasted_iota(jnp.int32, (rows, 1), 0) // lat_rows
    inside = (owner[...] == row_item) & (place[2] != row_item)
    found = jnp.where(inside, dot(asks[...], edge), -1e30)
    raised = jnp.exp(found - jnp.max(found, axis=1, keepdims=True))
    weights = raised * (1.0 / jnp.sum(raised, axis=1, keepdims=True))
    weights = jnp.where(inside, weights, 0.0).astype(BF)
    kept[...] = weights
    mixed[...] = dot_nt(weights, edge)
    heap[...] = jnp.zeros(heap.shape, F32)
    peak = top[...]

    def gather(n, carry):
        raised = jnp.exp(scores[n] - peak)
        heap[...] += dot_nt(raised.astype(BF), normal[n])
        return carry + jnp.sum(raised, axis=1, keepdims=True)

    whole = lax.fori_loop(0, ways, gather, jnp.zeros((lat_rows, 1), F32))
    mixed[large, :] = heap[...] * (1.0 / whole)
    top[...] = peak + jnp.log(whole)
    flush(2, 3, 4)
    need(5, 6, 7, 8, 9)

    def net(part):
        first = residual[part, :] + dot(mixed[part, :].astype(BF), core_out[...])
        first_sum[part, :] = first
        hat, unused = norm_parts(first)
        normed = (hat * vectors[0:1, :] + vectors[1:2, :]).astype(BF)
        cross_normed[part, :] = normed
        active, slope = gelu_both(dot(normed, up_w[...]))
        active = active.astype(BF)
        cross_active[part, :] = active
        slopes[part, :] = slope
        value = first + dot(active, down_w[...])
        second_sum[part, :] = value
        second[part, :] = value.astype(BF)

    each_part(rows, net)


def cross_back_body(place, near, made, extra, need, flush):
    (
        got, upstream, slopes, down_w, up_w, first_sum, vectors, core_out, normal, mixed, kept, asks, scores, top,
        raw, value_w, cross_active, cross_normed, *latent_side,
    ) = near
    grad, corner, heap, turned, *small_scratch = extra
    if not latent_side:
        (
            grad_second_low, grad_cross_hidden, grad_first, grad_first_low, sums, moves, pix, pixel_sums,
            core_value, cross_mixed,
        ) = made
    else:
        grad_second_low, grad_cross_hidden, grad_first_low, moves, pixel_sums, sums, grad_first, cross_mixed = (
            small_scratch[:8]
        )
        pix, grad_latents, small_mine, small_other, *halves = made
    ways, channels, size = normal.shape
    rows = asks.shape[0]
    lat_rows = heap.shape[0]
    at = pl.multiple_of(place[2] * lat_rows, lat_rows)
    large = pl.ds(at, lat_rows)
    sums[...] = jnp.zeros(sums.shape, F32)
    pixel_sums[...] = jnp.zeros(pixel_sums.shape, F32)
    need(0, 1, 2, 3, 4, 5, 6, 7)

    def net(part):
        grad_second = upstream[part, :] + got[part, :].astype(F32)
        low = grad_second.astype(BF)
        grad_second_low[part, :] = low
        grad_hidden = (dot_nt(low, down_w[...]) * slopes[part, :]).astype(BF)
        grad_cross_hidden[part, :] = grad_hidden
        grad_normed = dot_nt(grad_hidden, up_w[...])
        hat, inv = norm_parts(first_sum[part, :])
        sums[0:1, :] += jnp.sum(grad_normed * hat, axis=0, keepdims=True)
        sums[1:2, :] += jnp.sum(grad_normed, axis=0, keepdims=True)
        value = grad_second + norm_slope(hat, inv, vectors[0:1, :], grad_normed)
        grad_first[part, :] = value
        low = value.astype(BF)
        grad_first_low[part, :] = low
        grad[part, :] = dot_nt(low, core_out[...]).astype(BF)

    each_part(rows, net)
    if not latent_side:
        flush(0, 1, 2, 3, 4)
    need(8, 9, 10, 11, 12, 13, 14)
    columns = lax.broadcasted_iota(jnp.int32, (1, size), 1)
    early = columns < place[0]
    edge = jnp.where(early, normal[0].astype(F32), normal[ways - 1].astype(F32)).astype(BF)
    deltas = jnp.sum(grad[...].astype(F32) * mixed[...], axis=1, keepdims=True)
    weights = kept[...]
    spread = (weights.astype(F32) * (dot(grad[...], edge) - deltas)).astype(BF)
    moves[...] = dot_nt(spread, edge).astype(BF)
    corner[...] = dot_tn(asks[...], spread) + dot_tn(grad[...], weights)
    heap[...] = jnp.zeros(heap.shape, F32)
    own = grad[large, :]
    own_asks = asks[large, :]
    deltas = jnp.sum(own.astype(F32) * mixed[large, :], axis=1, keepdims=True)
    level = top[...]

    def block(n):
        value = normal[n]
        weights = jnp.exp(scores[n] - level)
        spread = (weights * (dot(own, value) - deltas)).astype(BF)
        heap[...] += dot_nt(spread, value)
        part = dot_tn(own_asks, spread) + dot_tn(own, weights.astype(BF))
        use = ((n == 0) & early) | ((n == ways - 1) & jnp.logical_not(early))
        part = part + jnp.where(use, corner[...], 0.0)
        pix[n] = part.astype(BF)
        hat = pixel_hat(raw[n].astype(F32), place[3])
        pixel_sums[0] += jnp.sum(part * hat, axis=1, keepdims=True)
        pixel_sums[1] += jnp.sum(part, axis=1, keepdims=True)

    each_block(ways, block)
    moves[large, :] = heap[...].astype(BF)
    if latent_side:
        flush(0)
    else:
        flush(5, 6, 7)
    need(15, 16, 17)
    mixed_low = mixed[...].astype(BF)
    cross_mixed[...] = dot(mixed_low, value_w[...]).astype(BF)
    core_low = dot_tn(mixed_low, grad_first_low[...]).astype(BF)
    if not latent_side:
        core_value[...] = core_low
        return
    write_halves(
        ((cross_active, grad_second_low), (cross_normed, grad_cross_hidden)),
        ((halves[0], place[4]), (halves[1], 1 - place[4])), place[5], X_FIRST, ways // 2, turned,
    )
    write_halves(
        ((cross_mixed, grad_first_low),),
        ((halves[2], place[4]), (halves[3], 1 - place[4])), place[5], Y_FIRST, ways // 2, turned,
    )
    flush(4, 5, 6, 7)
    core_in, residual, gain_row, out_w, normed, queries, item_sums = latent_side
    need(18, 19, 20, 21, 22, 23, 24)
    small_parts(
        place[4], place[5], moves, core_in, residual, grad_first, gain_row, core_low, out_w, normed, queries,
        sums, item_sums, pixel_sums, grad_latents, small_mine, small_other, *small_scratch[8:],
    )


def cross(place, raw_all, gain, shift, asks, owner, residual, core_out, vectors, up, down, lat_rows):
    ways, channels, size = raw_all.shape
    rows, width = residual.shape
    low = jax.ShapeDtypeStruct((rows, width), BF)
    wide = jax.ShapeDtypeStruct((rows, width), F32)
    (
        normal, scores, kept, mixed, top, first_sum, cross_normed, slopes, cross_active, second_sum, second
    ) = streamed(
        "cross",
        cross_body,
        place,
        [asks, gain, shift, raw_all, owner, core_out, residual, vectors, up, down],
        [
            jax.ShapeDtypeStruct((ways, channels, size), BF),
            jax.ShapeDtypeStruct((ways, lat_rows, size), F32),
            jax.ShapeDtypeStruct((rows, size), BF),
            jax.ShapeDtypeStruct((rows, channels), F32),
            jax.ShapeDtypeStruct((lat_rows, 1), F32),
            wide,
            low,
            wide,
            low,
            wide,
            low,
        ],
        [pltpu.VMEM((lat_rows, channels), F32)],
    )
    return mixed, kept, scores, top, normal, first_sum, second_sum, second, cross_normed, cross_active, slopes


def cross_back(
    place, got, upstream, first_sum, slopes, vectors, core_out, up, down,
    raw_all, normal, asks, mixed, kept, scores, top, cross_active, cross_normed, value_w, latent_side, groups,
):
    ways, channels, size = raw_all.shape
    rows, width = upstream.shape
    lat_rows = top.shape[0]
    shape = jax.ShapeDtypeStruct
    low, wide = shape((rows, width), BF), shape((rows, width), F32)
    scratch = [
        pltpu.VMEM((rows, channels), BF),
        pltpu.VMEM((channels, size), F32),
        pltpu.VMEM((lat_rows, channels), F32),
        pltpu.VMEM((width // 2, rows), BF),
    ]
    moves, pixel_sums, sums = shape((rows, channels), BF), shape((2, channels, 1), F32), shape((2, width), F32)
    pix = shape((ways, channels, size), BF)
    if latent_side:
        total = small_lines(channels)
        small = shape((4, ways // 4 * (total // 4), 2 * width // ways), BF)
        outs = [pix, wide, small, small] + [
            shape((groups, width // 2, count * width // groups), BF) for count in (2, 2, 1, 1)
        ]
        inner = [low, low, low, moves, pixel_sums, sums, wide, low, shape((16, width), F32), shape((total, width), BF)]
        scratch += [pltpu.VMEM(value.shape, value.dtype) for value in inner]
    else:
        outs = [low, low, wide, low, sums, moves, pix, pixel_sums, shape((channels, width), BF), low]
    return streamed(
        "cross_back",
        cross_back_body,
        place,
        [
            got, upstream, slopes, down, up, first_sum, vectors, core_out, normal, mixed, kept, asks, scores, top,
            raw_all, value_w, cross_active, cross_normed, *latent_side,
        ],
        outs,
        scratch,
    )


def on_device(
    latents,
    pixels,
    lengths,
    out_grad,
    latent_gain,
    latent_shift,
    pixel_gain,
    pixel_shift,
    query_weight,
    key_weight,
    value_weight,
    out_weight,
    cross_gain,
    cross_shift,
    cross_up,
    cross_down,
    self_gain,
    self_shift,
    self_packed,
    self_out,
    final_gain,
    final_shift,
    latent_up,
    latent_down,
):
    items = latents.shape[1]
    lat_rows = latents.shape[2]
    width = latents.shape[3]
    pix_rows = pixels.shape[1]
    cin = pixels.shape[2]
    ways = lax.axis_size("lat")
    groups = lax.axis_size("items")
    sub = ways // items
    rows = items * lat_rows
    piece = lat_rows // sub
    score_scale = 1.0 / math.sqrt(width)
    head_scale = 1.0 / math.sqrt(HEAD)
    lat_index = lax.axis_index("lat")
    core = lat_index % 2

    channels = -(-cin // 16) * 16
    pad = ((0, channels - cin), (0, 0))
    spans = lengths[0]
    starts = jnp.cumsum(spans) - spans
    largest = jnp.argmax(spans).astype(jnp.int32)
    large_start = starts[largest]
    place = jnp.stack(
        [
            large_start,
            large_start + spans[largest],
            largest,
            jnp.asarray(cin, jnp.int32),
            core,
            lax.axis_index("items"),
        ]
    ).astype(jnp.int32)
    edge_places = jnp.arange(pix_rows, dtype=jnp.int32)
    edge_places = jnp.where(edge_places < large_start, edge_places, edge_places + pix_rows * (ways - 1))
    owner = jnp.sum((edge_places[None, :] >= starts[:, None]).astype(jnp.int32), axis=0) - 1
    owner = owner[None, :]

    swap = [(i, i ^ 1) for i in range(ways)]
    same_core = [list(range(0, ways, 2)), list(range(1, ways, 2))]
    block = width // ways

    tie = lax.optimization_barrier

    chips = ways // 2
    chip = lat_index // 2
    item = lax.axis_index("items")

    def swap_items(part, m):
        return lax.ppermute(part, "items", [(i, i ^ m) for i in range(groups)])

    def near_chips(pieces):
        if chips != 4:
            whole = jnp.stack([pieces(j) for j in range(chips)])
            moved = lax.all_to_all(
                whole, "lat", split_axis=0, concat_axis=0, tiled=True, axis_index_groups=same_core
            )
            return [moved[j] for j in range(chips)]
        return [pieces(chip)] + [
            lax.ppermute(
                pieces(chip ^ m), "lat", [(i, ((i // 2) ^ m) * 2 + i % 2) for i in range(ways)]
            )
            for m in range(1, chips)
        ]

    def total(parts):
        value = parts[0].astype(F32)
        for part in parts[1:]:
            value = value + part.astype(F32)
        return value

    def add(left, right):
        return (left.astype(F32) + right.astype(F32)).astype(BF)

    def over_chips_whole(here):
        parts = lax.all_to_all(
            here, "lat", split_axis=0, concat_axis=0, tiled=True, axis_index_groups=same_core
        )
        return jnp.sum(parts.astype(F32), axis=0).astype(BF)

    def gather_items(part):
        return jnp.stack([part] + [swap_items(part, m) for m in range(1, groups)])

    def by_item(parts):
        return [lax.dynamic_index_in_dim(parts, item ^ j, 0, keepdims=False) for j in range(groups)]

    def weight_of(parts):
        return jnp.concatenate(by_item(parts), axis=1).astype(F32)

    pixels_low = jnp.pad(pixels[0].T, pad)
    raw_all = lax.all_gather(pixels_low, "lat", axis=0, tiled=False)
    gain_column = jnp.pad(pixel_gain[:, None], pad)
    shift_column = jnp.pad(pixel_shift[:, None], pad)
    key_pad = jnp.pad(key_weight, pad)
    value_pad = jnp.pad(value_weight, pad)

    to_pixels = (dot_nt(query_weight, key_pad) * score_scale).astype(BF)
    from_pixels = dot(value_pad, out_weight).astype(BF)

    residual = latents.reshape(rows, width)
    upstream = out_grad.reshape(rows, width)
    normed = layer_norm(residual, latent_gain, latent_shift).astype(BF)
    asks = dot(normed, to_pixels).astype(BF)
    latent_queries = dot(normed, query_weight).astype(BF)

    def reshare(values):
        moved = lax.all_to_all(
            values.reshape(ways, piece, width), "lat", split_axis=0, concat_axis=0, tiled=True
        )
        return moved.reshape(rows, width)

    (
        raw_all, value_pad, upstream_low, asks, latent_queries, from_pixels, to_pixels, gain_column, shift_column, place, owner
    ) = tie(
        (
            raw_all, value_pad, upstream.astype(BF), asks, latent_queries, from_pixels, to_pixels, gain_column, shift_column,
            place, owner,
        )
    )
    grad_low = reshare(upstream_low)
    cross_vectors = jnp.stack([cross_gain, cross_shift])
    (
        mixed, kept, scores, top, normal, first_sum, second_sum, second, cross_normed, cross_active, slopes
    ) = cross(
        place, raw_all, gain_column, shift_column, asks, owner, residual, from_pixels, cross_vectors,
        cross_up, cross_down, lat_rows,
    )
    second, grad_low = tie((second, grad_low))
    second = reshare(second)
    item_place = jnp.stack([core, item]).astype(jnp.int32)
    item_vectors = jnp.stack([self_gain, self_shift, final_gain, final_shift])
    if sub == 1:
        (
            result_add, second_add, self_normed, grad_packed, self_mixed, grad_third_low,
            final_normed, final_active, grad_final_hidden, item_sums, final_other, packed_other,
        ) = item_block(item_place, groups, second, grad_low, item_vectors, self_packed, self_out, latent_up, latent_down)
    else:
        whole_rows = rows * sub
        same_item = [[i * sub + s for s in range(sub)] for i in range(items)]
        second_wide = second.astype(F32)
        self_normed = layer_norm(second_wide, self_gain, self_shift).astype(BF)
        packed = dot(self_normed, self_packed).astype(BF)
        pairs = lax.all_gather(
            packed[:, width:], "lat", axis=0, tiled=True, axis_index_groups=same_item
        )
        self_mixed, self_low = attend(packed, pairs, rows, whole_rows)
        self_add = dot(self_mixed, self_out)
        third = second_wide + self_add
        final_normed = layer_norm(third, final_gain, final_shift).astype(BF)
        final_hidden = dot(final_normed, latent_up)
        final_active = jax.nn.gelu(final_hidden).astype(BF)
        result_add = (self_add + dot(final_active, latent_down)).astype(BF)
        grad_final_hidden = gelu_back(final_hidden, dot_nt(grad_low, latent_down)).astype(BF)
        back_third, grad_final_gain, grad_final_shift = norm_back(
            third, final_gain, dot_nt(grad_final_hidden, latent_up)
        )
        grad_third_low = (grad_low.astype(F32) + back_third).astype(BF)
        grad_mixed = dot_nt(grad_third_low, self_out).astype(BF)
        grad_queries, grad_pairs = attend_back(grad_mixed, self_low, packed, pairs, rows, whole_rows)
        grad_pairs = lax.psum_scatter(
            grad_pairs, "lat", scatter_dimension=0, tiled=True, axis_index_groups=same_item
        )
        grad_packed = jnp.concatenate([grad_queries, grad_pairs], axis=1)
        back_second, grad_self_gain, grad_self_shift = norm_back(
            second_wide, self_gain, dot_nt(grad_packed, self_packed)
        )
        second_add = (back_third + back_second).astype(BF)
        item_sums = jnp.stack([grad_self_gain, grad_self_shift, grad_final_gain, grad_final_shift])
    second_got = reshare(second_add)
    item_pairs = (
        (final_active, grad_low),
        (final_normed, grad_final_hidden),
        (self_mixed, grad_third_low),
        (self_normed, grad_packed),
    )
    final_pairs, packed_pairs = item_pairs[:3], item_pairs[3:]
    if sub > 1:
        final_other = half_plain(final_pairs, 1 - core, item, X_FIRST, ways).astype(BF)
        packed_other = half_plain(packed_pairs, 1 - core, item, Y_FIRST, ways).astype(BF)
    final_got = lax.ppermute(final_other, "lat", swap)
    packed_got = lax.ppermute(packed_other, "lat", swap)
    final_sent, final_kept = half_grads(final_pairs, core, item, X_FIRST, ways, final_got)
    packed_sent, packed_kept = half_grads(packed_pairs, core, item, Y_FIRST, ways, packed_got)
    second_got, result_add, *unused = tie((second_got, result_add, final_sent, packed_sent))
    result_got = reshare(result_add)
    final_got = swap_items(final_sent, 1)
    packed_got = swap_items(packed_sent, 2)

    back_args = (
        place, second_got, upstream, first_sum, slopes, cross_vectors, from_pixels, cross_up, cross_down,
        raw_all, normal, asks, mixed, kept, scores, top, cross_active, cross_normed, value_pad,
    )
    if block % 128 == 0:
        latent_side = (
            to_pixels, residual, latent_gain[None], out_weight, normed, latent_queries, item_sums
        )
        (
            parts_pix, grad_latents, small_mine, small_other, net_mine, net_other, out_mine, out_other
        ) = cross_back(*back_args, latent_side, groups)
    else:
        (
            grad_second_low, grad_cross_hidden, grad_first, grad_first_low, cross_sums, moves, parts_pix, pixel_sums,
            core_value, cross_mixed,
        ) = cross_back(*back_args, (), groups)
        cross_pairs = ((cross_active, grad_second_low), (cross_normed, grad_cross_hidden))
        net_mine, net_other, out_mine, out_other = [
            half_plain(pairs, half, item, order, ways).astype(BF)
            for pairs, order in ((cross_pairs, X_FIRST), (((cross_mixed, grad_first_low),), Y_FIRST))
            for half in (core, 1 - core)
        ]
        grad_latents, small_mine, small_other = last_block(
            core, item, ways, moves, to_pixels, residual, grad_first, latent_gain[None], core_value, out_weight,
            normed, latent_queries, jnp.concatenate([cross_sums, item_sums, jnp.zeros((2, width), F32)]), pixel_sums,
        )
    (
        parts_pix, grad_latents, small_mine, small_other, net_mine, net_other, out_mine, out_other,
        final_got, packed_got, result_got,
    ) = tie(
        (
            parts_pix, grad_latents, small_mine, small_other, net_mine, net_other, out_mine, out_other,
            final_got, packed_got, result_got,
        )
    )
    grad_pn = lax.psum_scatter(parts_pix, "lat", scatter_dimension=0, tiled=False)
    net_got = lax.ppermute(net_other, "lat", swap)
    out_got = lax.ppermute(out_other, "lat", swap)
    final_two, packed_two = add(final_kept[1], final_got[1]), add(packed_kept[1], packed_got[1])
    final_two, packed_two = swap_items(final_two, 2), swap_items(packed_two, 1)
    small_got = lax.ppermute(small_other, "lat", swap)
    net_first, out_first = add(net_mine[:2], net_got[:2]), add(out_mine[:2], out_got[:2])
    small_first = add(small_mine[:2], small_got[:2])
    final_two, packed_two, net_first, out_first, small_first = tie(
        (final_two, packed_two, net_first, out_first, small_first)
    )
    first_got = [swap_items(net_first, 1), swap_items(out_first, 2), swap_items(small_first, 2)]
    item_here = jnp.concatenate(
        [
            total([final_kept[0], final_got[0], final_two]).astype(BF),
            total([packed_kept[0], packed_got[0], packed_two]).astype(BF),
        ],
        axis=1,
    )
    grad_pn, *first_got = tie((grad_pn, *first_got))
    item_part = over_chips_whole(item_here.reshape(chips, block, -1))
    flows = ((net_mine, net_got, 2), (out_mine, out_got, 1), (small_mine, small_got, 1))
    hops = [
        swap_items(total([mine[3], got[3], first[1]]).astype(BF), hop)
        for (mine, got, hop), first in zip(flows, first_got)
    ]
    item_part, *hops = tie((item_part, *hops))
    net_here, out_here, small_here = [
        total([mine[2], got[2], first[0], last]).astype(BF)
        for (mine, got, hop), first, last in zip(flows, first_got, hops)
    ]
    lines = small_here.shape[0] // (chips // 2)
    pieces = jnp.stack(
        [
            jnp.concatenate(
                [
                    whole[z * block : (z + 1) * block, k * block : (k + 1) * block]
                    for whole in (net_here, out_here)
                    for k in range(whole.shape[1] // block)
                ]
                + [small_here[z // 2 * lines : (z // 2 + 1) * lines, z % 2 * block : (z % 2 + 1) * block]]
            )
            for z in range(chips)
        ]
    )
    rest = near_chips(lambda z: lax.dynamic_index_in_dim(pieces, z, 0, keepdims=False))
    item_parts = [item_part] + [swap_items(item_part, m) for m in range(1, groups)]
    tied = tie((*rest, *item_parts))
    rest, item_parts = total(tied[: len(rest)]).astype(BF), jnp.stack(tied[len(rest) :])
    rest_parts = gather_items(rest)
    quarter = width // groups
    grad_latent_down, grad_latent_up, grad_self_out = [
        weight_of(item_parts[:, :, at * quarter : (at + 1) * quarter]) for at in range(3)
    ]
    grad_self_packed = weight_of(item_parts[:, :, 3 * quarter :])
    tall = quarter // block * block
    grad_cross_down, grad_cross_up, grad_out_weight = [
        weight_of(
            rest_parts[:, at * tall : (at + 1) * tall]
            .reshape(groups, quarter // block, block, block)
            .transpose(0, 2, 1, 3)
            .reshape(groups, block, quarter)
        )
        for at in range(3)
    ]
    small = jnp.concatenate(by_item(rest_parts[:, 3 * tall :]), axis=0).astype(F32)
    result = second_sum + result_got.astype(F32)
    grad_pn = grad_pn.astype(F32)[:cin]
    pix_hat, pix_inv = norm_parts(pixels[0].T.astype(F32), 0)
    scaled = grad_pn * pixel_gain[:, None]
    grad_pixels = pix_inv * (
        scaled
        - jnp.mean(scaled, axis=0, keepdims=True)
        - pix_hat * jnp.mean(scaled * pix_hat, axis=0, keepdims=True)
    )
    grad_query_weight = dot_tn(small[channels : 2 * channels].astype(BF), key_pad) * score_scale
    grad_key_weight = small[2 * channels : 2 * channels + cin] * score_scale
    grad_value_weight = small[:cin]
    sums = small[3 * channels + 2 :]
    count = -(-channels // block)
    grad_pixel_gain = sums[:count].reshape(-1)[:cin]
    grad_pixel_shift = sums[count : 2 * count].reshape(-1)[:cin]
    gains = [small[3 * channels], small[3 * channels + 1]] + [sums[2 * count + at] for at in range(6)]
    shape = (1, items, lat_rows, width)
    return (
        result.reshape(shape),
        grad_latents.reshape(shape),
        grad_pixels.T[None],
        gains[0],
        gains[1],
        grad_pixel_gain,
        grad_pixel_shift,
        grad_query_weight,
        grad_key_weight,
        grad_value_weight,
        grad_out_weight,
        gains[2],
        gains[3],
        grad_cross_up,
        grad_cross_down,
        gains[4],
        gains[5],
        grad_self_packed,
        grad_self_out,
        gains[6],
        gains[7],
        grad_latent_up,
        grad_latent_down,
    )


def solution(mesh):
    rows = P("items", None, "lat", None)
    in_specs = (rows, P("items", "lat", None), P("items", None), rows) + (P(),) * 20
    lane = P("lat")
    tall = P("lat", None)
    wide = P(None, "lat")
    out_specs = (
        rows,
        rows,
        P("items", "lat", None),
        lane,
        lane,
        P(),
        P(),
        tall,
        wide,
        wide,
        tall,
        lane,
        lane,
        tall,
        tall,
        lane,
        lane,
        tall,
        tall,
        lane,
        lane,
        tall,
        tall,
    )
    return jax.shard_map(
        on_device, mesh=mesh, in_specs=in_specs, out_specs=out_specs, check_vma=False
    )
```

```python
import math

import jax
import jax.numpy as jnp
from jax import lax
from jax.experimental import pallas as pl
from jax.experimental.pallas import tpu as pltpu
from jax.sharding import PartitionSpec as P

HEADS = 8
HEAD = 128
X_FIRST = (1, 3, 0, 2)
Y_FIRST = (2, 3, 0, 1)
BF = jnp.bfloat16
F32 = jnp.float32


def norm_parts(values, axis=-1):
    centre = values - jnp.mean(values, axis=axis, keepdims=True)
    spread = jnp.mean(centre * centre, axis=axis, keepdims=True)
    inv = lax.rsqrt(spread + 1e-05)
    return centre * inv, inv


def layer_norm(values, gain, shift):
    hat, unused = norm_parts(values)
    return hat * gain + shift


def norm_back(values, gain, upstream):
    hat, inv = norm_parts(values)
    scaled = upstream * gain
    back = inv * (
        scaled
        - jnp.mean(scaled, axis=-1, keepdims=True)
        - hat * jnp.mean(scaled * hat, axis=-1, keepdims=True)
    )
    return back, jnp.sum(upstream * hat, axis=0), jnp.sum(upstream, axis=0)


def gelu_back(hidden, upstream):
    unused, pullback = jax.vjp(jax.nn.gelu, hidden)
    return pullback(upstream)[0]


def dot(left, right):
    return jnp.dot(left, right, preferred_element_type=F32)


def dot_tn(left, right):
    return lax.dot_general(left, right, (((0,), (0,)), ((), ())), preferred_element_type=F32)


def dot_nt(left, right):
    return lax.dot_general(left, right, (((1,), (1,)), ((), ())), preferred_element_type=F32)


def softmax(scores):
    raised = jnp.exp(scores - jnp.max(scores, axis=-1, keepdims=True))
    return raised / jnp.sum(raised, axis=-1, keepdims=True)


def attend_kernel(query, key, value, out, kept):
    scores = dot_nt(query[...], key[...]) * (1.0 / math.sqrt(HEAD))
    raised = jnp.exp(scores - jnp.max(scores, axis=-1, keepdims=True))
    weights = (raised * (1.0 / jnp.sum(raised, axis=-1, keepdims=True))).astype(BF)
    kept[0] = weights
    out[...] = dot(weights, value[...]).astype(BF)


def attend(queries, pairs, rows, whole_rows):
    column = lambda at: pl.BlockSpec((whole_rows, HEAD), lambda h: (0, h + at))
    own = pl.BlockSpec((rows, HEAD), lambda h: (0, h))
    return pl.pallas_call(
        attend_kernel,
        grid=(HEADS,),
        in_specs=[own, column(0), column(HEADS)],
        out_specs=[own, pl.BlockSpec((1, rows, whole_rows), lambda h: (h, 0, 0))],
        out_shape=[
            jax.ShapeDtypeStruct((rows, HEADS * HEAD), BF),
            jax.ShapeDtypeStruct((HEADS, rows, whole_rows), BF),
        ],
        compiler_params=pltpu.CompilerParams(vmem_limit_bytes=40 << 20),
        name="attend",
    )(queries, pairs, pairs)


def attend_back_kernel(grad, weights_ref, query, key, value, grad_query, grad_pair):
    at = pl.multiple_of(pl.program_id(0) * HEAD, HEAD)
    also = pl.multiple_of(pl.program_id(0) * HEAD + HEADS * HEAD, HEAD)
    weights_low = weights_ref[0]
    weights = weights_low.astype(F32)
    upstream = grad[...]
    grad_weights = dot_nt(upstream, value[...])
    grad_pair[:, pl.ds(also, HEAD)] = dot_tn(weights_low, upstream).astype(BF)
    inner = jnp.sum(weights * grad_weights, axis=-1, keepdims=True)
    spread = (weights * (grad_weights - inner)).astype(BF)
    scale = 1.0 / math.sqrt(HEAD)
    grad_query[...] = (dot(spread, key[...]) * scale).astype(BF)
    grad_pair[:, pl.ds(at, HEAD)] = (dot_tn(spread, query[...]) * scale).astype(BF)


def attend_back(grad, weights, queries, pairs, rows, whole_rows):
    column = lambda at: pl.BlockSpec((whole_rows, HEAD), lambda h: (0, h + at))
    own = pl.BlockSpec((rows, HEAD), lambda h: (0, h))
    return pl.pallas_call(
        attend_back_kernel,
        grid=(HEADS,),
        in_specs=[
            own,
            pl.BlockSpec((1, rows, whole_rows), lambda h: (h, 0, 0)),
            own,
            column(0),
            column(HEADS),
        ],
        out_specs=[own, pl.BlockSpec((whole_rows, 2 * HEADS * HEAD), lambda h: (0, 0))],
        out_shape=[
            jax.ShapeDtypeStruct((rows, HEADS * HEAD), BF),
            jax.ShapeDtypeStruct((whole_rows, 2 * HEADS * HEAD), BF),
        ],
        compiler_params=pltpu.CompilerParams(vmem_limit_bytes=40 << 20),
        name="attend_back",
    )(grad, weights, queries, pairs, pairs)


def half_columns(left, half, blocks):
    step = left.shape[1] // (2 * blocks)
    return jnp.concatenate(
        [left[:, pl.ds(pl.multiple_of((2 * z + half) * step, step), step)] for z in range(blocks)], axis=1
    ).T


def half_body(order, blocks, place, near, made, extra, need, flush):
    (turned,) = extra
    count = (len(near) - 1) // 2
    added = near[2 * count]
    groups = len(order)
    for index in range(count):
        need(index)
        turned[index] = half_columns(near[index], place[0], blocks)
    need(*range(count, 2 * count + 1))
    cut = len(made) > groups
    for p in (1, 0, 2, 3):
        at = 0
        outs = [p + (cut and p > 1)] if p != 1 or not cut else [1, 2]
        for index, right in enumerate(near[count : 2 * count]):
            size = right.shape[1] // groups
            lanes = pl.ds(pl.multiple_of((place[1] ^ order[p]) * size, HEAD), size)
            value = dot(turned[index], right[:, lanes]) + added[p, :, at : at + size].astype(F32)
            value = value.astype(BF)
            lines = 0
            for out in outs:
                count_of = made[out].shape[0]
                made[out][:, at : at + size] = value[lines : lines + count_of]
                lines += count_of
            at += size
        flush(*outs)


def half_plain(pairs, half, item, order, ways):
    blocks = ways // 2
    rows, width = pairs[0][0].shape
    groups = len(order)
    outs = []
    for left, right in pairs:
        columns = lax.dynamic_index_in_dim(
            left.reshape(rows, blocks, 2, width // ways), half, 2, keepdims=False
        ).reshape(rows, width // 2)
        value = dot_tn(columns, right).reshape(width // 2, groups, -1).transpose(1, 0, 2)
        outs.append(value)
    value = jnp.concatenate(outs, axis=2)
    return jnp.stack([lax.dynamic_index_in_dim(value, item ^ m, 0, keepdims=False) for m in order])


def half_grads(pairs, half, item, order, ways, added, cut=False):
    rows, width = pairs[0][0].shape
    blocks, groups = ways // 2, len(order)
    total = sum(right.shape[1] for unused, right in pairs) // groups
    if (width // ways) % 128:
        value = (half_plain(pairs, half, item, order, ways) + added.astype(F32)).astype(BF)
        parts = [value[p] for p in range(groups)]
        if cut:
            parts[1:2] = [parts[1][: width // 4], parts[1][width // 4 :]]
        return parts
    shapes = [jax.ShapeDtypeStruct((width // 2, total), BF)] * groups
    if cut:
        shapes[1:2] = [jax.ShapeDtypeStruct((width // 4, total), BF)] * 2
    return streamed(
        "half_grads",
        lambda *refs: half_body(order, blocks, *refs),
        jnp.stack([half, item]).astype(jnp.int32),
        [left for left, unused in pairs] + [right for unused, right in pairs] + [added],
        shapes,
        [pltpu.VMEM((len(pairs), width // 2, rows), BF)],
    )


def small_parts(
    core, item, moves, core_in, residual, grad_first, gain, core_value, out_w, normed, queries,
    sums, item_sums, pixel_sums, grad_latents, mine, other, stacked, rest,
):
    rows, width = residual.shape
    block = mine.shape[2] // 2
    chips = width // block // 2
    channels = moves.shape[1]
    stacked[...] = jnp.zeros(stacked.shape, F32)

    def back(part):
        grad_normed = dot_nt(moves[part, :], core_in[...])
        hat, inv = norm_parts(residual[part, :])
        stacked[0:1, :] += jnp.sum(grad_normed * hat, axis=0, keepdims=True)
        stacked[1:2, :] += jnp.sum(grad_normed, axis=0, keepdims=True)
        grad_latents[part, :] = grad_first[part, :] + norm_slope(hat, inv, gain[...], grad_normed)

    each_part(rows, back)
    stacked[8:10, :] = sums[...]
    stacked[10:14, :] = item_sums[...]
    for at in range(2):
        line = jnp.broadcast_to(pixel_sums[at], (channels, 128)).T[0:1, :]
        line = jnp.concatenate([line, jnp.zeros((1, -channels % 128), F32)], axis=1)
        for k in range(line.shape[1] // 128):
            for j in range(width // block):
                stacked[2 + 3 * at + k : 3 + 3 * at + k, j * block : j * block + 128] = line[
                    :, k * 128 : (k + 1) * 128
                ]
    rest[0:channels, :] = dot_nt(core_value, out_w[...]).astype(BF)
    rest[channels : 2 * channels, :] = dot_tn(moves[...], normed[...]).astype(BF)
    rest[2 * channels : 3 * channels, :] = dot_tn(moves[...], queries[...]).astype(BF)
    rest[3 * channels :, :] = stacked[...].astype(BF)
    size = rest.shape[0] // 4
    for p, m in enumerate(Y_FIRST):
        lines = pl.ds(pl.multiple_of((item ^ m) * size, 16), size)
        for out, half in ((mine, core), (other, 1 - core)):
            for z in range(chips):
                lanes = pl.ds(pl.multiple_of((2 * z + half) * block, block), block)
                out[p, z // 2 * size : (z // 2 + 1) * size, z % 2 * block : (z % 2 + 1) * block] = rest[
                    lines, lanes
                ]


def small_lines(channels):
    return 3 * channels + 16


def last_block(
    core, item, ways, moves, core_in, residual, grad_first, gain, core_value, out_w, normed, queries,
    vectors, pixel_sums,
):
    rows, width = residual.shape
    channels = moves.shape[1]
    block, chips = width // ways, ways // 2
    grad_normed = dot_nt(moves, core_in)
    back, grad_gain, grad_shift = norm_back(residual, gain[0], grad_normed)
    sums = jnp.pad(pixel_sums.reshape(2, channels), ((0, 0), (0, -channels % block)))
    lines = sums.reshape(-1, 1, block)
    lines = jnp.broadcast_to(lines, (lines.shape[0], ways, block)).reshape(-1, width)
    stack = [
        dot_nt(core_value, out_w),
        dot_tn(moves, normed),
        dot_tn(moves, queries),
        grad_gain[None],
        grad_shift[None],
        lines,
        vectors,
    ]
    count = sum(value.shape[0] for value in stack)
    stack = jnp.concatenate(stack + [jnp.zeros((-count % 64, width), F32)]).astype(BF)
    size = stack.shape[0] // 4
    stack = stack.reshape(4, size, chips // 2, 2, 2, block)
    halves = []
    for half in (core, 1 - core):
        value = lax.dynamic_index_in_dim(stack, half, 4, keepdims=False)
        value = value.transpose(0, 2, 1, 3, 4).reshape(4, chips // 2 * size, 2 * block)
        halves.append(
            jnp.stack([lax.dynamic_index_in_dim(value, item ^ m, 0, keepdims=False) for m in Y_FIRST])
        )
    return grad_first + back, halves[0], halves[1]


GELU_A = 0.044715
GELU_C = math.sqrt(2.0 / math.pi)
PART = 256


def gelu_both(hidden):
    square = hidden * hidden
    bent = jnp.tanh(hidden * (GELU_C + (GELU_C * GELU_A) * square))
    half = 0.5 + 0.5 * bent
    slope = half + (0.5 * hidden) * (1.0 - bent * bent) * (GELU_C + (3.0 * GELU_C * GELU_A) * square)
    return hidden * half, slope


def norm_slope(hat, inv, gain, upstream):
    scaled = upstream * gain
    centre = jnp.mean(scaled, axis=-1, keepdims=True)
    along = jnp.mean(scaled * hat, axis=-1, keepdims=True)
    return inv * (scaled - centre - hat * along)


def each_part(rows, body):
    size = min(PART, rows)

    def step(r, carry):
        body(pl.ds(pl.multiple_of(r * size, size), size))
        return carry

    lax.fori_loop(0, rows // size, step, 0, unroll=True)


def each_head(body):
    def step(h, carry):
        body(h)
        return carry

    lax.fori_loop(0, HEADS, step, 0, unroll=2)


def write_halves(pairs, outs, item, order, blocks, turned):
    at = 0
    for left, right in pairs:
        size = right.shape[1] // len(order)
        for out, half in outs:
            turned[...] = half_columns(left, half, blocks)
            for p, m in enumerate(order):
                lanes = pl.ds(pl.multiple_of((item ^ m) * size, HEAD), size)
                out[p, :, at : at + size] = dot(turned[...], right[:, lanes]).astype(BF)
        at += size


def item_body(place, near, made, extra, need, flush):
    second, vectors, packed_w0, packed_w1, packed_w2, out_w, up_w, down_w, grad_low = near
    (
        self_normed, self_mixed, final_normed, final_active, result_add, grad_final_hidden, grad_third_low,
        second_add, grad_packed, sums, other_first, other_packed,
    ) = made
    packed, raised_low, inverse, mixed, back_third, grad_mixed, turned = extra
    packed_w = (packed_w0, packed_w1, packed_w2)
    rows, width = second.shape
    need(0, 1)
    sums[...] = jnp.zeros(sums.shape, F32)

    def normalize(part):
        hat, unused = norm_parts(second[part, :].astype(F32))
        self_normed[part, :] = (hat * vectors[0:1, :] + vectors[1:2, :]).astype(BF)

    each_part(rows, normalize)
    flush(0)
    for c in range(3):
        need(2 + c)

        def project(part):
            packed[part, c * width : (c + 1) * width] = dot(
                self_normed[part, :], packed_w[c][...]
            ).astype(BF)

        each_part(rows, project)

    def lanes(h, group):
        return pl.ds(pl.multiple_of(h * HEAD + group * width, HEAD), HEAD)

    scale = 1.0 / math.sqrt(HEAD)

    def attend_head(h):
        scores = dot_nt(packed[:, lanes(h, 0)], packed[:, lanes(h, 1)])
        peak = jnp.max(scores, axis=-1, keepdims=True)
        raised = jnp.exp2((scores - peak) * (scale * math.log2(math.e)))
        inv = 1.0 / jnp.sum(raised, axis=-1, keepdims=True)
        low = raised.astype(BF)
        raised_low[h] = low
        inverse[h] = inv
        mixed[:, lanes(h, 0)] = dot(low, packed[:, lanes(h, 2)]) * inv

    each_head(attend_head)
    need(5, 6, 7, 8)

    def middle(part):
        low = mixed[part, :].astype(BF)
        self_mixed[part, :] = low
        added = dot(low, out_w[...])
        hat, inv = norm_parts(second[part, :].astype(F32) + added)
        normed = (hat * vectors[2:3, :] + vectors[3:4, :]).astype(BF)
        final_normed[part, :] = normed
        active, slope = gelu_both(dot(normed, up_w[...]))
        active = active.astype(BF)
        final_active[part, :] = active
        result_add[part, :] = (added + dot(active, down_w[...])).astype(BF)
        upstream = grad_low[part, :]
        grad_hidden = (dot_nt(upstream, down_w[...]) * slope).astype(BF)
        grad_final_hidden[part, :] = grad_hidden
        grad_normed = dot_nt(grad_hidden, up_w[...])
        sums[2:3, :] += jnp.sum(grad_normed * hat, axis=0, keepdims=True)
        sums[3:4, :] += jnp.sum(grad_normed, axis=0, keepdims=True)
        back = norm_slope(hat, inv, vectors[2:3, :], grad_normed)
        back_third[part, :] = back
        third_low = (upstream.astype(F32) + back).astype(BF)
        grad_third_low[part, :] = third_low
        grad_mixed[part, :] = dot_nt(third_low, out_w[...]).astype(BF)

    each_part(rows, middle)
    flush(1, 2, 3, 4, 5, 6)

    def attend_back_head(h):
        upstream = grad_mixed[:, lanes(h, 0)]
        low = raised_low[h]
        inv = inverse[h]
        up32 = upstream.astype(F32)
        inner = jnp.sum(up32 * mixed[:, lanes(h, 0)], axis=-1, keepdims=True)
        grad_packed[:, lanes(h, 2)] = dot_tn(low, (up32 * inv).astype(BF)).astype(BF)
        grad_weights = dot_nt(upstream, packed[:, lanes(h, 2)])
        spread = (low.astype(F32) * ((grad_weights - inner) * (inv * scale))).astype(BF)
        grad_packed[:, lanes(h, 0)] = dot(spread, packed[:, lanes(h, 1)]).astype(BF)
        grad_packed[:, lanes(h, 1)] = dot_tn(spread, packed[:, lanes(h, 0)]).astype(BF)

    each_head(attend_back_head)
    flush(8)

    def last(part):
        hat, inv = norm_parts(second[part, :].astype(F32))
        grad_normed = dot_nt(grad_packed[part, :width], packed_w[0][...])
        for c in range(1, 3):
            grad_normed += dot_nt(grad_packed[part, c * width : (c + 1) * width], packed_w[c][...])
        sums[0:1, :] += jnp.sum(grad_normed * hat, axis=0, keepdims=True)
        sums[1:2, :] += jnp.sum(grad_normed, axis=0, keepdims=True)
        back = norm_slope(hat, inv, vectors[0:1, :], grad_normed)
        second_add[part, :] = (back_third[part, :] + back).astype(BF)

    each_part(rows, last)
    flush(7, 9)
    blocks = width // 2 // HEAD
    write_halves(
        ((final_active, grad_low), (final_normed, grad_final_hidden), (self_mixed, grad_third_low)),
        ((other_first, 1 - place[0]),), place[1], X_FIRST, blocks, turned,
    )
    flush(10)
    write_halves(
        ((self_normed, grad_packed),), ((other_packed, 1 - place[0]),), place[1], Y_FIRST, blocks, turned
    )


def item_block(place, groups, second, grad_low, vectors, self_packed, self_out, latent_up, latent_down):
    rows, width = second.shape
    low = jax.ShapeDtypeStruct((rows, width), BF)
    half = jax.ShapeDtypeStruct((groups, width // 2, 3 * width // groups), BF)
    packed_parts = [(self_packed, c * width, width) for c in range(3)]
    (
        self_normed, self_mixed, final_normed, final_active, result_add, grad_final_hidden, grad_third_low,
        second_add, grad_packed, sums, other_first, other_packed,
    ) = streamed(
        "item_block",
        item_body,
        place,
        [second, vectors, *packed_parts, self_out, latent_up, latent_down, grad_low],
        [low] * 8
        + [
            jax.ShapeDtypeStruct((rows, 3 * width), BF),
            jax.ShapeDtypeStruct((4, width), F32),
            half,
            half,
        ],
        [
            pltpu.VMEM((rows, 3 * width), BF),
            pltpu.VMEM((HEADS, rows, rows), BF),
            pltpu.VMEM((HEADS, rows, 1), F32),
            pltpu.VMEM((rows, width), F32),
            pltpu.VMEM((rows, width), F32),
            pltpu.VMEM((rows, width), BF),
            pltpu.VMEM((width // 2, rows), BF),
        ],
    )
    return (
        result_add, second_add, self_normed, grad_packed, self_mixed, grad_third_low,
        final_normed, final_active, grad_final_hidden, sums, other_first, other_packed,
    )


def streamed(name, body, place, ins, outs, scratch):
    cuts = [value[1:] if isinstance(value, tuple) else None for value in ins]
    ins = [value[0] if isinstance(value, tuple) else value for value in ins]
    shapes = [
        value.shape if cut is None else value.shape[1:] if len(cut) == 1 else (value.shape[0], cut[1])
        for value, cut in zip(ins, cuts)
    ]
    anywhere = pl.BlockSpec(memory_space=pl.ANY)

    def kernel(place_ref, *refs):
        sources, refs = refs[: len(ins)], refs[len(ins) :]
        targets, refs = refs[: len(outs)], refs[len(outs) :]
        near, refs = refs[: len(ins)], refs[len(ins) :]
        made, refs = refs[: len(outs)], refs[len(outs) :]
        extra, (in_sems, out_sems) = refs[:-2], refs[-2:]
        sources = [
            ref if cut is None else ref.at[cut[0]] if len(cut) == 1 else ref.at[:, pl.ds(*cut)]
            for ref, cut in zip(sources, cuts)
        ]
        loads = [pltpu.make_async_copy(a, b, in_sems.at[i]) for i, (a, b) in enumerate(zip(sources, near))]
        stores = [pltpu.make_async_copy(a, b, out_sems.at[i]) for i, (a, b) in enumerate(zip(made, targets))]
        left_in, left_out = list(range(len(ins))), list(range(len(outs)))
        for load in loads:
            load.start()

        def need(*which):
            for i in which:
                left_in.remove(i)
                loads[i].wait()

        def flush(*which):
            for i in which:
                left_out.remove(i)
                stores[i].start()

        body(place_ref, near, made, extra, need, flush)
        need(*list(left_in))
        flush(*list(left_out))
        for store in stores:
            store.wait()

    return pl.pallas_call(
        kernel,
        in_specs=[pl.BlockSpec(memory_space=pltpu.SMEM)] + [anywhere] * len(ins),
        out_specs=[anywhere] * len(outs),
        out_shape=list(outs),
        scratch_shapes=[pltpu.VMEM(shape, value.dtype) for shape, value in zip(shapes, ins)]
        + [pltpu.VMEM(value.shape, value.dtype) for value in outs]
        + list(scratch)
        + [pltpu.SemaphoreType.DMA((len(ins),)), pltpu.SemaphoreType.DMA((len(outs),))],
        compiler_params=pltpu.CompilerParams(vmem_limit_bytes=60 << 20),
        name=name,
    )(place, *ins)


def pixel_hat(values, cin):
    real = lax.broadcasted_iota(jnp.int32, (values.shape[0], 1), 0) < cin
    portion = 1.0 / cin.astype(F32)
    centre = jnp.where(real, values - jnp.sum(values, axis=0, keepdims=True) * portion, 0.0)
    return centre * lax.rsqrt(jnp.sum(centre * centre, axis=0, keepdims=True) * portion + 1e-05)


def each_block(count, body):
    def step(n, carry):
        body(n)
        return carry

    lax.fori_loop(0, count, step, 0, unroll=2)


def cross_body(place, near, made, extra, need, flush):
    asks, gain, shift, raw, owner, core_out, residual, vectors, up_w, down_w = near
    (
        normal, scores, kept, mixed, top, first_sum, cross_normed, slopes, cross_active, second_sum, second
    ) = made
    (heap,) = extra
    ways, channels, size = normal.shape
    rows = asks.shape[0]
    lat_rows = heap.shape[0]
    at = pl.multiple_of(place[2] * lat_rows, lat_rows)
    large = pl.ds(at, lat_rows)
    need(0, 1, 2, 3)
    columns = lax.broadcasted_iota(jnp.int32, (1, size), 1)
    top[...] = jnp.full(top.shape, -1e30, F32)

    def score(n):
        value = (pixel_hat(raw[n].astype(F32), place[3]) * gain[...] + shift[...]).astype(BF)
        normal[n] = value
        places = columns + n * size
        found = dot(asks[large, :], value)
        found = jnp.where((places >= place[0]) & (places < place[1]), found, -1e30)
        scores[n] = found
        top[...] = jnp.maximum(top[...], jnp.max(found, axis=1, keepdims=True))

    each_block(ways, score)
    flush(0, 1)
    need(4)
    edge = jnp.where(
        columns < place[0], normal[0].astype(F32), normal[ways - 1].astype(F32)
    ).astype(BF)
    row_item = lax.broadcasted_iota(jnp.int32, (rows, 1), 0) // lat_rows
    inside = (owner[...] == row_item) & (place[2] != row_item)
    found = jnp.where(inside, dot(asks[...], edge), -1e30)
    raised = jnp.exp(found - jnp.max(found, axis=1, keepdims=True))
    weights = raised * (1.0 / jnp.sum(raised, axis=1, keepdims=True))
    weights = jnp.where(inside, weights, 0.0).astype(BF)
    kept[...] = weights
    mixed[...] = dot_nt(weights, edge)
    heap[...] = jnp.zeros(heap.shape, F32)
    peak = top[...]

    def gather(n, carry):
        raised = jnp.exp(scores[n] - peak)
        heap[...] += dot_nt(raised.astype(BF), normal[n])
        return carry + jnp.sum(raised, axis=1, keepdims=True)

    whole = lax.fori_loop(0, ways, gather, jnp.zeros((lat_rows, 1), F32))
    mixed[large, :] = heap[...] * (1.0 / whole)
    top[...] = peak + jnp.log(whole)
    flush(2, 3, 4)
    need(5, 6, 7, 8, 9)

    def net(part):
        first = residual[part, :] + dot(mixed[part, :].astype(BF), core_out[...])
        first_sum[part, :] = first
        hat, unused = norm_parts(first)
        normed = (hat * vectors[0:1, :] + vectors[1:2, :]).astype(BF)
        cross_normed[part, :] = normed
        active, slope = gelu_both(dot(normed, up_w[...]))
        active = active.astype(BF)
        cross_active[part, :] = active
        slopes[part, :] = slope
        value = first + dot(active, down_w[...])
        second_sum[part, :] = value
        second[part, :] = value.astype(BF)

    each_part(rows, net)


def cross_back_body(place, near, made, extra, need, flush):
    (
        got, upstream, slopes, down_w, up_w, first_sum, vectors, core_out, normal, mixed, kept, asks, scores, top,
        raw, value_w, cross_active, cross_normed, *latent_side,
    ) = near
    grad, corner, heap, turned, *small_scratch = extra
    if not latent_side:
        (
            grad_second_low, grad_cross_hidden, grad_first, grad_first_low, sums, moves, pix, pixel_sums,
            core_value, cross_mixed,
        ) = made
    else:
        grad_second_low, grad_cross_hidden, grad_first_low, moves, pixel_sums, sums, grad_first, cross_mixed = (
            small_scratch[:8]
        )
        pix, grad_latents, small_mine, small_other, *halves = made
    ways, channels, size = normal.shape
    rows = asks.shape[0]
    lat_rows = heap.shape[0]
    at = pl.multiple_of(place[2] * lat_rows, lat_rows)
    large = pl.ds(at, lat_rows)
    sums[...] = jnp.zeros(sums.shape, F32)
    pixel_sums[...] = jnp.zeros(pixel_sums.shape, F32)
    need(0, 1, 2, 3, 4, 5, 6, 7)

    def net(part):
        grad_second = upstream[part, :] + got[part, :].astype(F32)
        low = grad_second.astype(BF)
        grad_second_low[part, :] = low
        grad_hidden = (dot_nt(low, down_w[...]) * slopes[part, :]).astype(BF)
        grad_cross_hidden[part, :] = grad_hidden
        grad_normed = dot_nt(grad_hidden, up_w[...])
        hat, inv = norm_parts(first_sum[part, :])
        sums[0:1, :] += jnp.sum(grad_normed * hat, axis=0, keepdims=True)
        sums[1:2, :] += jnp.sum(grad_normed, axis=0, keepdims=True)
        value = grad_second + norm_slope(hat, inv, vectors[0:1, :], grad_normed)
        grad_first[part, :] = value
        low = value.astype(BF)
        grad_first_low[part, :] = low
        grad[part, :] = dot_nt(low, core_out[...]).astype(BF)

    each_part(rows, net)
    if not latent_side:
        flush(0, 1, 2, 3, 4)
    need(8, 9, 10, 11, 12, 13, 14)
    columns = lax.broadcasted_iota(jnp.int32, (1, size), 1)
    early = columns < place[0]
    edge = jnp.where(early, normal[0].astype(F32), normal[ways - 1].astype(F32)).astype(BF)
    deltas = jnp.sum(grad[...].astype(F32) * mixed[...], axis=1, keepdims=True)
    weights = kept[...]
    spread = (weights.astype(F32) * (dot(grad[...], edge) - deltas)).astype(BF)
    moves[...] = dot_nt(spread, edge).astype(BF)
    corner[...] = dot_tn(asks[...], spread) + dot_tn(grad[...], weights)
    heap[...] = jnp.zeros(heap.shape, F32)
    own = grad[large, :]
    own_asks = asks[large, :]
    deltas = jnp.sum(own.astype(F32) * mixed[large, :], axis=1, keepdims=True)
    level = top[...]

    def block(n):
        value = normal[n]
        weights = jnp.exp(scores[n] - level)
        spread = (weights * (dot(own, value) - deltas)).astype(BF)
        heap[...] += dot_nt(spread, value)
        part = dot_tn(own_asks, spread) + dot_tn(own, weights.astype(BF))
        use = ((n == 0) & early) | ((n == ways - 1) & jnp.logical_not(early))
        part = part + jnp.where(use, corner[...], 0.0)
        pix[n] = part.astype(BF)
        hat = pixel_hat(raw[n].astype(F32), place[3])
        pixel_sums[0] += jnp.sum(part * hat, axis=1, keepdims=True)
        pixel_sums[1] += jnp.sum(part, axis=1, keepdims=True)

    each_block(ways, block)
    moves[large, :] = heap[...].astype(BF)
    if latent_side:
        flush(0)
    else:
        flush(5, 6, 7)
    need(15, 16, 17)
    mixed_low = mixed[...].astype(BF)
    cross_mixed[...] = dot(mixed_low, value_w[...]).astype(BF)
    core_low = dot_tn(mixed_low, grad_first_low[...]).astype(BF)
    if not latent_side:
        core_value[...] = core_low
        return
    write_halves(
        ((cross_active, grad_second_low), (cross_normed, grad_cross_hidden)),
        ((halves[0], place[4]), (halves[1], 1 - place[4])), place[5], X_FIRST, ways // 2, turned,
    )
    write_halves(
        ((cross_mixed, grad_first_low),),
        ((halves[2], place[4]), (halves[3], 1 - place[4])), place[5], Y_FIRST, ways // 2, turned,
    )
    flush(4, 5, 6, 7)
    core_in, residual, gain_row, out_w, normed, queries, item_sums = latent_side
    need(18, 19, 20, 21, 22, 23, 24)
    small_parts(
        place[4], place[5], moves, core_in, residual, grad_first, gain_row, core_low, out_w, normed, queries,
        sums, item_sums, pixel_sums, grad_latents, small_mine, small_other, *small_scratch[8:],
    )


def cross(place, raw_all, gain, shift, asks, owner, residual, core_out, vectors, up, down, lat_rows):
    ways, channels, size = raw_all.shape
    rows, width = residual.shape
    low = jax.ShapeDtypeStruct((rows, width), BF)
    wide = jax.ShapeDtypeStruct((rows, width), F32)
    (
        normal, scores, kept, mixed, top, first_sum, cross_normed, slopes, cross_active, second_sum, second
    ) = streamed(
        "cross",
        cross_body,
        place,
        [asks, gain, shift, raw_all, owner, core_out, residual, vectors, up, down],
        [
            jax.ShapeDtypeStruct((ways, channels, size), BF),
            jax.ShapeDtypeStruct((ways, lat_rows, size), F32),
            jax.ShapeDtypeStruct((rows, size), BF),
            jax.ShapeDtypeStruct((rows, channels), F32),
            jax.ShapeDtypeStruct((lat_rows, 1), F32),
            wide,
            low,
            wide,
            low,
            wide,
            low,
        ],
        [pltpu.VMEM((lat_rows, channels), F32)],
    )
    return mixed, kept, scores, top, normal, first_sum, second_sum, second, cross_normed, cross_active, slopes


def cross_back(
    place, got, upstream, first_sum, slopes, vectors, core_out, up, down,
    raw_all, normal, asks, mixed, kept, scores, top, cross_active, cross_normed, value_w, latent_side, groups,
):
    ways, channels, size = raw_all.shape
    rows, width = upstream.shape
    lat_rows = top.shape[0]
    shape = jax.ShapeDtypeStruct
    low, wide = shape((rows, width), BF), shape((rows, width), F32)
    scratch = [
        pltpu.VMEM((rows, channels), BF),
        pltpu.VMEM((channels, size), F32),
        pltpu.VMEM((lat_rows, channels), F32),
        pltpu.VMEM((width // 2, rows), BF),
    ]
    moves, pixel_sums, sums = shape((rows, channels), BF), shape((2, channels, 1), F32), shape((2, width), F32)
    pix = shape((ways, channels, size), BF)
    if latent_side:
        total = small_lines(channels)
        small = shape((4, ways // 4 * (total // 4), 2 * width // ways), BF)
        outs = [pix, wide, small, small] + [
            shape((groups, width // 2, count * width // groups), BF) for count in (2, 2, 1, 1)
        ]
        inner = [low, low, low, moves, pixel_sums, sums, wide, low, shape((16, width), F32), shape((total, width), BF)]
        scratch += [pltpu.VMEM(value.shape, value.dtype) for value in inner]
    else:
        outs = [low, low, wide, low, sums, moves, pix, pixel_sums, shape((channels, width), BF), low]
    return streamed(
        "cross_back",
        cross_back_body,
        place,
        [
            got, upstream, slopes, down, up, first_sum, vectors, core_out, normal, mixed, kept, asks, scores, top,
            raw_all, value_w, cross_active, cross_normed, *latent_side,
        ],
        outs,
        scratch,
    )


def second_hop_body(place, near, made, extra, need, flush):
    for at, out in enumerate(made):
        need(3 * at, 3 * at + 1, 3 * at + 2)
        value = near[3 * at][...].astype(F32) + near[3 * at + 1][...].astype(F32)
        out[...] = (value + near[3 * at + 2][...].astype(F32)).astype(BF)
        flush(at)


def pieces_body(place, near, made, extra, need, flush):
    sums, every = extra[:3], extra[3]
    chips, unused, block = every.shape
    for at, here in enumerate(sums):
        need(*range(4 * at, 4 * at + 4))
        value = near[4 * at][...].astype(F32)
        for k in range(1, 4):
            value = value + near[4 * at + k][...].astype(F32)
        here[...] = value.astype(BF)
    lines = sums[2].shape[0] // (chips // 2)
    for z in range(chips):
        at = 0
        for here in sums[:2]:
            for k in range(here.shape[1] // block):
                every[z, at : at + block, :] = here[z * block : (z + 1) * block, k * block : (k + 1) * block]
                at += block
        every[z, at:, :] = sums[2][
            z // 2 * lines : (z // 2 + 1) * lines, z % 2 * block : (z % 2 + 1) * block
        ]
    for m, out in enumerate(made):
        out[...] = every[place[0] ^ m]
        flush(m)


def second_hop(flows, first_got):
    ins = []
    for (mine, got, unused), first in zip(flows, first_got):
        ins += [(mine, 3), (got, 3), (first, 1)]
    return streamed(
        "second_hop",
        second_hop_body,
        jnp.zeros((1,), jnp.int32),
        ins,
        [jax.ShapeDtypeStruct(mine.shape[1:], BF) for mine, unused, hop in flows],
        [],
    )


def pieces_of(chip, chips, block, flows, first_got, hops):
    ins = []
    for (mine, got, unused), first, last in zip(flows, first_got, hops):
        ins += [(mine, 2), (got, 2), (first, 0), last]
    shapes = [mine.shape[1:] for mine, unused, hop in flows]
    lines = sum(shape[1] for shape in shapes[:2]) + shapes[2][0] // (chips // 2)
    return streamed(
        "pieces",
        pieces_body,
        chip.astype(jnp.int32).reshape(1),
        ins,
        [jax.ShapeDtypeStruct((lines, block), BF)] * chips,
        [pltpu.VMEM(shape, BF) for shape in shapes] + [pltpu.VMEM((chips, lines, block), BF)],
    )


def finish_body(place, near, made, extra, need, flush):
    parts, key_w = near[:4], near[4]
    net_down, net_up, out_weight, query, key, value, pixel_gain, pixel_shift, *gains = made
    every, small = extra
    block = parts[0].shape[1]
    channels, width = key_w.shape
    quarter = width // 4
    tiles = quarter // block
    size = small.shape[0] // 4
    for m in range(4):
        need(m)
        every[m] = parts[m][...]
    for j in range(4):
        m = place[0] ^ j
        small[j * size : (j + 1) * size, :] = every[m, 3 * quarter // block * block :, :]
        for at, out in enumerate((net_down, net_up, out_weight)):
            for k in range(tiles):
                lines = (at * tiles + k) * block
                out[:, j * quarter + k * block : j * quarter + (k + 1) * block] = every[
                    m, lines : lines + block, :
                ].astype(F32)
    flush(0, 1, 2)
    need(4)
    scale = 1.0 / math.sqrt(width)
    query[...] = dot_tn(small[channels : 2 * channels, :], key_w[...]) * scale
    cin = key.shape[0]
    value[...] = small[:channels, :].astype(F32)[:cin]
    key[...] = small[2 * channels : 3 * channels, :].astype(F32)[:cin] * scale
    vectors = small[3 * channels :, :].astype(F32)
    count = -(-channels // block)
    for at, out in enumerate((pixel_gain, pixel_shift)):
        line = [vectors[2 + at * count + k : 3 + at * count + k, :] for k in range(count)]
        out[...] = jnp.concatenate(line, axis=1)[:, :cin]
    for at, out in enumerate(gains):
        line = at if at < 2 else 2 * count + at
        out[...] = vectors[line : line + 1, :]


def finish(item, parts, key_w, cin):
    lines, block = parts[0].shape
    channels, width = key_w.shape
    shape = jax.ShapeDtypeStruct
    total = small_lines(channels)
    tall, flat = shape((block, width), F32), shape((cin, block), F32)
    return streamed(
        "finish",
        finish_body,
        item.astype(jnp.int32).reshape(1),
        [*parts, key_w],
        [tall, tall, tall, tall, flat, flat] + [shape((1, cin), F32)] * 2 + [shape((1, block), F32)] * 8,
        [pltpu.VMEM((4, lines, block), BF), pltpu.VMEM((total, block), BF)],
    )


def on_device(
    latents,
    pixels,
    lengths,
    out_grad,
    latent_gain,
    latent_shift,
    pixel_gain,
    pixel_shift,
    query_weight,
    key_weight,
    value_weight,
    out_weight,
    cross_gain,
    cross_shift,
    cross_up,
    cross_down,
    self_gain,
    self_shift,
    self_packed,
    self_out,
    final_gain,
    final_shift,
    latent_up,
    latent_down,
):
    items = latents.shape[1]
    lat_rows = latents.shape[2]
    width = latents.shape[3]
    pix_rows = pixels.shape[1]
    cin = pixels.shape[2]
    ways = lax.axis_size("lat")
    groups = lax.axis_size("items")
    sub = ways // items
    rows = items * lat_rows
    piece = lat_rows // sub
    score_scale = 1.0 / math.sqrt(width)
    head_scale = 1.0 / math.sqrt(HEAD)
    lat_index = lax.axis_index("lat")
    core = lat_index % 2

    channels = -(-cin // 16) * 16
    pad = ((0, channels - cin), (0, 0))
    spans = lengths[0]
    starts = jnp.cumsum(spans) - spans
    largest = jnp.argmax(spans).astype(jnp.int32)
    large_start = starts[largest]
    place = jnp.stack(
        [
            large_start,
            large_start + spans[largest],
            largest,
            jnp.asarray(cin, jnp.int32),
            core,
            lax.axis_index("items"),
        ]
    ).astype(jnp.int32)
    edge_places = jnp.arange(pix_rows, dtype=jnp.int32)
    edge_places = jnp.where(edge_places < large_start, edge_places, edge_places + pix_rows * (ways - 1))
    owner = jnp.sum((edge_places[None, :] >= starts[:, None]).astype(jnp.int32), axis=0) - 1
    owner = owner[None, :]

    swap = [(i, i ^ 1) for i in range(ways)]
    same_core = [list(range(0, ways, 2)), list(range(1, ways, 2))]
    block = width // ways

    tie = lax.optimization_barrier

    chips = ways // 2
    chip = lat_index // 2
    item = lax.axis_index("items")

    def swap_items(part, m):
        return lax.ppermute(part, "items", [(i, i ^ m) for i in range(groups)])

    def near_chips(pieces):
        if chips != 4:
            whole = jnp.stack([pieces(j) for j in range(chips)])
            moved = lax.all_to_all(
                whole, "lat", split_axis=0, concat_axis=0, tiled=True, axis_index_groups=same_core
            )
            return [moved[j] for j in range(chips)]
        return [pieces(chip)] + [
            lax.ppermute(
                pieces(chip ^ m), "lat", [(i, ((i // 2) ^ m) * 2 + i % 2) for i in range(ways)]
            )
            for m in range(1, chips)
        ]

    def total(parts):
        value = parts[0].astype(F32)
        for part in parts[1:]:
            value = value + part.astype(F32)
        return value

    def add(left, right):
        return (left.astype(F32) + right.astype(F32)).astype(BF)

    def over_chips_whole(here):
        parts = lax.all_to_all(
            here, "lat", split_axis=0, concat_axis=0, tiled=True, axis_index_groups=same_core
        )
        return jnp.sum(parts.astype(F32), axis=0).astype(BF)

    def gather_items(part):
        return jnp.stack([part] + [swap_items(part, m) for m in range(1, groups)])

    def by_item(parts):
        return [lax.dynamic_index_in_dim(parts, item ^ j, 0, keepdims=False) for j in range(groups)]

    def weight_of(parts):
        return jnp.concatenate(by_item(parts), axis=1).astype(F32)

    pixels_low = jnp.pad(pixels[0].T, pad)
    raw_all = lax.all_gather(pixels_low, "lat", axis=0, tiled=False)
    gain_column = jnp.pad(pixel_gain[:, None], pad)
    shift_column = jnp.pad(pixel_shift[:, None], pad)
    key_pad = jnp.pad(key_weight, pad)
    value_pad = jnp.pad(value_weight, pad)

    to_pixels = (dot_nt(query_weight, key_pad) * score_scale).astype(BF)
    from_pixels = dot(value_pad, out_weight).astype(BF)

    residual = latents.reshape(rows, width)
    upstream = out_grad.reshape(rows, width)
    normed = layer_norm(residual, latent_gain, latent_shift).astype(BF)
    asks = dot(normed, to_pixels).astype(BF)
    latent_queries = dot(normed, query_weight).astype(BF)

    def reshare(values):
        moved = lax.all_to_all(
            values.reshape(ways, piece, width), "lat", split_axis=0, concat_axis=0, tiled=True
        )
        return moved.reshape(rows, width)

    (
        raw_all, value_pad, upstream_low, asks, latent_queries, from_pixels, to_pixels, gain_column, shift_column, place, owner
    ) = tie(
        (
            raw_all, value_pad, upstream.astype(BF), asks, latent_queries, from_pixels, to_pixels, gain_column, shift_column,
            place, owner,
        )
    )
    grad_low = reshare(upstream_low)
    cross_vectors = jnp.stack([cross_gain, cross_shift])
    (
        mixed, kept, scores, top, normal, first_sum, second_sum, second, cross_normed, cross_active, slopes
    ) = cross(
        place, raw_all, gain_column, shift_column, asks, owner, residual, from_pixels, cross_vectors,
        cross_up, cross_down, lat_rows,
    )
    second, grad_low = tie((second, grad_low))
    second = reshare(second)
    item_place = jnp.stack([core, item]).astype(jnp.int32)
    item_vectors = jnp.stack([self_gain, self_shift, final_gain, final_shift])
    if sub == 1:
        (
            result_add, second_add, self_normed, grad_packed, self_mixed, grad_third_low,
            final_normed, final_active, grad_final_hidden, item_sums, final_other, packed_other,
        ) = item_block(item_place, groups, second, grad_low, item_vectors, self_packed, self_out, latent_up, latent_down)
    else:
        whole_rows = rows * sub
        same_item = [[i * sub + s for s in range(sub)] for i in range(items)]
        second_wide = second.astype(F32)
        self_normed = layer_norm(second_wide, self_gain, self_shift).astype(BF)
        packed = dot(self_normed, self_packed).astype(BF)
        pairs = lax.all_gather(
            packed[:, width:], "lat", axis=0, tiled=True, axis_index_groups=same_item
        )
        self_mixed, self_low = attend(packed, pairs, rows, whole_rows)
        self_add = dot(self_mixed, self_out)
        third = second_wide + self_add
        final_normed = layer_norm(third, final_gain, final_shift).astype(BF)
        final_hidden = dot(final_normed, latent_up)
        final_active = jax.nn.gelu(final_hidden).astype(BF)
        result_add = (self_add + dot(final_active, latent_down)).astype(BF)
        grad_final_hidden = gelu_back(final_hidden, dot_nt(grad_low, latent_down)).astype(BF)
        back_third, grad_final_gain, grad_final_shift = norm_back(
            third, final_gain, dot_nt(grad_final_hidden, latent_up)
        )
        grad_third_low = (grad_low.astype(F32) + back_third).astype(BF)
        grad_mixed = dot_nt(grad_third_low, self_out).astype(BF)
        grad_queries, grad_pairs = attend_back(grad_mixed, self_low, packed, pairs, rows, whole_rows)
        grad_pairs = lax.psum_scatter(
            grad_pairs, "lat", scatter_dimension=0, tiled=True, axis_index_groups=same_item
        )
        grad_packed = jnp.concatenate([grad_queries, grad_pairs], axis=1)
        back_second, grad_self_gain, grad_self_shift = norm_back(
            second_wide, self_gain, dot_nt(grad_packed, self_packed)
        )
        second_add = (back_third + back_second).astype(BF)
        item_sums = jnp.stack([grad_self_gain, grad_self_shift, grad_final_gain, grad_final_shift])
    second_got = reshare(second_add)
    item_pairs = (
        (final_active, grad_low),
        (final_normed, grad_final_hidden),
        (self_mixed, grad_third_low),
        (self_normed, grad_packed),
    )
    final_pairs, packed_pairs = item_pairs[:3], item_pairs[3:]
    if sub > 1:
        final_other = half_plain(final_pairs, 1 - core, item, X_FIRST, ways).astype(BF)
        packed_other = half_plain(packed_pairs, 1 - core, item, Y_FIRST, ways).astype(BF)
    final_got = lax.ppermute(final_other, "lat", swap)
    packed_got = lax.ppermute(packed_other, "lat", swap)
    final_parts = half_grads(final_pairs, core, item, X_FIRST, ways, final_got)
    packed_parts = list(half_grads(packed_pairs, core, item, Y_FIRST, ways, packed_got, True))
    final_got, packed_got = [None, swap_items(final_parts[1], 1)], [None, swap_items(packed_parts[1], 2)]
    second_got, result_add, final_got[1], packed_got[1] = tie(
        (second_got, result_add, final_got[1], packed_got[1])
    )
    final_got[0], packed_got[0] = swap_items(final_parts[0], 1), swap_items(packed_parts[0], 2)
    packed_low = swap_items(packed_parts.pop(2), 2)
    final_kept, packed_kept = final_parts[2:], packed_parts[2:]
    result_got = reshare(result_add)

    back_args = (
        place, second_got, upstream, first_sum, slopes, cross_vectors, from_pixels, cross_up, cross_down,
        raw_all, normal, asks, mixed, kept, scores, top, cross_active, cross_normed, value_pad,
    )
    if block % 128 == 0:
        latent_side = (
            to_pixels, residual, latent_gain[None], out_weight, normed, latent_queries, item_sums
        )
        (
            parts_pix, grad_latents, small_mine, small_other, net_mine, net_other, out_mine, out_other
        ) = cross_back(*back_args, latent_side, groups)
    else:
        (
            grad_second_low, grad_cross_hidden, grad_first, grad_first_low, cross_sums, moves, parts_pix, pixel_sums,
            core_value, cross_mixed,
        ) = cross_back(*back_args, (), groups)
        cross_pairs = ((cross_active, grad_second_low), (cross_normed, grad_cross_hidden))
        net_mine, net_other, out_mine, out_other = [
            half_plain(pairs, half, item, order, ways).astype(BF)
            for pairs, order in ((cross_pairs, X_FIRST), (((cross_mixed, grad_first_low),), Y_FIRST))
            for half in (core, 1 - core)
        ]
        grad_latents, small_mine, small_other = last_block(
            core, item, ways, moves, to_pixels, residual, grad_first, latent_gain[None], core_value, out_weight,
            normed, latent_queries, jnp.concatenate([cross_sums, item_sums, jnp.zeros((2, width), F32)]), pixel_sums,
        )
    (
        parts_pix, grad_latents, small_mine, small_other, net_mine, net_other, out_mine, out_other,
        final_got[0], packed_got[0], packed_low, result_got,
    ) = tie(
        (
            parts_pix, grad_latents, small_mine, small_other, net_mine, net_other, out_mine, out_other,
            final_got[0], packed_got[0], packed_low, result_got,
        )
    )
    grad_pn = lax.psum_scatter(parts_pix, "lat", scatter_dimension=0, tiled=False)
    packed_got[1] = jnp.concatenate([packed_got[1], packed_low])
    net_got = lax.ppermute(net_other, "lat", swap)
    out_got = lax.ppermute(out_other, "lat", swap)
    final_two, packed_two = add(final_kept[1], final_got[1]), add(packed_kept[1], packed_got[1])
    final_two, packed_two = swap_items(final_two, 2), swap_items(packed_two, 1)
    small_got = lax.ppermute(small_other, "lat", swap)
    net_first, out_first = add(net_mine[:2], net_got[:2]), add(out_mine[:2], out_got[:2])
    small_first = add(small_mine[:2], small_got[:2])
    final_two, packed_two, net_first, out_first, small_first = tie(
        (final_two, packed_two, net_first, out_first, small_first)
    )
    first_got = [swap_items(net_first, 1), swap_items(out_first, 2), swap_items(small_first, 2)]
    item_here = jnp.concatenate(
        [
            total([final_kept[0], final_got[0], final_two]).astype(BF),
            total([packed_kept[0], packed_got[0], packed_two]).astype(BF),
        ],
        axis=1,
    )
    first_got = tie(tuple(first_got))
    item_part = over_chips_whole(item_here.reshape(chips, block, -1))
    flows = ((net_mine, net_got, 2), (out_mine, out_got, 1), (small_mine, small_got, 1))
    fast = block % 128 == 0 and chips == 4
    if fast:
        hops = second_hop(flows, first_got)
    else:
        hops = [
            total([mine[3], got[3], first[1]]).astype(BF)
            for (mine, got, hop), first in zip(flows, first_got)
        ]
    hops = [swap_items(part, hop) for part, (mine, got, hop) in zip(hops, flows)]
    if fast:
        pieces = pieces_of(chip, chips, block, flows, first_got, hops)
        item_part, grad_pn, *pieces = tie((item_part, grad_pn, *pieces))
        rest = [pieces[0]] + [
            lax.ppermute(
                pieces[m], "lat", [(i, ((i // 2) ^ m) * 2 + i % 2) for i in range(ways)]
            )
            for m in range(1, chips)
        ]
    else:
        item_part, grad_pn, *hops = tie((item_part, grad_pn, *hops))
        net_here, out_here, small_here = [
            total([mine[2], got[2], first[0], last]).astype(BF)
            for (mine, got, hop), first, last in zip(flows, first_got, hops)
        ]
        lines = small_here.shape[0] // (chips // 2)
        pieces = jnp.stack(
            [
                jnp.concatenate(
                    [
                        whole[z * block : (z + 1) * block, k * block : (k + 1) * block]
                        for whole in (net_here, out_here)
                        for k in range(whole.shape[1] // block)
                    ]
                    + [small_here[z // 2 * lines : (z // 2 + 1) * lines, z % 2 * block : (z % 2 + 1) * block]]
                )
                for z in range(chips)
            ]
        )
        rest = near_chips(lambda z: lax.dynamic_index_in_dim(pieces, z, 0, keepdims=False))
    item_parts = [item_part] + [swap_items(item_part, m) for m in range(1, groups)]
    tied = tie((*rest, *item_parts))
    rest, item_parts = total(tied[: len(rest)]).astype(BF), jnp.stack(tied[len(rest) :])
    quarter = width // groups
    grad_latent_down, grad_latent_up, grad_self_out = [
        weight_of(item_parts[:, :, at * quarter : (at + 1) * quarter]) for at in range(3)
    ]
    grad_self_packed = weight_of(item_parts[:, :, 3 * quarter :])
    result = second_sum + result_got.astype(F32)
    grad_pn = grad_pn.astype(F32)[:cin]
    pix_hat, pix_inv = norm_parts(pixels[0].T.astype(F32), 0)
    scaled = grad_pn * pixel_gain[:, None]
    grad_pixels = pix_inv * (
        scaled
        - jnp.mean(scaled, axis=0, keepdims=True)
        - pix_hat * jnp.mean(scaled * pix_hat, axis=0, keepdims=True)
    )
    rest_parts = [rest] + [swap_items(rest, m) for m in range(1, groups)]
    if block % 128 == 0:
        (
            grad_cross_down, grad_cross_up, grad_out_weight, grad_query_weight, grad_key_weight, grad_value_weight,
            *vectors,
        ) = finish(item, rest_parts, key_pad, cin)
        grad_pixel_gain, grad_pixel_shift, *gains = [value.reshape(-1) for value in vectors]
    else:
        rest_parts = jnp.stack(rest_parts)
        tall = quarter // block * block
        grad_cross_down, grad_cross_up, grad_out_weight = [
            weight_of(
                rest_parts[:, at * tall : (at + 1) * tall]
                .reshape(groups, quarter // block, block, block)
                .transpose(0, 2, 1, 3)
                .reshape(groups, block, quarter)
            )
            for at in range(3)
        ]
        small = jnp.concatenate(by_item(rest_parts[:, 3 * tall :]), axis=0).astype(F32)
        grad_query_weight = dot_tn(small[channels : 2 * channels].astype(BF), key_pad) * score_scale
        grad_key_weight = small[2 * channels : 2 * channels + cin] * score_scale
        grad_value_weight = small[:cin]
        head = small[3 * channels : 3 * channels + 2]
        sums = small[3 * channels + 2 :]
        count = -(-channels // block)
        grad_pixel_gain = sums[:count].reshape(-1)[:cin]
        grad_pixel_shift = sums[count : 2 * count].reshape(-1)[:cin]
        gains = [head[0], head[1]] + [sums[2 * count + at] for at in range(6)]
    shape = (1, items, lat_rows, width)
    return (
        result.reshape(shape),
        grad_latents.reshape(shape),
        grad_pixels.T[None],
        gains[0],
        gains[1],
        grad_pixel_gain,
        grad_pixel_shift,
        grad_query_weight,
        grad_key_weight,
        grad_value_weight,
        grad_out_weight,
        gains[2],
        gains[3],
        grad_cross_up,
        grad_cross_down,
        gains[4],
        gains[5],
        grad_self_packed,
        grad_self_out,
        gains[6],
        gains[7],
        grad_latent_up,
        grad_latent_down,
    )


def solution(mesh):
    rows = P("items", None, "lat", None)
    in_specs = (rows, P("items", "lat", None), P("items", None), rows) + (P(),) * 20
    lane = P("lat")
    tall = P("lat", None)
    wide = P(None, "lat")
    out_specs = (
        rows,
        rows,
        P("items", "lat", None),
        lane,
        lane,
        P(),
        P(),
        tall,
        wide,
        wide,
        tall,
        lane,
        lane,
        tall,
        tall,
        lane,
        lane,
        tall,
        tall,
        lane,
        lane,
        tall,
        tall,
    )
    return jax.shard_map(
        on_device, mesh=mesh, in_specs=in_specs, out_specs=out_specs, check_vma=False
    )
```

```python
import math

import jax
import jax.numpy as jnp
from jax import lax
from jax.experimental import pallas as pl
from jax.experimental.pallas import tpu as pltpu
from jax.sharding import PartitionSpec as P

HEADS = 8
HEAD = 128
X_FIRST = (1, 3, 0, 2)
Y_FIRST = (2, 3, 0, 1)
BF = jnp.bfloat16
F32 = jnp.float32


def norm_parts(values, axis=-1):
    centre = values - jnp.mean(values, axis=axis, keepdims=True)
    spread = jnp.mean(centre * centre, axis=axis, keepdims=True)
    inv = lax.rsqrt(spread + 1e-05)
    return centre * inv, inv


def layer_norm(values, gain, shift):
    hat, unused = norm_parts(values)
    return hat * gain + shift


def norm_back(values, gain, upstream):
    hat, inv = norm_parts(values)
    scaled = upstream * gain
    back = inv * (
        scaled
        - jnp.mean(scaled, axis=-1, keepdims=True)
        - hat * jnp.mean(scaled * hat, axis=-1, keepdims=True)
    )
    return back, jnp.sum(upstream * hat, axis=0), jnp.sum(upstream, axis=0)


def gelu_back(hidden, upstream):
    unused, pullback = jax.vjp(jax.nn.gelu, hidden)
    return pullback(upstream)[0]


def dot(left, right):
    return jnp.dot(left, right, preferred_element_type=F32)


def dot_tn(left, right):
    return lax.dot_general(left, right, (((0,), (0,)), ((), ())), preferred_element_type=F32)


def dot_nt(left, right):
    return lax.dot_general(left, right, (((1,), (1,)), ((), ())), preferred_element_type=F32)


def softmax(scores):
    raised = jnp.exp(scores - jnp.max(scores, axis=-1, keepdims=True))
    return raised / jnp.sum(raised, axis=-1, keepdims=True)


def attend_kernel(query, key, value, out, kept):
    scores = dot_nt(query[...], key[...]) * (1.0 / math.sqrt(HEAD))
    raised = jnp.exp(scores - jnp.max(scores, axis=-1, keepdims=True))
    weights = (raised * (1.0 / jnp.sum(raised, axis=-1, keepdims=True))).astype(BF)
    kept[0] = weights
    out[...] = dot(weights, value[...]).astype(BF)


def attend(queries, pairs, rows, whole_rows):
    column = lambda at: pl.BlockSpec((whole_rows, HEAD), lambda h: (0, h + at))
    own = pl.BlockSpec((rows, HEAD), lambda h: (0, h))
    return pl.pallas_call(
        attend_kernel,
        grid=(HEADS,),
        in_specs=[own, column(0), column(HEADS)],
        out_specs=[own, pl.BlockSpec((1, rows, whole_rows), lambda h: (h, 0, 0))],
        out_shape=[
            jax.ShapeDtypeStruct((rows, HEADS * HEAD), BF),
            jax.ShapeDtypeStruct((HEADS, rows, whole_rows), BF),
        ],
        compiler_params=pltpu.CompilerParams(vmem_limit_bytes=40 << 20),
        name="attend",
    )(queries, pairs, pairs)


def attend_back_kernel(grad, weights_ref, query, key, value, grad_query, grad_pair):
    at = pl.multiple_of(pl.program_id(0) * HEAD, HEAD)
    also = pl.multiple_of(pl.program_id(0) * HEAD + HEADS * HEAD, HEAD)
    weights_low = weights_ref[0]
    weights = weights_low.astype(F32)
    upstream = grad[...]
    grad_weights = dot_nt(upstream, value[...])
    grad_pair[:, pl.ds(also, HEAD)] = dot_tn(weights_low, upstream).astype(BF)
    inner = jnp.sum(weights * grad_weights, axis=-1, keepdims=True)
    spread = (weights * (grad_weights - inner)).astype(BF)
    scale = 1.0 / math.sqrt(HEAD)
    grad_query[...] = (dot(spread, key[...]) * scale).astype(BF)
    grad_pair[:, pl.ds(at, HEAD)] = (dot_tn(spread, query[...]) * scale).astype(BF)


def attend_back(grad, weights, queries, pairs, rows, whole_rows):
    column = lambda at: pl.BlockSpec((whole_rows, HEAD), lambda h: (0, h + at))
    own = pl.BlockSpec((rows, HEAD), lambda h: (0, h))
    return pl.pallas_call(
        attend_back_kernel,
        grid=(HEADS,),
        in_specs=[
            own,
            pl.BlockSpec((1, rows, whole_rows), lambda h: (h, 0, 0)),
            own,
            column(0),
            column(HEADS),
        ],
        out_specs=[own, pl.BlockSpec((whole_rows, 2 * HEADS * HEAD), lambda h: (0, 0))],
        out_shape=[
            jax.ShapeDtypeStruct((rows, HEADS * HEAD), BF),
            jax.ShapeDtypeStruct((whole_rows, 2 * HEADS * HEAD), BF),
        ],
        compiler_params=pltpu.CompilerParams(vmem_limit_bytes=40 << 20),
        name="attend_back",
    )(grad, weights, queries, pairs, pairs)


def half_columns(left, half, blocks):
    step = left.shape[1] // (2 * blocks)
    return jnp.concatenate(
        [left[:, pl.ds(pl.multiple_of((2 * z + half) * step, step), step)] for z in range(blocks)], axis=1
    ).T


def half_body(order, blocks, place, near, made, extra, need, flush):
    (turned,) = extra
    groups = len(order)
    count = (len(near) - groups) // 2
    added = near[2 * count :]
    for index in range(count):
        need(index)
        turned[index] = half_columns(near[index], place[0], blocks)
    need(*range(count, 2 * count))
    cut = len(made) > groups
    for place_in, p in enumerate((1, 0, 2, 3)):
        need(2 * count + place_in)
        at = 0
        outs = [p + (cut and p > 1)] if p != 1 or not cut else [1, 2]
        for index, right in enumerate(near[count : 2 * count]):
            size = right.shape[1] // groups
            lanes = pl.ds(pl.multiple_of((place[1] ^ order[p]) * size, HEAD), size)
            value = dot(turned[index], right[:, lanes]) + added[place_in][:, at : at + size].astype(F32)
            value = value.astype(BF)
            lines = 0
            for out in outs:
                count_of = made[out].shape[0]
                made[out][:, at : at + size] = value[lines : lines + count_of]
                lines += count_of
            at += size
        flush(*outs)


def half_plain(pairs, half, item, order, ways):
    blocks = ways // 2
    rows, width = pairs[0][0].shape
    groups = len(order)
    outs = []
    for left, right in pairs:
        columns = lax.dynamic_index_in_dim(
            left.reshape(rows, blocks, 2, width // ways), half, 2, keepdims=False
        ).reshape(rows, width // 2)
        value = dot_tn(columns, right).reshape(width // 2, groups, -1).transpose(1, 0, 2)
        outs.append(value)
    value = jnp.concatenate(outs, axis=2)
    return jnp.stack([lax.dynamic_index_in_dim(value, item ^ m, 0, keepdims=False) for m in order])


def half_grads(pairs, half, item, order, ways, added, cut=False):
    rows, width = pairs[0][0].shape
    blocks, groups = ways // 2, len(order)
    total = sum(right.shape[1] for unused, right in pairs) // groups
    if (width // ways) % 128:
        value = (half_plain(pairs, half, item, order, ways) + added.astype(F32)).astype(BF)
        parts = [value[p] for p in range(groups)]
        if cut:
            parts[1:2] = [parts[1][: width // 4], parts[1][width // 4 :]]
        return parts
    shapes = [jax.ShapeDtypeStruct((width // 2, total), BF)] * groups
    if cut:
        shapes[1:2] = [jax.ShapeDtypeStruct((width // 4, total), BF)] * 2
    return streamed(
        "half_grads",
        lambda *refs: half_body(order, blocks, *refs),
        jnp.stack([half, item]).astype(jnp.int32),
        [left for left, unused in pairs]
        + [right for unused, right in pairs]
        + [(added, p) for p in (1, 0, 2, 3)],
        shapes,
        [pltpu.VMEM((len(pairs), width // 2, rows), BF)],
    )


def small_parts(
    core, item, moves, core_in, residual, grad_first, gain, core_value, out_w, normed, queries,
    sums, item_sums, pixel_sums, grad_latents, mine, other, stacked, rest,
):
    rows, width = residual.shape
    block = mine.shape[2] // 2
    chips = width // block // 2
    channels = moves.shape[1]
    stacked[...] = jnp.zeros(stacked.shape, F32)

    def back(part):
        grad_normed = dot_nt(moves[part, :], core_in[...])
        hat, inv = norm_parts(residual[part, :])
        stacked[0:1, :] += jnp.sum(grad_normed * hat, axis=0, keepdims=True)
        stacked[1:2, :] += jnp.sum(grad_normed, axis=0, keepdims=True)
        grad_latents[part, :] = grad_first[part, :] + norm_slope(hat, inv, gain[...], grad_normed)

    each_part(rows, back)
    stacked[8:10, :] = sums[...]
    stacked[10:14, :] = item_sums[...]
    for at in range(2):
        line = jnp.broadcast_to(pixel_sums[at], (channels, 128)).T[0:1, :]
        line = jnp.concatenate([line, jnp.zeros((1, -channels % 128), F32)], axis=1)
        for k in range(line.shape[1] // 128):
            for j in range(width // block):
                stacked[2 + 3 * at + k : 3 + 3 * at + k, j * block : j * block + 128] = line[
                    :, k * 128 : (k + 1) * 128
                ]
    rest[0:channels, :] = dot_nt(core_value, out_w[...]).astype(BF)
    rest[channels : 2 * channels, :] = dot_tn(moves[...], normed[...]).astype(BF)
    rest[2 * channels : 3 * channels, :] = dot_tn(moves[...], queries[...]).astype(BF)
    rest[3 * channels :, :] = stacked[...].astype(BF)
    size = rest.shape[0] // 4
    for p, m in enumerate(Y_FIRST):
        lines = pl.ds(pl.multiple_of((item ^ m) * size, 16), size)
        for out, half in ((mine, core), (other, 1 - core)):
            for z in range(chips):
                lanes = pl.ds(pl.multiple_of((2 * z + half) * block, block), block)
                out[p, z // 2 * size : (z // 2 + 1) * size, z % 2 * block : (z % 2 + 1) * block] = rest[
                    lines, lanes
                ]


def small_lines(channels):
    return 3 * channels + 16


def last_block(
    core, item, ways, moves, core_in, residual, grad_first, gain, core_value, out_w, normed, queries,
    vectors, pixel_sums,
):
    rows, width = residual.shape
    channels = moves.shape[1]
    block, chips = width // ways, ways // 2
    grad_normed = dot_nt(moves, core_in)
    back, grad_gain, grad_shift = norm_back(residual, gain[0], grad_normed)
    sums = jnp.pad(pixel_sums.reshape(2, channels), ((0, 0), (0, -channels % block)))
    lines = sums.reshape(-1, 1, block)
    lines = jnp.broadcast_to(lines, (lines.shape[0], ways, block)).reshape(-1, width)
    stack = [
        dot_nt(core_value, out_w),
        dot_tn(moves, normed),
        dot_tn(moves, queries),
        grad_gain[None],
        grad_shift[None],
        lines,
        vectors,
    ]
    count = sum(value.shape[0] for value in stack)
    stack = jnp.concatenate(stack + [jnp.zeros((-count % 64, width), F32)]).astype(BF)
    size = stack.shape[0] // 4
    stack = stack.reshape(4, size, chips // 2, 2, 2, block)
    halves = []
    for half in (core, 1 - core):
        value = lax.dynamic_index_in_dim(stack, half, 4, keepdims=False)
        value = value.transpose(0, 2, 1, 3, 4).reshape(4, chips // 2 * size, 2 * block)
        halves.append(
            jnp.stack([lax.dynamic_index_in_dim(value, item ^ m, 0, keepdims=False) for m in Y_FIRST])
        )
    return grad_first + back, halves[0], halves[1]


GELU_A = 0.044715
GELU_C = math.sqrt(2.0 / math.pi)
PART = 256


def gelu_both(hidden):
    square = hidden * hidden
    bent = jnp.tanh(hidden * (GELU_C + (GELU_C * GELU_A) * square))
    half = 0.5 + 0.5 * bent
    slope = half + (0.5 * hidden) * (1.0 - bent * bent) * (GELU_C + (3.0 * GELU_C * GELU_A) * square)
    return hidden * half, slope


def norm_slope(hat, inv, gain, upstream):
    scaled = upstream * gain
    centre = jnp.mean(scaled, axis=-1, keepdims=True)
    along = jnp.mean(scaled * hat, axis=-1, keepdims=True)
    return inv * (scaled - centre - hat * along)


def each_part(rows, body):
    size = min(PART, rows)

    def step(r, carry):
        body(pl.ds(pl.multiple_of(r * size, size), size))
        return carry

    lax.fori_loop(0, rows // size, step, 0, unroll=True)


def each_head(body):
    def step(h, carry):
        body(h)
        return carry

    lax.fori_loop(0, HEADS, step, 0, unroll=4)


def write_halves(pairs, outs, item, order, blocks, turned):
    at = 0
    for left, right in pairs:
        size = right.shape[1] // len(order)
        for out, half in outs:
            turned[...] = half_columns(left, half, blocks)
            for p, m in enumerate(order):
                lanes = pl.ds(pl.multiple_of((item ^ m) * size, HEAD), size)
                out[p, :, at : at + size] = dot(turned[...], right[:, lanes]).astype(BF)
        at += size


def item_body(place, near, made, extra, need, flush):
    second, vectors, packed_w0, packed_w1, packed_w2, out_w, up_w, down_w, grad_low = near
    (
        self_normed, self_mixed, final_normed, final_active, result_add, grad_final_hidden, grad_third_low,
        second_add, grad_packed, sums, other_first, other_packed,
    ) = made
    packed, raised_low, inverse, mixed, back_third, grad_mixed, turned = extra
    packed_w = (packed_w0, packed_w1, packed_w2)
    rows, width = second.shape
    need(0, 1)
    sums[...] = jnp.zeros(sums.shape, F32)

    def normalize(part):
        hat, unused = norm_parts(second[part, :].astype(F32))
        self_normed[part, :] = (hat * vectors[0:1, :] + vectors[1:2, :]).astype(BF)

    each_part(rows, normalize)
    flush(0)
    for c in range(3):
        need(2 + c)

        def project(part):
            packed[part, c * width : (c + 1) * width] = dot(
                self_normed[part, :], packed_w[c][...]
            ).astype(BF)

        each_part(rows, project)

    def lanes(h, group):
        return pl.ds(pl.multiple_of(h * HEAD + group * width, HEAD), HEAD)

    scale = 1.0 / math.sqrt(HEAD)

    def attend_head(h):
        scores = dot_nt(packed[:, lanes(h, 0)], packed[:, lanes(h, 1)])
        peak = jnp.max(scores, axis=-1, keepdims=True)
        raised = jnp.exp2((scores - peak) * (scale * math.log2(math.e)))
        inv = 1.0 / jnp.sum(raised, axis=-1, keepdims=True)
        low = raised.astype(BF)
        raised_low[h] = low
        inverse[h] = inv
        mixed[:, lanes(h, 0)] = dot(low, packed[:, lanes(h, 2)]) * inv

    each_head(attend_head)
    need(5, 6, 7, 8)

    def middle(part):
        low = mixed[part, :].astype(BF)
        self_mixed[part, :] = low
        added = dot(low, out_w[...])
        hat, inv = norm_parts(second[part, :].astype(F32) + added)
        normed = (hat * vectors[2:3, :] + vectors[3:4, :]).astype(BF)
        final_normed[part, :] = normed
        active, slope = gelu_both(dot(normed, up_w[...]))
        active = active.astype(BF)
        final_active[part, :] = active
        result_add[part, :] = (added + dot(active, down_w[...])).astype(BF)
        upstream = grad_low[part, :]
        grad_hidden = (dot_nt(upstream, down_w[...]) * slope).astype(BF)
        grad_final_hidden[part, :] = grad_hidden
        grad_normed = dot_nt(grad_hidden, up_w[...])
        sums[2:3, :] += jnp.sum(grad_normed * hat, axis=0, keepdims=True)
        sums[3:4, :] += jnp.sum(grad_normed, axis=0, keepdims=True)
        back = norm_slope(hat, inv, vectors[2:3, :], grad_normed)
        back_third[part, :] = back
        third_low = (upstream.astype(F32) + back).astype(BF)
        grad_third_low[part, :] = third_low
        grad_mixed[part, :] = dot_nt(third_low, out_w[...]).astype(BF)

    each_part(rows, middle)
    flush(1, 2, 3, 4, 5, 6)

    def attend_back_head(h):
        upstream = grad_mixed[:, lanes(h, 0)]
        low = raised_low[h]
        inv = inverse[h]
        up32 = upstream.astype(F32)
        inner = jnp.sum(up32 * mixed[:, lanes(h, 0)], axis=-1, keepdims=True)
        grad_packed[:, lanes(h, 2)] = dot_tn(low, (up32 * inv).astype(BF)).astype(BF)
        grad_weights = dot_nt(upstream, packed[:, lanes(h, 2)])
        spread = (low.astype(F32) * ((grad_weights - inner) * (inv * scale))).astype(BF)
        grad_packed[:, lanes(h, 0)] = dot(spread, packed[:, lanes(h, 1)]).astype(BF)
        grad_packed[:, lanes(h, 1)] = dot_tn(spread, packed[:, lanes(h, 0)]).astype(BF)

    each_head(attend_back_head)
    flush(8)

    def last(part):
        hat, inv = norm_parts(second[part, :].astype(F32))
        grad_normed = dot_nt(grad_packed[part, :width], packed_w[0][...])
        for c in range(1, 3):
            grad_normed += dot_nt(grad_packed[part, c * width : (c + 1) * width], packed_w[c][...])
        sums[0:1, :] += jnp.sum(grad_normed * hat, axis=0, keepdims=True)
        sums[1:2, :] += jnp.sum(grad_normed, axis=0, keepdims=True)
        back = norm_slope(hat, inv, vectors[0:1, :], grad_normed)
        second_add[part, :] = (back_third[part, :] + back).astype(BF)

    each_part(rows, last)
    flush(7, 9)
    blocks = width // 2 // HEAD
    write_halves(
        ((final_active, grad_low), (final_normed, grad_final_hidden), (self_mixed, grad_third_low)),
        ((other_first, 1 - place[0]),), place[1], X_FIRST, blocks, turned,
    )
    flush(10)
    write_halves(
        ((self_normed, grad_packed),), ((other_packed, 1 - place[0]),), place[1], Y_FIRST, blocks, turned
    )


def item_block(place, groups, second, grad_low, vectors, self_packed, self_out, latent_up, latent_down):
    rows, width = second.shape
    low = jax.ShapeDtypeStruct((rows, width), BF)
    half = jax.ShapeDtypeStruct((groups, width // 2, 3 * width // groups), BF)
    packed_parts = [(self_packed, c * width, width) for c in range(3)]
    (
        self_normed, self_mixed, final_normed, final_active, result_add, grad_final_hidden, grad_third_low,
        second_add, grad_packed, sums, other_first, other_packed,
    ) = streamed(
        "item_block",
        item_body,
        place,
        [second, vectors, *packed_parts, self_out, latent_up, latent_down, grad_low],
        [low] * 8
        + [
            jax.ShapeDtypeStruct((rows, 3 * width), BF),
            jax.ShapeDtypeStruct((4, width), F32),
            half,
            half,
        ],
        [
            pltpu.VMEM((rows, 3 * width), BF),
            pltpu.VMEM((HEADS, rows, rows), BF),
            pltpu.VMEM((HEADS, rows, 1), F32),
            pltpu.VMEM((rows, width), F32),
            pltpu.VMEM((rows, width), F32),
            pltpu.VMEM((rows, width), BF),
            pltpu.VMEM((width // 2, rows), BF),
        ],
    )
    return (
        result_add, second_add, self_normed, grad_packed, self_mixed, grad_third_low,
        final_normed, final_active, grad_final_hidden, sums, other_first, other_packed,
    )


def streamed(name, body, place, ins, outs, scratch):
    cuts = [value[1:] if isinstance(value, tuple) else None for value in ins]
    ins = [value[0] if isinstance(value, tuple) else value for value in ins]
    shapes = [
        value.shape if cut is None else value.shape[1:] if len(cut) == 1 else (value.shape[0], cut[1])
        for value, cut in zip(ins, cuts)
    ]
    anywhere = pl.BlockSpec(memory_space=pl.ANY)

    def kernel(place_ref, *refs):
        sources, refs = refs[: len(ins)], refs[len(ins) :]
        targets, refs = refs[: len(outs)], refs[len(outs) :]
        near, refs = refs[: len(ins)], refs[len(ins) :]
        made, refs = refs[: len(outs)], refs[len(outs) :]
        extra, (in_sems, out_sems) = refs[:-2], refs[-2:]
        sources = [
            ref if cut is None else ref.at[cut[0]] if len(cut) == 1 else ref.at[:, pl.ds(*cut)]
            for ref, cut in zip(sources, cuts)
        ]
        loads = [pltpu.make_async_copy(a, b, in_sems.at[i]) for i, (a, b) in enumerate(zip(sources, near))]
        stores = [pltpu.make_async_copy(a, b, out_sems.at[i]) for i, (a, b) in enumerate(zip(made, targets))]
        left_in, left_out = list(range(len(ins))), list(range(len(outs)))
        for load in loads:
            load.start()

        def need(*which):
            for i in which:
                left_in.remove(i)
                loads[i].wait()

        def flush(*which):
            for i in which:
                left_out.remove(i)
                stores[i].start()

        body(place_ref, near, made, extra, need, flush)
        need(*list(left_in))
        flush(*list(left_out))
        for store in stores:
            store.wait()

    return pl.pallas_call(
        kernel,
        in_specs=[pl.BlockSpec(memory_space=pltpu.SMEM)] + [anywhere] * len(ins),
        out_specs=[anywhere] * len(outs),
        out_shape=list(outs),
        scratch_shapes=[pltpu.VMEM(shape, value.dtype) for shape, value in zip(shapes, ins)]
        + [pltpu.VMEM(value.shape, value.dtype) for value in outs]
        + list(scratch)
        + [pltpu.SemaphoreType.DMA((len(ins),)), pltpu.SemaphoreType.DMA((len(outs),))],
        compiler_params=pltpu.CompilerParams(vmem_limit_bytes=60 << 20),
        name=name,
    )(place, *ins)


def pixel_hat(values, cin):
    real = lax.broadcasted_iota(jnp.int32, (values.shape[0], 1), 0) < cin
    portion = 1.0 / cin.astype(F32)
    centre = jnp.where(real, values - jnp.sum(values, axis=0, keepdims=True) * portion, 0.0)
    return centre * lax.rsqrt(jnp.sum(centre * centre, axis=0, keepdims=True) * portion + 1e-05)


def each_block(count, body):
    def step(n, carry):
        body(n)
        return carry

    lax.fori_loop(0, count, step, 0, unroll=4)


def cross_body(place, near, made, extra, need, flush):
    asks, gain, shift, raw, owner, core_out, residual, vectors, up_w, down_w = near
    (
        normal, scores, kept, mixed, top, first_sum, cross_normed, slopes, cross_active, second_sum, second, hats
    ) = made
    (heap,) = extra
    ways, channels, size = normal.shape
    rows = asks.shape[0]
    lat_rows = heap.shape[0]
    at = pl.multiple_of(place[2] * lat_rows, lat_rows)
    large = pl.ds(at, lat_rows)
    need(0, 1, 2, 3)
    columns = lax.broadcasted_iota(jnp.int32, (1, size), 1)
    top[...] = jnp.full(top.shape, -1e30, F32)

    def score(n):
        hat = pixel_hat(raw[n].astype(F32), place[3])
        hats[n] = hat.astype(BF)
        value = (hat * gain[...] + shift[...]).astype(BF)
        normal[n] = value
        places = columns + n * size
        found = dot(asks[large, :], value)
        found = jnp.where((places >= place[0]) & (places < place[1]), found, -1e30)
        scores[n] = found
        top[...] = jnp.maximum(top[...], jnp.max(found, axis=1, keepdims=True))

    each_block(ways, score)
    flush(0, 1, 11)
    need(4)
    edge = jnp.where(
        columns < place[0], normal[0].astype(F32), normal[ways - 1].astype(F32)
    ).astype(BF)
    row_item = lax.broadcasted_iota(jnp.int32, (rows, 1), 0) // lat_rows
    inside = (owner[...] == row_item) & (place[2] != row_item)
    found = jnp.where(inside, dot(asks[...], edge), -1e30)
    raised = jnp.exp(found - jnp.max(found, axis=1, keepdims=True))
    weights = raised * (1.0 / jnp.sum(raised, axis=1, keepdims=True))
    weights = jnp.where(inside, weights, 0.0).astype(BF)
    kept[...] = weights
    mixed[...] = dot_nt(weights, edge)
    heap[...] = jnp.zeros(heap.shape, F32)
    peak = top[...]

    def gather(n, carry):
        raised = jnp.exp(scores[n] - peak)
        heap[...] += dot_nt(raised.astype(BF), normal[n])
        return carry + jnp.sum(raised, axis=1, keepdims=True)

    whole = lax.fori_loop(0, ways, gather, jnp.zeros((lat_rows, 1), F32))
    mixed[large, :] = heap[...] * (1.0 / whole)
    top[...] = peak + jnp.log(whole)
    flush(2, 3, 4)
    need(5, 6, 7, 8, 9)

    def net(part):
        first = residual[part, :] + dot(mixed[part, :].astype(BF), core_out[...])
        first_sum[part, :] = first
        hat, unused = norm_parts(first)
        normed = (hat * vectors[0:1, :] + vectors[1:2, :]).astype(BF)
        cross_normed[part, :] = normed
        active, slope = gelu_both(dot(normed, up_w[...]))
        active = active.astype(BF)
        cross_active[part, :] = active
        slopes[part, :] = slope
        value = first + dot(active, down_w[...])
        second_sum[part, :] = value
        second[part, :] = value.astype(BF)

    each_part(rows, net)


def cross_back_body(place, near, made, extra, need, flush):
    (
        got, upstream, slopes, down_w, up_w, first_sum, vectors, core_out, normal, mixed, kept, asks, scores, top,
        hats, value_w, cross_active, cross_normed, *latent_side,
    ) = near
    grad, corner, heap, turned, *small_scratch = extra
    if not latent_side:
        (
            grad_second_low, grad_cross_hidden, grad_first, grad_first_low, sums, moves, pix, pixel_sums,
            core_value, cross_mixed,
        ) = made
    else:
        grad_second_low, grad_cross_hidden, grad_first_low, moves, pixel_sums, sums, grad_first, cross_mixed = (
            small_scratch[:8]
        )
        pix, grad_latents, small_mine, small_other, *halves = made
    ways, channels, size = normal.shape
    rows = asks.shape[0]
    lat_rows = heap.shape[0]
    at = pl.multiple_of(place[2] * lat_rows, lat_rows)
    large = pl.ds(at, lat_rows)
    sums[...] = jnp.zeros(sums.shape, F32)
    pixel_sums[...] = jnp.zeros(pixel_sums.shape, F32)
    need(0, 1, 2, 3, 4, 5, 6, 7)

    def net(part):
        grad_second = upstream[part, :] + got[part, :].astype(F32)
        low = grad_second.astype(BF)
        grad_second_low[part, :] = low
        grad_hidden = (dot_nt(low, down_w[...]) * slopes[part, :]).astype(BF)
        grad_cross_hidden[part, :] = grad_hidden
        grad_normed = dot_nt(grad_hidden, up_w[...])
        hat, inv = norm_parts(first_sum[part, :])
        sums[0:1, :] += jnp.sum(grad_normed * hat, axis=0, keepdims=True)
        sums[1:2, :] += jnp.sum(grad_normed, axis=0, keepdims=True)
        value = grad_second + norm_slope(hat, inv, vectors[0:1, :], grad_normed)
        grad_first[part, :] = value
        low = value.astype(BF)
        grad_first_low[part, :] = low
        grad[part, :] = dot_nt(low, core_out[...]).astype(BF)

    each_part(rows, net)
    if not latent_side:
        flush(0, 1, 2, 3, 4)
    need(8, 9, 10, 11, 12, 13, 14)
    columns = lax.broadcasted_iota(jnp.int32, (1, size), 1)
    early = columns < place[0]
    edge = jnp.where(early, normal[0].astype(F32), normal[ways - 1].astype(F32)).astype(BF)
    deltas = jnp.sum(grad[...].astype(F32) * mixed[...], axis=1, keepdims=True)
    weights = kept[...]
    spread = (weights.astype(F32) * (dot(grad[...], edge) - deltas)).astype(BF)
    moves[...] = dot_nt(spread, edge).astype(BF)
    corner[...] = dot_tn(asks[...], spread) + dot_tn(grad[...], weights)
    heap[...] = jnp.zeros(heap.shape, F32)
    own = grad[large, :]
    own_asks = asks[large, :]
    deltas = jnp.sum(own.astype(F32) * mixed[large, :], axis=1, keepdims=True)
    level = top[...]

    def block(n):
        value = normal[n]
        weights = jnp.exp(scores[n] - level)
        spread = (weights * (dot(own, value) - deltas)).astype(BF)
        heap[...] += dot_nt(spread, value)
        part = dot_tn(own_asks, spread) + dot_tn(own, weights.astype(BF))
        use = ((n == 0) & early) | ((n == ways - 1) & jnp.logical_not(early))
        part = part + jnp.where(use, corner[...], 0.0)
        pix[n] = part.astype(BF)
        hat = hats[n].astype(F32)
        pixel_sums[0] += jnp.sum(part * hat, axis=1, keepdims=True)
        pixel_sums[1] += jnp.sum(part, axis=1, keepdims=True)

    each_block(ways, block)
    moves[large, :] = heap[...].astype(BF)
    if latent_side:
        flush(0)
    else:
        flush(5, 6, 7)
    need(15, 16, 17)
    mixed_low = mixed[...].astype(BF)
    cross_mixed[...] = dot(mixed_low, value_w[...]).astype(BF)
    core_low = dot_tn(mixed_low, grad_first_low[...]).astype(BF)
    if not latent_side:
        core_value[...] = core_low
        return
    write_halves(
        ((cross_active, grad_second_low), (cross_normed, grad_cross_hidden)),
        ((halves[0], place[4]), (halves[1], 1 - place[4])), place[5], X_FIRST, ways // 2, turned,
    )
    write_halves(
        ((cross_mixed, grad_first_low),),
        ((halves[2], place[4]), (halves[3], 1 - place[4])), place[5], Y_FIRST, ways // 2, turned,
    )
    flush(4, 5, 6, 7)
    core_in, residual, gain_row, out_w, normed, queries, item_sums = latent_side
    need(18, 19, 20, 21, 22, 23, 24)
    small_parts(
        place[4], place[5], moves, core_in, residual, grad_first, gain_row, core_low, out_w, normed, queries,
        sums, item_sums, pixel_sums, grad_latents, small_mine, small_other, *small_scratch[8:],
    )


def cross(place, raw_all, gain, shift, asks, owner, residual, core_out, vectors, up, down, lat_rows):
    ways, channels, size = raw_all.shape
    rows, width = residual.shape
    low = jax.ShapeDtypeStruct((rows, width), BF)
    wide = jax.ShapeDtypeStruct((rows, width), F32)
    (
        normal, scores, kept, mixed, top, first_sum, cross_normed, slopes, cross_active, second_sum, second, hats
    ) = streamed(
        "cross",
        cross_body,
        place,
        [asks, gain, shift, raw_all, owner, core_out, residual, vectors, up, down],
        [
            jax.ShapeDtypeStruct((ways, channels, size), BF),
            jax.ShapeDtypeStruct((ways, lat_rows, size), F32),
            jax.ShapeDtypeStruct((rows, size), BF),
            jax.ShapeDtypeStruct((rows, channels), F32),
            jax.ShapeDtypeStruct((lat_rows, 1), F32),
            wide,
            low,
            wide,
            low,
            wide,
            low,
            jax.ShapeDtypeStruct((ways, channels, size), BF),
        ],
        [pltpu.VMEM((lat_rows, channels), F32)],
    )
    return (
        mixed, kept, scores, top, normal, first_sum, second_sum, second, cross_normed, cross_active, slopes, hats
    )


def cross_back(
    place, got, upstream, first_sum, slopes, vectors, core_out, up, down,
    hats, normal, asks, mixed, kept, scores, top, cross_active, cross_normed, value_w, latent_side, groups,
):
    ways, channels, size = hats.shape
    rows, width = upstream.shape
    lat_rows = top.shape[0]
    shape = jax.ShapeDtypeStruct
    low, wide = shape((rows, width), BF), shape((rows, width), F32)
    scratch = [
        pltpu.VMEM((rows, channels), BF),
        pltpu.VMEM((channels, size), F32),
        pltpu.VMEM((lat_rows, channels), F32),
        pltpu.VMEM((width // 2, rows), BF),
    ]
    moves, pixel_sums, sums = shape((rows, channels), BF), shape((2, channels, 1), F32), shape((2, width), F32)
    pix = shape((ways, channels, size), BF)
    if latent_side:
        total = small_lines(channels)
        small = shape((4, ways // 4 * (total // 4), 2 * width // ways), BF)
        outs = [pix, wide, small, small] + [
            shape((groups, width // 2, count * width // groups), BF) for count in (2, 2, 1, 1)
        ]
        inner = [low, low, low, moves, pixel_sums, sums, wide, low, shape((16, width), F32), shape((total, width), BF)]
        scratch += [pltpu.VMEM(value.shape, value.dtype) for value in inner]
    else:
        outs = [low, low, wide, low, sums, moves, pix, pixel_sums, shape((channels, width), BF), low]
    return streamed(
        "cross_back",
        cross_back_body,
        place,
        [
            got, upstream, slopes, down, up, first_sum, vectors, core_out, normal, mixed, kept, asks, scores, top,
            hats, value_w, cross_active, cross_normed, *latent_side,
        ],
        outs,
        scratch,
    )


def second_hop_body(place, near, made, extra, need, flush):
    for at, out in enumerate(made):
        need(3 * at, 3 * at + 1, 3 * at + 2)
        value = near[3 * at][...].astype(F32) + near[3 * at + 1][...].astype(F32)
        out[...] = (value + near[3 * at + 2][...].astype(F32)).astype(BF)
        flush(at)


def pieces_body(place, near, made, extra, need, flush):
    sums, every = extra[:3], extra[3]
    chips, unused, block = every.shape
    for at, here in enumerate(sums):
        need(*range(4 * at, 4 * at + 4))
        value = near[4 * at][...].astype(F32)
        for k in range(1, 4):
            value = value + near[4 * at + k][...].astype(F32)
        here[...] = value.astype(BF)
    lines = sums[2].shape[0] // (chips // 2)
    for z in range(chips):
        at = 0
        for here in sums[:2]:
            for k in range(here.shape[1] // block):
                every[z, at : at + block, :] = here[z * block : (z + 1) * block, k * block : (k + 1) * block]
                at += block
        every[z, at:, :] = sums[2][
            z // 2 * lines : (z // 2 + 1) * lines, z % 2 * block : (z % 2 + 1) * block
        ]
    for m, out in enumerate(made):
        out[...] = every[place[0] ^ m]
        flush(m)


def second_hop(flows, first_got):
    ins = []
    for (mine, got, unused), first in zip(flows, first_got):
        ins += [(mine, 3), (got, 3), (first, 1)]
    return streamed(
        "second_hop",
        second_hop_body,
        jnp.zeros((1,), jnp.int32),
        ins,
        [jax.ShapeDtypeStruct(mine.shape[1:], BF) for mine, unused, hop in flows],
        [],
    )


def pieces_of(chip, chips, block, flows, first_got, hops):
    ins = []
    for (mine, got, unused), first, last in zip(flows, first_got, hops):
        ins += [(mine, 2), (got, 2), (first, 0), last]
    shapes = [mine.shape[1:] for mine, unused, hop in flows]
    lines = sum(shape[1] for shape in shapes[:2]) + shapes[2][0] // (chips // 2)
    return streamed(
        "pieces",
        pieces_body,
        chip.astype(jnp.int32).reshape(1),
        ins,
        [jax.ShapeDtypeStruct((lines, block), BF)] * chips,
        [pltpu.VMEM(shape, BF) for shape in shapes] + [pltpu.VMEM((chips, lines, block), BF)],
    )


def finish_body(place, near, made, extra, need, flush):
    parts, key_w = near[:4], near[4]
    net_down, net_up, out_weight, query, key, value, pixel_gain, pixel_shift, *gains = made
    every, small = extra
    block = parts[0].shape[1]
    channels, width = key_w.shape
    quarter = width // 4
    tiles = quarter // block
    size = small.shape[0] // 4
    for m in range(4):
        need(m)
        every[m] = parts[m][...]
    for j in range(4):
        m = place[0] ^ j
        small[j * size : (j + 1) * size, :] = every[m, 3 * quarter // block * block :, :]
        for at, out in enumerate((net_down, net_up, out_weight)):
            for k in range(tiles):
                lines = (at * tiles + k) * block
                out[:, j * quarter + k * block : j * quarter + (k + 1) * block] = every[
                    m, lines : lines + block, :
                ].astype(F32)
    flush(0, 1, 2)
    need(4)
    scale = 1.0 / math.sqrt(width)
    query[...] = dot_tn(small[channels : 2 * channels, :], key_w[...]) * scale
    cin = key.shape[0]
    value[...] = small[:channels, :].astype(F32)[:cin]
    key[...] = small[2 * channels : 3 * channels, :].astype(F32)[:cin] * scale
    vectors = small[3 * channels :, :].astype(F32)
    count = -(-channels // block)
    for at, out in enumerate((pixel_gain, pixel_shift)):
        line = [vectors[2 + at * count + k : 3 + at * count + k, :] for k in range(count)]
        out[...] = jnp.concatenate(line, axis=1)[0, :cin]
    for at, out in enumerate(gains):
        line = at if at < 2 else 2 * count + at
        out[...] = vectors[line]


def finish(item, parts, key_w, cin):
    lines, block = parts[0].shape
    channels, width = key_w.shape
    shape = jax.ShapeDtypeStruct
    total = small_lines(channels)
    tall, flat = shape((block, width), F32), shape((cin, block), F32)
    return streamed(
        "finish",
        finish_body,
        item.astype(jnp.int32).reshape(1),
        [*parts, key_w],
        [tall, tall, tall, tall, flat, flat] + [shape((cin,), F32)] * 2 + [shape((block,), F32)] * 8,
        [pltpu.VMEM((4, lines, block), BF), pltpu.VMEM((total, block), BF)],
    )


def on_device(
    latents,
    pixels,
    lengths,
    out_grad,
    latent_gain,
    latent_shift,
    pixel_gain,
    pixel_shift,
    query_weight,
    key_weight,
    value_weight,
    out_weight,
    cross_gain,
    cross_shift,
    cross_up,
    cross_down,
    self_gain,
    self_shift,
    self_packed,
    self_out,
    final_gain,
    final_shift,
    latent_up,
    latent_down,
):
    items = latents.shape[1]
    lat_rows = latents.shape[2]
    width = latents.shape[3]
    pix_rows = pixels.shape[1]
    cin = pixels.shape[2]
    ways = lax.axis_size("lat")
    groups = lax.axis_size("items")
    sub = ways // items
    rows = items * lat_rows
    piece = lat_rows // sub
    score_scale = 1.0 / math.sqrt(width)
    head_scale = 1.0 / math.sqrt(HEAD)
    lat_index = lax.axis_index("lat")
    core = lat_index % 2

    channels = -(-cin // 16) * 16
    pad = ((0, channels - cin), (0, 0))
    spans = lengths[0]
    starts = jnp.cumsum(spans) - spans
    largest = jnp.argmax(spans).astype(jnp.int32)
    large_start = starts[largest]
    place = jnp.stack(
        [
            large_start,
            large_start + spans[largest],
            largest,
            jnp.asarray(cin, jnp.int32),
            core,
            lax.axis_index("items"),
        ]
    ).astype(jnp.int32)
    edge_places = jnp.arange(pix_rows, dtype=jnp.int32)
    edge_places = jnp.where(edge_places < large_start, edge_places, edge_places + pix_rows * (ways - 1))
    owner = jnp.sum((edge_places[None, :] >= starts[:, None]).astype(jnp.int32), axis=0) - 1
    owner = owner[None, :]

    swap = [(i, i ^ 1) for i in range(ways)]
    same_core = [list(range(0, ways, 2)), list(range(1, ways, 2))]
    block = width // ways

    tie = lax.optimization_barrier

    chips = ways // 2
    chip = lat_index // 2
    item = lax.axis_index("items")

    def swap_items(part, m):
        return lax.ppermute(part, "items", [(i, i ^ m) for i in range(groups)])

    def near_chips(pieces):
        if chips != 4:
            whole = jnp.stack([pieces(j) for j in range(chips)])
            moved = lax.all_to_all(
                whole, "lat", split_axis=0, concat_axis=0, tiled=True, axis_index_groups=same_core
            )
            return [moved[j] for j in range(chips)]
        return [pieces(chip)] + [
            lax.ppermute(
                pieces(chip ^ m), "lat", [(i, ((i // 2) ^ m) * 2 + i % 2) for i in range(ways)]
            )
            for m in range(1, chips)
        ]

    def total(parts):
        value = parts[0].astype(F32)
        for part in parts[1:]:
            value = value + part.astype(F32)
        return value

    def add(left, right):
        return (left.astype(F32) + right.astype(F32)).astype(BF)

    def over_chips_whole(here):
        parts = lax.all_to_all(
            here, "lat", split_axis=0, concat_axis=0, tiled=True, axis_index_groups=same_core
        )
        return jnp.sum(parts.astype(F32), axis=0).astype(BF)

    def gather_items(part):
        return jnp.stack([part] + [swap_items(part, m) for m in range(1, groups)])

    def by_item(parts):
        return [lax.dynamic_index_in_dim(parts, item ^ j, 0, keepdims=False) for j in range(groups)]

    def weight_of(parts):
        return jnp.concatenate(by_item(parts), axis=1).astype(F32)

    pixels_low = jnp.pad(pixels[0].T, pad)
    raw_all = lax.all_gather(pixels_low, "lat", axis=0, tiled=False)
    gain_column = jnp.pad(pixel_gain[:, None], pad)
    shift_column = jnp.pad(pixel_shift[:, None], pad)
    key_pad = jnp.pad(key_weight, pad)
    value_pad = jnp.pad(value_weight, pad)

    to_pixels = (dot_nt(query_weight, key_pad) * score_scale).astype(BF)
    from_pixels = dot(value_pad, out_weight).astype(BF)

    residual = latents.reshape(rows, width)
    upstream = out_grad.reshape(rows, width)
    normed = layer_norm(residual, latent_gain, latent_shift).astype(BF)
    asks = dot(normed, to_pixels).astype(BF)
    latent_queries = dot(normed, query_weight).astype(BF)

    def reshare(values):
        moved = lax.all_to_all(
            values.reshape(ways, piece, width), "lat", split_axis=0, concat_axis=0, tiled=True
        )
        return moved.reshape(rows, width)

    (
        raw_all, value_pad, upstream_low, asks, latent_queries, from_pixels, to_pixels, gain_column, shift_column, place, owner
    ) = tie(
        (
            raw_all, value_pad, upstream.astype(BF), asks, latent_queries, from_pixels, to_pixels, gain_column, shift_column,
            place, owner,
        )
    )
    grad_low = reshare(upstream_low)
    cross_vectors = jnp.stack([cross_gain, cross_shift])
    (
        mixed, kept, scores, top, normal, first_sum, second_sum, second, cross_normed, cross_active, slopes,
        hats,
    ) = cross(
        place, raw_all, gain_column, shift_column, asks, owner, residual, from_pixels, cross_vectors,
        cross_up, cross_down, lat_rows,
    )
    second, grad_low = tie((second, grad_low))
    second = reshare(second)
    item_place = jnp.stack([core, item]).astype(jnp.int32)
    item_vectors = jnp.stack([self_gain, self_shift, final_gain, final_shift])
    if sub == 1:
        (
            result_add, second_add, self_normed, grad_packed, self_mixed, grad_third_low,
            final_normed, final_active, grad_final_hidden, item_sums, final_other, packed_other,
        ) = item_block(item_place, groups, second, grad_low, item_vectors, self_packed, self_out, latent_up, latent_down)
    else:
        whole_rows = rows * sub
        same_item = [[i * sub + s for s in range(sub)] for i in range(items)]
        second_wide = second.astype(F32)
        self_normed = layer_norm(second_wide, self_gain, self_shift).astype(BF)
        packed = dot(self_normed, self_packed).astype(BF)
        pairs = lax.all_gather(
            packed[:, width:], "lat", axis=0, tiled=True, axis_index_groups=same_item
        )
        self_mixed, self_low = attend(packed, pairs, rows, whole_rows)
        self_add = dot(self_mixed, self_out)
        third = second_wide + self_add
        final_normed = layer_norm(third, final_gain, final_shift).astype(BF)
        final_hidden = dot(final_normed, latent_up)
        final_active = jax.nn.gelu(final_hidden).astype(BF)
        result_add = (self_add + dot(final_active, latent_down)).astype(BF)
        grad_final_hidden = gelu_back(final_hidden, dot_nt(grad_low, latent_down)).astype(BF)
        back_third, grad_final_gain, grad_final_shift = norm_back(
            third, final_gain, dot_nt(grad_final_hidden, latent_up)
        )
        grad_third_low = (grad_low.astype(F32) + back_third).astype(BF)
        grad_mixed = dot_nt(grad_third_low, self_out).astype(BF)
        grad_queries, grad_pairs = attend_back(grad_mixed, self_low, packed, pairs, rows, whole_rows)
        grad_pairs = lax.psum_scatter(
            grad_pairs, "lat", scatter_dimension=0, tiled=True, axis_index_groups=same_item
        )
        grad_packed = jnp.concatenate([grad_queries, grad_pairs], axis=1)
        back_second, grad_self_gain, grad_self_shift = norm_back(
            second_wide, self_gain, dot_nt(grad_packed, self_packed)
        )
        second_add = (back_third + back_second).astype(BF)
        item_sums = jnp.stack([grad_self_gain, grad_self_shift, grad_final_gain, grad_final_shift])
    second_got = reshare(second_add)
    item_pairs = (
        (final_active, grad_low),
        (final_normed, grad_final_hidden),
        (self_mixed, grad_third_low),
        (self_normed, grad_packed),
    )
    final_pairs, packed_pairs = item_pairs[:3], item_pairs[3:]
    if sub > 1:
        final_other = half_plain(final_pairs, 1 - core, item, X_FIRST, ways).astype(BF)
        packed_other = half_plain(packed_pairs, 1 - core, item, Y_FIRST, ways).astype(BF)
    final_got = lax.ppermute(final_other, "lat", swap)
    packed_got = lax.ppermute(packed_other, "lat", swap)
    final_parts = half_grads(final_pairs, core, item, X_FIRST, ways, final_got)
    packed_parts = list(half_grads(packed_pairs, core, item, Y_FIRST, ways, packed_got, True))
    final_got, packed_got = [None, swap_items(final_parts[1], 1)], [None, swap_items(packed_parts[1], 2)]
    second_got, result_add, final_got[1], packed_got[1] = tie(
        (second_got, result_add, final_got[1], packed_got[1])
    )
    final_got[0], packed_got[0] = swap_items(final_parts[0], 1), swap_items(packed_parts[0], 2)
    packed_low = swap_items(packed_parts.pop(2), 2)
    final_kept, packed_kept = final_parts[2:], packed_parts[2:]
    result_got = reshare(result_add)

    back_args = (
        place, second_got, upstream, first_sum, slopes, cross_vectors, from_pixels, cross_up, cross_down,
        hats, normal, asks, mixed, kept, scores, top, cross_active, cross_normed, value_pad,
    )
    if block % 128 == 0:
        latent_side = (
            to_pixels, residual, latent_gain[None], out_weight, normed, latent_queries, item_sums
        )
        (
            parts_pix, grad_latents, small_mine, small_other, net_mine, net_other, out_mine, out_other
        ) = cross_back(*back_args, latent_side, groups)
    else:
        (
            grad_second_low, grad_cross_hidden, grad_first, grad_first_low, cross_sums, moves, parts_pix, pixel_sums,
            core_value, cross_mixed,
        ) = cross_back(*back_args, (), groups)
        cross_pairs = ((cross_active, grad_second_low), (cross_normed, grad_cross_hidden))
        net_mine, net_other, out_mine, out_other = [
            half_plain(pairs, half, item, order, ways).astype(BF)
            for pairs, order in ((cross_pairs, X_FIRST), (((cross_mixed, grad_first_low),), Y_FIRST))
            for half in (core, 1 - core)
        ]
        grad_latents, small_mine, small_other = last_block(
            core, item, ways, moves, to_pixels, residual, grad_first, latent_gain[None], core_value, out_weight,
            normed, latent_queries, jnp.concatenate([cross_sums, item_sums, jnp.zeros((2, width), F32)]), pixel_sums,
        )
    (
        parts_pix, grad_latents, small_mine, small_other, net_mine, net_other, out_mine, out_other,
        final_got[0], packed_got[0], packed_low, result_got,
    ) = tie(
        (
            parts_pix, grad_latents, small_mine, small_other, net_mine, net_other, out_mine, out_other,
            final_got[0], packed_got[0], packed_low, result_got,
        )
    )
    grad_pn = lax.psum_scatter(parts_pix, "lat", scatter_dimension=0, tiled=False)
    packed_got[1] = jnp.concatenate([packed_got[1], packed_low])
    net_got = lax.ppermute(net_other, "lat", swap)
    out_got = lax.ppermute(out_other, "lat", swap)
    final_two, packed_two = add(final_kept[1], final_got[1]), add(packed_kept[1], packed_got[1])
    final_two, packed_two = swap_items(final_two, 2), swap_items(packed_two, 1)
    small_got = lax.ppermute(small_other, "lat", swap)
    net_first, out_first = add(net_mine[:2], net_got[:2]), add(out_mine[:2], out_got[:2])
    small_first = add(small_mine[:2], small_got[:2])
    final_two, packed_two, net_first, out_first, small_first = tie(
        (final_two, packed_two, net_first, out_first, small_first)
    )
    first_got = [swap_items(net_first, 1), swap_items(out_first, 2), swap_items(small_first, 2)]
    item_here = jnp.concatenate(
        [
            total([final_kept[0], final_got[0], final_two]).astype(BF),
            total([packed_kept[0], packed_got[0], packed_two]).astype(BF),
        ],
        axis=1,
    )
    first_got = tie(tuple(first_got))
    item_part = over_chips_whole(item_here.reshape(chips, block, -1))
    flows = ((net_mine, net_got, 2), (out_mine, out_got, 1), (small_mine, small_got, 1))
    fast = block % 128 == 0 and chips == 4
    if fast:
        hops = second_hop(flows, first_got)
    else:
        hops = [
            total([mine[3], got[3], first[1]]).astype(BF)
            for (mine, got, hop), first in zip(flows, first_got)
        ]
    hops = [swap_items(part, hop) for part, (mine, got, hop) in zip(hops, flows)]
    if fast:
        pieces = pieces_of(chip, chips, block, flows, first_got, hops)
        item_part, grad_pn, *pieces = tie((item_part, grad_pn, *pieces))
        rest = [pieces[0]] + [
            lax.ppermute(
                pieces[m], "lat", [(i, ((i // 2) ^ m) * 2 + i % 2) for i in range(ways)]
            )
            for m in range(1, chips)
        ]
    else:
        item_part, grad_pn, *hops = tie((item_part, grad_pn, *hops))
        net_here, out_here, small_here = [
            total([mine[2], got[2], first[0], last]).astype(BF)
            for (mine, got, hop), first, last in zip(flows, first_got, hops)
        ]
        lines = small_here.shape[0] // (chips // 2)
        pieces = jnp.stack(
            [
                jnp.concatenate(
                    [
                        whole[z * block : (z + 1) * block, k * block : (k + 1) * block]
                        for whole in (net_here, out_here)
                        for k in range(whole.shape[1] // block)
                    ]
                    + [small_here[z // 2 * lines : (z // 2 + 1) * lines, z % 2 * block : (z % 2 + 1) * block]]
                )
                for z in range(chips)
            ]
        )
        rest = near_chips(lambda z: lax.dynamic_index_in_dim(pieces, z, 0, keepdims=False))
    item_parts = [item_part] + [swap_items(item_part, m) for m in range(1, groups)]
    tied = tie((*rest, *item_parts))
    rest, item_parts = total(tied[: len(rest)]).astype(BF), jnp.stack(tied[len(rest) :])
    quarter = width // groups
    grad_latent_down, grad_latent_up, grad_self_out = [
        weight_of(item_parts[:, :, at * quarter : (at + 1) * quarter]) for at in range(3)
    ]
    grad_self_packed = weight_of(item_parts[:, :, 3 * quarter :])
    result = second_sum + result_got.astype(F32)
    grad_pn = grad_pn.astype(F32)[:cin]
    pix_hat, pix_inv = norm_parts(pixels[0].T.astype(F32), 0)
    scaled = grad_pn * pixel_gain[:, None]
    grad_pixels = pix_inv * (
        scaled
        - jnp.mean(scaled, axis=0, keepdims=True)
        - pix_hat * jnp.mean(scaled * pix_hat, axis=0, keepdims=True)
    )
    rest_parts = [rest] + [swap_items(rest, m) for m in range(1, groups)]
    if block % 128 == 0:
        (
            grad_cross_down, grad_cross_up, grad_out_weight, grad_query_weight, grad_key_weight, grad_value_weight,
            *vectors,
        ) = finish(item, rest_parts, key_pad, cin)
        grad_pixel_gain, grad_pixel_shift, *gains = [value.reshape(-1) for value in vectors]
    else:
        rest_parts = jnp.stack(rest_parts)
        tall = quarter // block * block
        grad_cross_down, grad_cross_up, grad_out_weight = [
            weight_of(
                rest_parts[:, at * tall : (at + 1) * tall]
                .reshape(groups, quarter // block, block, block)
                .transpose(0, 2, 1, 3)
                .reshape(groups, block, quarter)
            )
            for at in range(3)
        ]
        small = jnp.concatenate(by_item(rest_parts[:, 3 * tall :]), axis=0).astype(F32)
        grad_query_weight = dot_tn(small[channels : 2 * channels].astype(BF), key_pad) * score_scale
        grad_key_weight = small[2 * channels : 2 * channels + cin] * score_scale
        grad_value_weight = small[:cin]
        head = small[3 * channels : 3 * channels + 2]
        sums = small[3 * channels + 2 :]
        count = -(-channels // block)
        grad_pixel_gain = sums[:count].reshape(-1)[:cin]
        grad_pixel_shift = sums[count : 2 * count].reshape(-1)[:cin]
        gains = [head[0], head[1]] + [sums[2 * count + at] for at in range(6)]
    shape = (1, items, lat_rows, width)
    return (
        result.reshape(shape),
        grad_latents.reshape(shape),
        grad_pixels.T[None],
        gains[0],
        gains[1],
        grad_pixel_gain,
        grad_pixel_shift,
        grad_query_weight,
        grad_key_weight,
        grad_value_weight,
        grad_out_weight,
        gains[2],
        gains[3],
        grad_cross_up,
        grad_cross_down,
        gains[4],
        gains[5],
        grad_self_packed,
        grad_self_out,
        gains[6],
        gains[7],
        grad_latent_up,
        grad_latent_down,
    )


def solution(mesh):
    rows = P("items", None, "lat", None)
    in_specs = (rows, P("items", "lat", None), P("items", None), rows) + (P(),) * 20
    lane = P("lat")
    tall = P("lat", None)
    wide = P(None, "lat")
    out_specs = (
        rows,
        rows,
        P("items", "lat", None),
        lane,
        lane,
        P(),
        P(),
        tall,
        wide,
        wide,
        tall,
        lane,
        lane,
        tall,
        tall,
        lane,
        lane,
        tall,
        tall,
        lane,
        lane,
        tall,
        tall,
    )
    return jax.shard_map(
        on_device, mesh=mesh, in_specs=in_specs, out_specs=out_specs, check_vma=False
    )
```

```python
import math

import jax
import jax.numpy as jnp
from jax import lax
from jax.experimental import pallas as pl
from jax.experimental.pallas import tpu as pltpu
from jax.sharding import PartitionSpec as P

HEADS = 8
HEAD = 128
X_FIRST = (1, 3, 0, 2)
Y_FIRST = (2, 3, 0, 1)
BF = jnp.bfloat16
F32 = jnp.float32


def norm_parts(values, axis=-1):
    centre = values - jnp.mean(values, axis=axis, keepdims=True)
    spread = jnp.mean(centre * centre, axis=axis, keepdims=True)
    inv = lax.rsqrt(spread + 1e-05)
    return centre * inv, inv


def layer_norm(values, gain, shift):
    hat, unused = norm_parts(values)
    return hat * gain + shift


def norm_back(values, gain, upstream):
    hat, inv = norm_parts(values)
    scaled = upstream * gain
    back = inv * (
        scaled
        - jnp.mean(scaled, axis=-1, keepdims=True)
        - hat * jnp.mean(scaled * hat, axis=-1, keepdims=True)
    )
    return back, jnp.sum(upstream * hat, axis=0), jnp.sum(upstream, axis=0)


def gelu_back(hidden, upstream):
    unused, pullback = jax.vjp(jax.nn.gelu, hidden)
    return pullback(upstream)[0]


def dot(left, right):
    return jnp.dot(left, right, preferred_element_type=F32)


def dot_tn(left, right):
    return lax.dot_general(left, right, (((0,), (0,)), ((), ())), preferred_element_type=F32)


def dot_nt(left, right):
    return lax.dot_general(left, right, (((1,), (1,)), ((), ())), preferred_element_type=F32)


def softmax(scores):
    raised = jnp.exp(scores - jnp.max(scores, axis=-1, keepdims=True))
    return raised / jnp.sum(raised, axis=-1, keepdims=True)


def attend_kernel(query, key, value, out, kept):
    scores = dot_nt(query[...], key[...]) * (1.0 / math.sqrt(HEAD))
    raised = jnp.exp(scores - jnp.max(scores, axis=-1, keepdims=True))
    weights = (raised * (1.0 / jnp.sum(raised, axis=-1, keepdims=True))).astype(BF)
    kept[0] = weights
    out[...] = dot(weights, value[...]).astype(BF)


def attend(queries, pairs, rows, whole_rows):
    column = lambda at: pl.BlockSpec((whole_rows, HEAD), lambda h: (0, h + at))
    own = pl.BlockSpec((rows, HEAD), lambda h: (0, h))
    return pl.pallas_call(
        attend_kernel,
        grid=(HEADS,),
        in_specs=[own, column(0), column(HEADS)],
        out_specs=[own, pl.BlockSpec((1, rows, whole_rows), lambda h: (h, 0, 0))],
        out_shape=[
            jax.ShapeDtypeStruct((rows, HEADS * HEAD), BF),
            jax.ShapeDtypeStruct((HEADS, rows, whole_rows), BF),
        ],
        compiler_params=pltpu.CompilerParams(vmem_limit_bytes=40 << 20),
        name="attend",
    )(queries, pairs, pairs)


def attend_back_kernel(grad, weights_ref, query, key, value, grad_query, grad_pair):
    at = pl.multiple_of(pl.program_id(0) * HEAD, HEAD)
    also = pl.multiple_of(pl.program_id(0) * HEAD + HEADS * HEAD, HEAD)
    weights_low = weights_ref[0]
    weights = weights_low.astype(F32)
    upstream = grad[...]
    grad_weights = dot_nt(upstream, value[...])
    grad_pair[:, pl.ds(also, HEAD)] = dot_tn(weights_low, upstream).astype(BF)
    inner = jnp.sum(weights * grad_weights, axis=-1, keepdims=True)
    spread = (weights * (grad_weights - inner)).astype(BF)
    scale = 1.0 / math.sqrt(HEAD)
    grad_query[...] = (dot(spread, key[...]) * scale).astype(BF)
    grad_pair[:, pl.ds(at, HEAD)] = (dot_tn(spread, query[...]) * scale).astype(BF)


def attend_back(grad, weights, queries, pairs, rows, whole_rows):
    column = lambda at: pl.BlockSpec((whole_rows, HEAD), lambda h: (0, h + at))
    own = pl.BlockSpec((rows, HEAD), lambda h: (0, h))
    return pl.pallas_call(
        attend_back_kernel,
        grid=(HEADS,),
        in_specs=[
            own,
            pl.BlockSpec((1, rows, whole_rows), lambda h: (h, 0, 0)),
            own,
            column(0),
            column(HEADS),
        ],
        out_specs=[own, pl.BlockSpec((whole_rows, 2 * HEADS * HEAD), lambda h: (0, 0))],
        out_shape=[
            jax.ShapeDtypeStruct((rows, HEADS * HEAD), BF),
            jax.ShapeDtypeStruct((whole_rows, 2 * HEADS * HEAD), BF),
        ],
        compiler_params=pltpu.CompilerParams(vmem_limit_bytes=40 << 20),
        name="attend_back",
    )(grad, weights, queries, pairs, pairs)


def half_columns(left, half, blocks):
    step = left.shape[1] // (2 * blocks)
    return jnp.concatenate(
        [left[:, pl.ds(pl.multiple_of((2 * z + half) * step, step), step)] for z in range(blocks)], axis=1
    ).T


def half_body(order, blocks, place, near, made, extra, need, flush):
    (turned,) = extra
    groups = len(order)
    count = (len(near) - groups) // 2
    added = near[2 * count :]
    for index in range(count):
        need(index)
        turned[index] = half_columns(near[index], place[0], blocks)
    need(*range(count, 2 * count))
    cut = len(made) > groups
    for place_in, p in enumerate((1, 0, 2, 3)):
        need(2 * count + place_in)
        at = 0
        outs = [p + (cut and p > 1)] if p != 1 or not cut else [1, 2]
        for index, right in enumerate(near[count : 2 * count]):
            size = right.shape[1] // groups
            lanes = pl.ds(pl.multiple_of((place[1] ^ order[p]) * size, HEAD), size)
            value = dot(turned[index], right[:, lanes]) + added[place_in][:, at : at + size].astype(F32)
            value = value.astype(BF)
            lines = 0
            for out in outs:
                count_of = made[out].shape[0]
                made[out][:, at : at + size] = value[lines : lines + count_of]
                lines += count_of
            at += size
        flush(*outs)


def half_plain(pairs, half, item, order, ways):
    blocks = ways // 2
    rows, width = pairs[0][0].shape
    groups = len(order)
    outs = []
    for left, right in pairs:
        columns = lax.dynamic_index_in_dim(
            left.reshape(rows, blocks, 2, width // ways), half, 2, keepdims=False
        ).reshape(rows, width // 2)
        value = dot_tn(columns, right).reshape(width // 2, groups, -1).transpose(1, 0, 2)
        outs.append(value)
    value = jnp.concatenate(outs, axis=2)
    return jnp.stack([lax.dynamic_index_in_dim(value, item ^ m, 0, keepdims=False) for m in order])


def half_grads(pairs, half, item, order, ways, added, cut=False):
    rows, width = pairs[0][0].shape
    blocks, groups = ways // 2, len(order)
    total = sum(right.shape[1] for unused, right in pairs) // groups
    if (width // ways) % 128:
        value = (half_plain(pairs, half, item, order, ways) + added.astype(F32)).astype(BF)
        parts = [value[p] for p in range(groups)]
        if cut:
            parts[1:2] = [parts[1][: width // 4], parts[1][width // 4 :]]
        return parts
    shapes = [jax.ShapeDtypeStruct((width // 2, total), BF)] * groups
    if cut:
        shapes[1:2] = [jax.ShapeDtypeStruct((width // 4, total), BF)] * 2
    return streamed(
        "half_grads",
        lambda *refs: half_body(order, blocks, *refs),
        jnp.stack([half, item]).astype(jnp.int32),
        [left for left, unused in pairs]
        + [right for unused, right in pairs]
        + [(added, p) for p in (1, 0, 2, 3)],
        shapes,
        [pltpu.VMEM((len(pairs), width // 2, rows), BF)],
    )


def small_parts(
    core, item, moves, core_in, residual, grad_first, gain, core_value, out_w, normed, queries,
    sums, item_sums, pixel_sums, grad_latents, mine, other, stacked, rest,
):
    rows, width = residual.shape
    block = mine.shape[2] // 2
    chips = width // block // 2
    channels = moves.shape[1]
    stacked[...] = jnp.zeros(stacked.shape, F32)

    def back(part):
        grad_normed = dot_nt(moves[part, :], core_in[...])
        hat, inv = norm_parts(residual[part, :])
        stacked[0:1, :] += jnp.sum(grad_normed * hat, axis=0, keepdims=True)
        stacked[1:2, :] += jnp.sum(grad_normed, axis=0, keepdims=True)
        grad_latents[part, :] = grad_first[part, :] + norm_slope(hat, inv, gain[...], grad_normed)

    each_part(rows, back)
    stacked[8:10, :] = sums[...]
    stacked[10:14, :] = item_sums[...]
    for at in range(2):
        line = jnp.broadcast_to(pixel_sums[at], (channels, 128)).T[0:1, :]
        line = jnp.concatenate([line, jnp.zeros((1, -channels % 128), F32)], axis=1)
        for k in range(line.shape[1] // 128):
            for j in range(width // block):
                stacked[2 + 3 * at + k : 3 + 3 * at + k, j * block : j * block + 128] = line[
                    :, k * 128 : (k + 1) * 128
                ]
    rest[0:channels, :] = dot_nt(core_value, out_w[...]).astype(BF)
    rest[channels : 2 * channels, :] = dot_tn(moves[...], normed[...]).astype(BF)
    rest[2 * channels : 3 * channels, :] = dot_tn(moves[...], queries[...]).astype(BF)
    rest[3 * channels :, :] = stacked[...].astype(BF)
    size = rest.shape[0] // 4
    for p, m in enumerate(Y_FIRST):
        lines = pl.ds(pl.multiple_of((item ^ m) * size, 16), size)
        for out, half in ((mine, core), (other, 1 - core)):
            for z in range(chips):
                lanes = pl.ds(pl.multiple_of((2 * z + half) * block, block), block)
                out[p, z // 2 * size : (z // 2 + 1) * size, z % 2 * block : (z % 2 + 1) * block] = rest[
                    lines, lanes
                ]


def small_lines(channels):
    return 3 * channels + 16


def last_block(
    core, item, ways, moves, core_in, residual, grad_first, gain, core_value, out_w, normed, queries,
    vectors, pixel_sums,
):
    rows, width = residual.shape
    channels = moves.shape[1]
    block, chips = width // ways, ways // 2
    grad_normed = dot_nt(moves, core_in)
    back, grad_gain, grad_shift = norm_back(residual, gain[0], grad_normed)
    sums = jnp.pad(pixel_sums.reshape(2, channels), ((0, 0), (0, -channels % block)))
    lines = sums.reshape(-1, 1, block)
    lines = jnp.broadcast_to(lines, (lines.shape[0], ways, block)).reshape(-1, width)
    stack = [
        dot_nt(core_value, out_w),
        dot_tn(moves, normed),
        dot_tn(moves, queries),
        grad_gain[None],
        grad_shift[None],
        lines,
        vectors,
    ]
    count = sum(value.shape[0] for value in stack)
    stack = jnp.concatenate(stack + [jnp.zeros((-count % 64, width), F32)]).astype(BF)
    size = stack.shape[0] // 4
    stack = stack.reshape(4, size, chips // 2, 2, 2, block)
    halves = []
    for half in (core, 1 - core):
        value = lax.dynamic_index_in_dim(stack, half, 4, keepdims=False)
        value = value.transpose(0, 2, 1, 3, 4).reshape(4, chips // 2 * size, 2 * block)
        halves.append(
            jnp.stack([lax.dynamic_index_in_dim(value, item ^ m, 0, keepdims=False) for m in Y_FIRST])
        )
    return grad_first + back, halves[0], halves[1]


GELU_A = 0.044715
GELU_C = math.sqrt(2.0 / math.pi)
PART = 256


def gelu_both(hidden):
    square = hidden * hidden
    bent = jnp.tanh(hidden * (GELU_C + (GELU_C * GELU_A) * square))
    half = 0.5 + 0.5 * bent
    slope = half + (0.5 * hidden) * (1.0 - bent * bent) * (GELU_C + (3.0 * GELU_C * GELU_A) * square)
    return hidden * half, slope


def norm_slope(hat, inv, gain, upstream):
    scaled = upstream * gain
    centre = jnp.mean(scaled, axis=-1, keepdims=True)
    along = jnp.mean(scaled * hat, axis=-1, keepdims=True)
    return inv * (scaled - centre - hat * along)


def each_part(rows, body):
    size = min(PART, rows)

    def step(r, carry):
        body(pl.ds(pl.multiple_of(r * size, size), size))
        return carry

    lax.fori_loop(0, rows // size, step, 0, unroll=True)


def each_head(body):
    def step(h, carry):
        body(h)
        return carry

    lax.fori_loop(0, HEADS, step, 0, unroll=4)


def write_halves(pairs, outs, item, order, blocks, turned):
    at = 0
    for left, right in pairs:
        size = right.shape[1] // len(order)
        for out, half in outs:
            turned[...] = half_columns(left, half, blocks)
            for p, m in enumerate(order):
                lanes = pl.ds(pl.multiple_of((item ^ m) * size, HEAD), size)
                out[p, :, at : at + size] = dot(turned[...], right[:, lanes]).astype(BF)
        at += size


def item_body(place, near, made, extra, need, flush):
    second, vectors, packed_w0, packed_w1, packed_w2, out_w, up_w, down_w, grad_low = near
    (
        self_normed, self_mixed, final_normed, final_active, result_add, grad_final_hidden, grad_third_low,
        second_add, grad_packed, sums, other_first, other_packed,
    ) = made
    packed, raised_low, inverse, mixed, back_third, grad_mixed, turned = extra
    packed_w = (packed_w0, packed_w1, packed_w2)
    rows, width = second.shape
    need(0, 1)
    sums[...] = jnp.zeros(sums.shape, F32)

    def normalize(part):
        hat, unused = norm_parts(second[part, :].astype(F32))
        self_normed[part, :] = (hat * vectors[0:1, :] + vectors[1:2, :]).astype(BF)

    each_part(rows, normalize)
    flush(0)
    for c in range(3):
        need(2 + c)

        def project(part):
            packed[part, c * width : (c + 1) * width] = dot(
                self_normed[part, :], packed_w[c][...]
            ).astype(BF)

        each_part(rows, project)

    def lanes(h, group):
        return pl.ds(pl.multiple_of(h * HEAD + group * width, HEAD), HEAD)

    scale = 1.0 / math.sqrt(HEAD)

    def attend_head(h):
        scores = dot_nt(packed[:, lanes(h, 0)], packed[:, lanes(h, 1)])
        peak = jnp.max(scores, axis=-1, keepdims=True)
        raised = jnp.exp2((scores - peak) * (scale * math.log2(math.e)))
        inv = 1.0 / jnp.sum(raised, axis=-1, keepdims=True)
        low = raised.astype(BF)
        raised_low[h] = low
        inverse[h] = inv
        mixed[:, lanes(h, 0)] = dot(low, packed[:, lanes(h, 2)]) * inv

    each_head(attend_head)
    need(5, 6, 7, 8)

    def middle(part):
        low = mixed[part, :].astype(BF)
        self_mixed[part, :] = low
        added = dot(low, out_w[...])
        hat, inv = norm_parts(second[part, :].astype(F32) + added)
        normed = (hat * vectors[2:3, :] + vectors[3:4, :]).astype(BF)
        final_normed[part, :] = normed
        active, slope = gelu_both(dot(normed, up_w[...]))
        active = active.astype(BF)
        final_active[part, :] = active
        result_add[part, :] = (added + dot(active, down_w[...])).astype(BF)
        upstream = grad_low[part, :]
        grad_hidden = (dot_nt(upstream, down_w[...]) * slope).astype(BF)
        grad_final_hidden[part, :] = grad_hidden
        grad_normed = dot_nt(grad_hidden, up_w[...])
        sums[2:3, :] += jnp.sum(grad_normed * hat, axis=0, keepdims=True)
        sums[3:4, :] += jnp.sum(grad_normed, axis=0, keepdims=True)
        back = norm_slope(hat, inv, vectors[2:3, :], grad_normed)
        back_third[part, :] = back
        third_low = (upstream.astype(F32) + back).astype(BF)
        grad_third_low[part, :] = third_low
        grad_mixed[part, :] = dot_nt(third_low, out_w[...]).astype(BF)

    each_part(rows, middle)
    flush(1, 2, 3, 4, 5, 6)

    def attend_back_head(h):
        upstream = grad_mixed[:, lanes(h, 0)]
        low = raised_low[h]
        inv = inverse[h]
        up32 = upstream.astype(F32)
        inner = jnp.sum(up32 * mixed[:, lanes(h, 0)], axis=-1, keepdims=True)
        grad_packed[:, lanes(h, 2)] = dot_tn(low, (up32 * inv).astype(BF)).astype(BF)
        grad_weights = dot_nt(upstream, packed[:, lanes(h, 2)])
        spread = (low.astype(F32) * ((grad_weights - inner) * (inv * scale))).astype(BF)
        grad_packed[:, lanes(h, 0)] = dot(spread, packed[:, lanes(h, 1)]).astype(BF)
        grad_packed[:, lanes(h, 1)] = dot_tn(spread, packed[:, lanes(h, 0)]).astype(BF)

    each_head(attend_back_head)
    flush(8)

    def last(part):
        hat, inv = norm_parts(second[part, :].astype(F32))
        grad_normed = dot_nt(grad_packed[part, :width], packed_w[0][...])
        for c in range(1, 3):
            grad_normed += dot_nt(grad_packed[part, c * width : (c + 1) * width], packed_w[c][...])
        sums[0:1, :] += jnp.sum(grad_normed * hat, axis=0, keepdims=True)
        sums[1:2, :] += jnp.sum(grad_normed, axis=0, keepdims=True)
        back = norm_slope(hat, inv, vectors[0:1, :], grad_normed)
        second_add[part, :] = (back_third[part, :] + back).astype(BF)

    each_part(rows, last)
    flush(7, 9)
    blocks = width // 2 // HEAD
    write_halves(
        ((final_active, grad_low), (final_normed, grad_final_hidden), (self_mixed, grad_third_low)),
        ((other_first, 1 - place[0]),), place[1], X_FIRST, blocks, turned,
    )
    flush(10)
    write_halves(
        ((self_normed, grad_packed),), ((other_packed, 1 - place[0]),), place[1], Y_FIRST, blocks, turned
    )


def item_block(place, groups, second, grad_low, vectors, self_packed, self_out, latent_up, latent_down):
    rows, width = second.shape
    low = jax.ShapeDtypeStruct((rows, width), BF)
    half = jax.ShapeDtypeStruct((groups, width // 2, 3 * width // groups), BF)
    packed_parts = [(self_packed, c * width, width) for c in range(3)]
    (
        self_normed, self_mixed, final_normed, final_active, result_add, grad_final_hidden, grad_third_low,
        second_add, grad_packed, sums, other_first, other_packed,
    ) = streamed(
        "item_block",
        item_body,
        place,
        [second, vectors, *packed_parts, self_out, latent_up, latent_down, grad_low],
        [low] * 8
        + [
            jax.ShapeDtypeStruct((rows, 3 * width), BF),
            jax.ShapeDtypeStruct((4, width), F32),
            half,
            half,
        ],
        [
            pltpu.VMEM((rows, 3 * width), BF),
            pltpu.VMEM((HEADS, rows, rows), BF),
            pltpu.VMEM((HEADS, rows, 1), F32),
            pltpu.VMEM((rows, width), F32),
            pltpu.VMEM((rows, width), F32),
            pltpu.VMEM((rows, width), BF),
            pltpu.VMEM((width // 2, rows), BF),
        ],
    )
    return (
        result_add, second_add, self_normed, grad_packed, self_mixed, grad_third_low,
        final_normed, final_active, grad_final_hidden, sums, other_first, other_packed,
    )


def streamed(name, body, place, ins, outs, scratch):
    cuts = [value[1:] if isinstance(value, tuple) else None for value in ins]
    ins = [value[0] if isinstance(value, tuple) else value for value in ins]
    shapes = [
        value.shape if cut is None else value.shape[1:] if len(cut) == 1 else (value.shape[0], cut[1])
        for value, cut in zip(ins, cuts)
    ]
    anywhere = pl.BlockSpec(memory_space=pl.ANY)

    def kernel(place_ref, *refs):
        sources, refs = refs[: len(ins)], refs[len(ins) :]
        targets, refs = refs[: len(outs)], refs[len(outs) :]
        near, refs = refs[: len(ins)], refs[len(ins) :]
        made, refs = refs[: len(outs)], refs[len(outs) :]
        extra, (in_sems, out_sems) = refs[:-2], refs[-2:]
        sources = [
            ref if cut is None else ref.at[cut[0]] if len(cut) == 1 else ref.at[:, pl.ds(*cut)]
            for ref, cut in zip(sources, cuts)
        ]
        loads = [pltpu.make_async_copy(a, b, in_sems.at[i]) for i, (a, b) in enumerate(zip(sources, near))]
        stores = [pltpu.make_async_copy(a, b, out_sems.at[i]) for i, (a, b) in enumerate(zip(made, targets))]
        left_in, left_out = list(range(len(ins))), list(range(len(outs)))
        for load in loads:
            load.start()

        def need(*which):
            for i in which:
                left_in.remove(i)
                loads[i].wait()

        def flush(*which):
            for i in which:
                left_out.remove(i)
                stores[i].start()

        body(place_ref, near, made, extra, need, flush)
        need(*list(left_in))
        flush(*list(left_out))
        for store in stores:
            store.wait()

    return pl.pallas_call(
        kernel,
        in_specs=[pl.BlockSpec(memory_space=pltpu.SMEM)] + [anywhere] * len(ins),
        out_specs=[anywhere] * len(outs),
        out_shape=list(outs),
        scratch_shapes=[pltpu.VMEM(shape, value.dtype) for shape, value in zip(shapes, ins)]
        + [pltpu.VMEM(value.shape, value.dtype) for value in outs]
        + list(scratch)
        + [pltpu.SemaphoreType.DMA((len(ins),)), pltpu.SemaphoreType.DMA((len(outs),))],
        compiler_params=pltpu.CompilerParams(vmem_limit_bytes=60 << 20),
        name=name,
    )(place, *ins)


def pixel_hat(values, cin):
    real = lax.broadcasted_iota(jnp.int32, (values.shape[0], 1), 0) < cin
    portion = 1.0 / cin.astype(F32)
    centre = jnp.where(real, values - jnp.sum(values, axis=0, keepdims=True) * portion, 0.0)
    return centre * lax.rsqrt(jnp.sum(centre * centre, axis=0, keepdims=True) * portion + 1e-05)


def each_block(count, body):
    def step(n, carry):
        body(n)
        return carry

    lax.fori_loop(0, count, step, 0, unroll=4)


def cross_body(place, near, made, extra, need, flush):
    asks, gain, shift, raw, owner, core_out, residual, vectors, up_w, down_w = near
    (
        normal, scores, kept, mixed, top, first_sum, cross_normed, slopes, cross_active, second_sum, second, hats
    ) = made
    (heap,) = extra
    ways, channels, size = normal.shape
    rows = asks.shape[0]
    lat_rows = heap.shape[0]
    at = pl.multiple_of(place[2] * lat_rows, lat_rows)
    large = pl.ds(at, lat_rows)
    need(0, 1, 2, 3)
    columns = lax.broadcasted_iota(jnp.int32, (1, size), 1)
    top[...] = jnp.full(top.shape, -1e30, F32)

    def score(n):
        hat = pixel_hat(raw[n].astype(F32), place[3])
        hats[n] = hat.astype(BF)
        value = (hat * gain[...] + shift[...]).astype(BF)
        normal[n] = value
        places = columns + n * size
        found = dot(asks[large, :], value)
        found = jnp.where((places >= place[0]) & (places < place[1]), found, -1e30)
        scores[n] = found
        top[...] = jnp.maximum(top[...], jnp.max(found, axis=1, keepdims=True))

    each_block(ways, score)
    flush(0, 1, 11)
    need(4)
    edge = jnp.where(
        columns < place[0], normal[0].astype(F32), normal[ways - 1].astype(F32)
    ).astype(BF)
    row_item = lax.broadcasted_iota(jnp.int32, (rows, 1), 0) // lat_rows
    inside = (owner[...] == row_item) & (place[2] != row_item)
    found = jnp.where(inside, dot(asks[...], edge), -1e30)
    raised = jnp.exp(found - jnp.max(found, axis=1, keepdims=True))
    weights = raised * (1.0 / jnp.sum(raised, axis=1, keepdims=True))
    weights = jnp.where(inside, weights, 0.0).astype(BF)
    kept[...] = weights
    mixed[...] = dot_nt(weights, edge)
    heap[...] = jnp.zeros(heap.shape, F32)
    peak = top[...]

    def gather(n, carry):
        raised = jnp.exp(scores[n] - peak)
        heap[...] += dot_nt(raised.astype(BF), normal[n])
        return carry + jnp.sum(raised, axis=1, keepdims=True)

    whole = lax.fori_loop(0, ways, gather, jnp.zeros((lat_rows, 1), F32))
    mixed[large, :] = heap[...] * (1.0 / whole)
    top[...] = peak + jnp.log(whole)
    flush(2, 3, 4)
    need(5, 6, 7, 8, 9)

    def net(part):
        first = residual[part, :] + dot(mixed[part, :].astype(BF), core_out[...])
        first_sum[part, :] = first
        hat, unused = norm_parts(first)
        normed = (hat * vectors[0:1, :] + vectors[1:2, :]).astype(BF)
        cross_normed[part, :] = normed
        active, slope = gelu_both(dot(normed, up_w[...]))
        active = active.astype(BF)
        cross_active[part, :] = active
        slopes[part, :] = slope
        value = first + dot(active, down_w[...])
        second_sum[part, :] = value
        second[part, :] = value.astype(BF)

    each_part(rows, net)


def cross_back_body(place, near, made, extra, need, flush):
    (
        got, upstream, slopes, down_w, up_w, first_sum, vectors, core_out, normal, mixed, kept, asks, scores, top,
        hats, value_w, cross_active, cross_normed, *latent_side,
    ) = near
    grad, corner, heap, turned, *small_scratch = extra
    if not latent_side:
        (
            grad_second_low, grad_cross_hidden, grad_first, grad_first_low, sums, moves, pix, pixel_sums,
            core_value, cross_mixed,
        ) = made
    else:
        grad_second_low, grad_cross_hidden, grad_first_low, moves, pixel_sums, sums, grad_first, cross_mixed = (
            small_scratch[:8]
        )
        pix, grad_latents, small_mine, small_other, *halves = made
    ways, channels, size = normal.shape
    rows = asks.shape[0]
    lat_rows = heap.shape[0]
    at = pl.multiple_of(place[2] * lat_rows, lat_rows)
    large = pl.ds(at, lat_rows)
    sums[...] = jnp.zeros(sums.shape, F32)
    pixel_sums[...] = jnp.zeros(pixel_sums.shape, F32)
    need(0, 1, 2, 3, 4, 5, 6, 7)

    def net(part):
        grad_second = upstream[part, :] + got[part, :].astype(F32)
        low = grad_second.astype(BF)
        grad_second_low[part, :] = low
        grad_hidden = (dot_nt(low, down_w[...]) * slopes[part, :]).astype(BF)
        grad_cross_hidden[part, :] = grad_hidden
        grad_normed = dot_nt(grad_hidden, up_w[...])
        hat, inv = norm_parts(first_sum[part, :])
        sums[0:1, :] += jnp.sum(grad_normed * hat, axis=0, keepdims=True)
        sums[1:2, :] += jnp.sum(grad_normed, axis=0, keepdims=True)
        value = grad_second + norm_slope(hat, inv, vectors[0:1, :], grad_normed)
        grad_first[part, :] = value
        low = value.astype(BF)
        grad_first_low[part, :] = low
        grad[part, :] = dot_nt(low, core_out[...]).astype(BF)

    each_part(rows, net)
    if not latent_side:
        flush(0, 1, 2, 3, 4)
    need(8, 9, 10, 11, 12, 13, 14)
    columns = lax.broadcasted_iota(jnp.int32, (1, size), 1)
    early = columns < place[0]
    edge = jnp.where(early, normal[0].astype(F32), normal[ways - 1].astype(F32)).astype(BF)
    deltas = jnp.sum(grad[...].astype(F32) * mixed[...], axis=1, keepdims=True)
    weights = kept[...]
    spread = (weights.astype(F32) * (dot(grad[...], edge) - deltas)).astype(BF)
    moves[...] = dot_nt(spread, edge).astype(BF)
    corner[...] = dot_tn(asks[...], spread) + dot_tn(grad[...], weights)
    heap[...] = jnp.zeros(heap.shape, F32)
    own = grad[large, :]
    own_asks = asks[large, :]
    deltas = jnp.sum(own.astype(F32) * mixed[large, :], axis=1, keepdims=True)
    level = top[...]

    def block(n):
        value = normal[n]
        weights = jnp.exp(scores[n] - level)
        spread = (weights * (dot(own, value) - deltas)).astype(BF)
        heap[...] += dot_nt(spread, value)
        part = dot_tn(own_asks, spread) + dot_tn(own, weights.astype(BF))
        use = ((n == 0) & early) | ((n == ways - 1) & jnp.logical_not(early))
        part = part + jnp.where(use, corner[...], 0.0)
        pix[n] = part.astype(BF)
        hat = hats[n].astype(F32)
        pixel_sums[0] += jnp.sum(part * hat, axis=1, keepdims=True)
        pixel_sums[1] += jnp.sum(part, axis=1, keepdims=True)

    each_block(ways, block)
    moves[large, :] = heap[...].astype(BF)
    if latent_side:
        flush(0)
    else:
        flush(5, 6, 7)
    need(15, 16, 17)
    mixed_low = mixed[...].astype(BF)
    cross_mixed[...] = dot(mixed_low, value_w[...]).astype(BF)
    core_low = dot_tn(mixed_low, grad_first_low[...]).astype(BF)
    if not latent_side:
        core_value[...] = core_low
        return
    write_halves(
        ((cross_active, grad_second_low), (cross_normed, grad_cross_hidden)),
        ((halves[0], place[4]), (halves[1], 1 - place[4])), place[5], X_FIRST, ways // 2, turned,
    )
    write_halves(
        ((cross_mixed, grad_first_low),),
        ((halves[2], place[4]), (halves[3], 1 - place[4])), place[5], Y_FIRST, ways // 2, turned,
    )
    flush(4, 5, 6, 7)
    core_in, residual, gain_row, out_w, normed, queries, item_sums = latent_side
    need(18, 19, 20, 21, 22, 23, 24)
    small_parts(
        place[4], place[5], moves, core_in, residual, grad_first, gain_row, core_low, out_w, normed, queries,
        sums, item_sums, pixel_sums, grad_latents, small_mine, small_other, *small_scratch[8:],
    )


def cross(place, raw_all, gain, shift, asks, owner, residual, core_out, vectors, up, down, lat_rows):
    ways, channels, size = raw_all.shape
    rows, width = residual.shape
    low = jax.ShapeDtypeStruct((rows, width), BF)
    wide = jax.ShapeDtypeStruct((rows, width), F32)
    (
        normal, scores, kept, mixed, top, first_sum, cross_normed, slopes, cross_active, second_sum, second, hats
    ) = streamed(
        "cross",
        cross_body,
        place,
        [asks, gain, shift, raw_all, owner, core_out, residual, vectors, up, down],
        [
            jax.ShapeDtypeStruct((ways, channels, size), BF),
            jax.ShapeDtypeStruct((ways, lat_rows, size), F32),
            jax.ShapeDtypeStruct((rows, size), BF),
            jax.ShapeDtypeStruct((rows, channels), F32),
            jax.ShapeDtypeStruct((lat_rows, 1), F32),
            wide,
            low,
            wide,
            low,
            wide,
            low,
            jax.ShapeDtypeStruct((ways, channels, size), BF),
        ],
        [pltpu.VMEM((lat_rows, channels), F32)],
    )
    return (
        mixed, kept, scores, top, normal, first_sum, second_sum, second, cross_normed, cross_active, slopes, hats
    )


def cross_back(
    place, got, upstream, first_sum, slopes, vectors, core_out, up, down,
    hats, normal, asks, mixed, kept, scores, top, cross_active, cross_normed, value_w, latent_side, groups,
):
    ways, channels, size = hats.shape
    rows, width = upstream.shape
    lat_rows = top.shape[0]
    shape = jax.ShapeDtypeStruct
    low, wide = shape((rows, width), BF), shape((rows, width), F32)
    scratch = [
        pltpu.VMEM((rows, channels), BF),
        pltpu.VMEM((channels, size), F32),
        pltpu.VMEM((lat_rows, channels), F32),
        pltpu.VMEM((width // 2, rows), BF),
    ]
    moves, pixel_sums, sums = shape((rows, channels), BF), shape((2, channels, 1), F32), shape((2, width), F32)
    pix = shape((ways, channels, size), BF)
    if latent_side:
        total = small_lines(channels)
        small = shape((4, ways // 4 * (total // 4), 2 * width // ways), BF)
        outs = [pix, wide, small, small] + [
            shape((groups, width // 2, count * width // groups), BF) for count in (2, 2, 1, 1)
        ]
        inner = [low, low, low, moves, pixel_sums, sums, wide, low, shape((16, width), F32), shape((total, width), BF)]
        scratch += [pltpu.VMEM(value.shape, value.dtype) for value in inner]
    else:
        outs = [low, low, wide, low, sums, moves, pix, pixel_sums, shape((channels, width), BF), low]
    return streamed(
        "cross_back",
        cross_back_body,
        place,
        [
            got, upstream, slopes, down, up, first_sum, vectors, core_out, normal, mixed, kept, asks, scores, top,
            hats, value_w, cross_active, cross_normed, *latent_side,
        ],
        outs,
        scratch,
    )


def second_hop_body(place, near, made, extra, need, flush):
    for at, out in enumerate(made):
        need(3 * at, 3 * at + 1, 3 * at + 2)
        value = near[3 * at][...].astype(F32) + near[3 * at + 1][...].astype(F32)
        out[...] = (value + near[3 * at + 2][...].astype(F32)).astype(BF)
        flush(at)


def pieces_body(place, near, made, extra, need, flush):
    sums, every = extra[:3], extra[3]
    chips, unused, block = every.shape
    for at, here in enumerate(sums):
        need(*range(4 * at, 4 * at + 4))
        value = near[4 * at][...].astype(F32)
        for k in range(1, 4):
            value = value + near[4 * at + k][...].astype(F32)
        here[...] = value.astype(BF)
    lines = sums[2].shape[0] // (chips // 2)
    for z in range(chips):
        at = 0
        for here in sums[:2]:
            for k in range(here.shape[1] // block):
                every[z, at : at + block, :] = here[z * block : (z + 1) * block, k * block : (k + 1) * block]
                at += block
        every[z, at:, :] = sums[2][
            z // 2 * lines : (z // 2 + 1) * lines, z % 2 * block : (z % 2 + 1) * block
        ]
    for m, out in enumerate(made):
        out[...] = every[place[0] ^ m]
        flush(m)


def second_hop(flows, first_got):
    ins = []
    for (mine, got, unused), first in zip(flows, first_got):
        ins += [(mine, 3), (got, 3), (first, 1)]
    return streamed(
        "second_hop",
        second_hop_body,
        jnp.zeros((1,), jnp.int32),
        ins,
        [jax.ShapeDtypeStruct(mine.shape[1:], BF) for mine, unused, hop in flows],
        [],
    )


def pieces_of(chip, chips, block, flows, first_got, hops):
    ins = []
    for (mine, got, unused), first, last in zip(flows, first_got, hops):
        ins += [(mine, 2), (got, 2), (first, 0), last]
    shapes = [mine.shape[1:] for mine, unused, hop in flows]
    lines = sum(shape[1] for shape in shapes[:2]) + shapes[2][0] // (chips // 2)
    return streamed(
        "pieces",
        pieces_body,
        chip.astype(jnp.int32).reshape(1),
        ins,
        [jax.ShapeDtypeStruct((lines, block), BF)] * chips,
        [pltpu.VMEM(shape, BF) for shape in shapes] + [pltpu.VMEM((chips, lines, block), BF)],
    )


def finish_body(place, near, made, extra, need, flush):
    parts, key_w = near[:4], near[4]
    net_down, net_up, out_weight, query, key, value, pixel_gain, pixel_shift, *gains = made
    every, small = extra
    block = parts[0].shape[1]
    channels, width = key_w.shape
    quarter = width // 4
    tiles = quarter // block
    size = small.shape[0] // 4
    for m in range(4):
        need(m)
        every[m] = parts[m][...]
    for j in range(4):
        m = place[0] ^ j
        small[j * size : (j + 1) * size, :] = every[m, 3 * quarter // block * block :, :]
        for at, out in enumerate((net_down, net_up, out_weight)):
            for k in range(tiles):
                lines = (at * tiles + k) * block
                out[:, j * quarter + k * block : j * quarter + (k + 1) * block] = every[
                    m, lines : lines + block, :
                ].astype(F32)
    flush(0, 1, 2)
    need(4)
    scale = 1.0 / math.sqrt(width)
    query[...] = dot_tn(small[channels : 2 * channels, :], key_w[...]) * scale
    cin = key.shape[0]
    value[...] = small[:channels, :].astype(F32)[:cin]
    key[...] = small[2 * channels : 3 * channels, :].astype(F32)[:cin] * scale
    vectors = small[3 * channels :, :].astype(F32)
    count = -(-channels // block)
    for at, out in enumerate((pixel_gain, pixel_shift)):
        line = [vectors[2 + at * count + k : 3 + at * count + k, :] for k in range(count)]
        out[...] = jnp.concatenate(line, axis=1)[0, :cin]
    for at, out in enumerate(gains):
        line = at if at < 2 else 2 * count + at
        out[...] = vectors[line]


def finish(item, parts, key_w, cin):
    lines, block = parts[0].shape
    channels, width = key_w.shape
    shape = jax.ShapeDtypeStruct
    total = small_lines(channels)
    tall, flat = shape((block, width), F32), shape((cin, block), F32)
    return streamed(
        "finish",
        finish_body,
        item.astype(jnp.int32).reshape(1),
        [*parts, key_w],
        [tall, tall, tall, tall, flat, flat] + [shape((cin,), F32)] * 2 + [shape((block,), F32)] * 8,
        [pltpu.VMEM((4, lines, block), BF), pltpu.VMEM((total, block), BF)],
    )


def on_device(
    latents,
    pixels,
    lengths,
    out_grad,
    latent_gain,
    latent_shift,
    pixel_gain,
    pixel_shift,
    query_weight,
    key_weight,
    value_weight,
    out_weight,
    cross_gain,
    cross_shift,
    cross_up,
    cross_down,
    self_gain,
    self_shift,
    self_packed,
    self_out,
    final_gain,
    final_shift,
    latent_up,
    latent_down,
):
    items = latents.shape[1]
    lat_rows = latents.shape[2]
    width = latents.shape[3]
    pix_rows = pixels.shape[1]
    cin = pixels.shape[2]
    ways = lax.axis_size("lat")
    groups = lax.axis_size("items")
    sub = ways // items
    rows = items * lat_rows
    piece = lat_rows // sub
    score_scale = 1.0 / math.sqrt(width)
    head_scale = 1.0 / math.sqrt(HEAD)
    lat_index = lax.axis_index("lat")
    core = lat_index % 2

    channels = -(-cin // 16) * 16
    pad = ((0, channels - cin), (0, 0))
    spans = lengths[0]
    starts = jnp.cumsum(spans) - spans
    largest = jnp.argmax(spans).astype(jnp.int32)
    large_start = starts[largest]
    place = jnp.stack(
        [
            large_start,
            large_start + spans[largest],
            largest,
            jnp.asarray(cin, jnp.int32),
            core,
            lax.axis_index("items"),
        ]
    ).astype(jnp.int32)
    edge_places = jnp.arange(pix_rows, dtype=jnp.int32)
    edge_places = jnp.where(edge_places < large_start, edge_places, edge_places + pix_rows * (ways - 1))
    owner = jnp.sum((edge_places[None, :] >= starts[:, None]).astype(jnp.int32), axis=0) - 1
    owner = owner[None, :]

    swap = [(i, i ^ 1) for i in range(ways)]
    same_core = [list(range(0, ways, 2)), list(range(1, ways, 2))]
    block = width // ways

    tie = lax.optimization_barrier

    chips = ways // 2
    chip = lat_index // 2
    item = lax.axis_index("items")

    def swap_items(part, m):
        return lax.ppermute(part, "items", [(i, i ^ m) for i in range(groups)])

    def near_chips(pieces):
        if chips != 4:
            whole = jnp.stack([pieces(j) for j in range(chips)])
            moved = lax.all_to_all(
                whole, "lat", split_axis=0, concat_axis=0, tiled=True, axis_index_groups=same_core
            )
            return [moved[j] for j in range(chips)]
        return [pieces(chip)] + [
            lax.ppermute(
                pieces(chip ^ m), "lat", [(i, ((i // 2) ^ m) * 2 + i % 2) for i in range(ways)]
            )
            for m in range(1, chips)
        ]

    def total(parts):
        value = parts[0].astype(F32)
        for part in parts[1:]:
            value = value + part.astype(F32)
        return value

    def add(left, right):
        return (left.astype(F32) + right.astype(F32)).astype(BF)

    def over_chips_whole(here):
        parts = lax.all_to_all(
            here, "lat", split_axis=0, concat_axis=0, tiled=True, axis_index_groups=same_core
        )
        return jnp.sum(parts.astype(F32), axis=0).astype(BF)

    def gather_items(part):
        return jnp.stack([part] + [swap_items(part, m) for m in range(1, groups)])

    def by_item(parts):
        return [lax.dynamic_index_in_dim(parts, item ^ j, 0, keepdims=False) for j in range(groups)]

    def weight_of(parts):
        return jnp.concatenate(by_item(parts), axis=1).astype(F32)

    pixels_low = jnp.pad(pixels[0].T, pad)
    raw_all = lax.all_gather(pixels_low, "lat", axis=0, tiled=False)
    gain_column = jnp.pad(pixel_gain[:, None], pad)
    shift_column = jnp.pad(pixel_shift[:, None], pad)
    key_pad = jnp.pad(key_weight, pad)
    value_pad = jnp.pad(value_weight, pad)

    to_pixels = (dot_nt(query_weight, key_pad) * score_scale).astype(BF)
    from_pixels = dot(value_pad, out_weight).astype(BF)

    residual = latents.reshape(rows, width)
    upstream = out_grad.reshape(rows, width)
    normed = layer_norm(residual, latent_gain, latent_shift).astype(BF)
    asks = dot(normed, to_pixels).astype(BF)
    latent_queries = dot(normed, query_weight).astype(BF)

    def reshare(values):
        moved = lax.all_to_all(
            values.reshape(ways, piece, width), "lat", split_axis=0, concat_axis=0, tiled=True
        )
        return moved.reshape(rows, width)

    (
        raw_all, value_pad, upstream_low, asks, latent_queries, from_pixels, to_pixels, gain_column, shift_column, place, owner
    ) = tie(
        (
            raw_all, value_pad, upstream.astype(BF), asks, latent_queries, from_pixels, to_pixels, gain_column, shift_column,
            place, owner,
        )
    )
    grad_low = reshare(upstream_low)
    cross_vectors = jnp.stack([cross_gain, cross_shift])
    (
        mixed, kept, scores, top, normal, first_sum, second_sum, second, cross_normed, cross_active, slopes,
        hats,
    ) = cross(
        place, raw_all, gain_column, shift_column, asks, owner, residual, from_pixels, cross_vectors,
        cross_up, cross_down, lat_rows,
    )
    second, grad_low = tie((second, grad_low))
    second = reshare(second)
    item_place = jnp.stack([core, item]).astype(jnp.int32)
    item_vectors = jnp.stack([self_gain, self_shift, final_gain, final_shift])
    if sub == 1:
        (
            result_add, second_add, self_normed, grad_packed, self_mixed, grad_third_low,
            final_normed, final_active, grad_final_hidden, item_sums, final_other, packed_other,
        ) = item_block(item_place, groups, second, grad_low, item_vectors, self_packed, self_out, latent_up, latent_down)
    else:
        whole_rows = rows * sub
        same_item = [[i * sub + s for s in range(sub)] for i in range(items)]
        second_wide = second.astype(F32)
        self_normed = layer_norm(second_wide, self_gain, self_shift).astype(BF)
        packed = dot(self_normed, self_packed).astype(BF)
        pairs = lax.all_gather(
            packed[:, width:], "lat", axis=0, tiled=True, axis_index_groups=same_item
        )
        self_mixed, self_low = attend(packed, pairs, rows, whole_rows)
        self_add = dot(self_mixed, self_out)
        third = second_wide + self_add
        final_normed = layer_norm(third, final_gain, final_shift).astype(BF)
        final_hidden = dot(final_normed, latent_up)
        final_active = jax.nn.gelu(final_hidden).astype(BF)
        result_add = (self_add + dot(final_active, latent_down)).astype(BF)
        grad_final_hidden = gelu_back(final_hidden, dot_nt(grad_low, latent_down)).astype(BF)
        back_third, grad_final_gain, grad_final_shift = norm_back(
            third, final_gain, dot_nt(grad_final_hidden, latent_up)
        )
        grad_third_low = (grad_low.astype(F32) + back_third).astype(BF)
        grad_mixed = dot_nt(grad_third_low, self_out).astype(BF)
        grad_queries, grad_pairs = attend_back(grad_mixed, self_low, packed, pairs, rows, whole_rows)
        grad_pairs = lax.psum_scatter(
            grad_pairs, "lat", scatter_dimension=0, tiled=True, axis_index_groups=same_item
        )
        grad_packed = jnp.concatenate([grad_queries, grad_pairs], axis=1)
        back_second, grad_self_gain, grad_self_shift = norm_back(
            second_wide, self_gain, dot_nt(grad_packed, self_packed)
        )
        second_add = (back_third + back_second).astype(BF)
        item_sums = jnp.stack([grad_self_gain, grad_self_shift, grad_final_gain, grad_final_shift])
    second_got = reshare(second_add)
    item_pairs = (
        (final_active, grad_low),
        (final_normed, grad_final_hidden),
        (self_mixed, grad_third_low),
        (self_normed, grad_packed),
    )
    final_pairs, packed_pairs = item_pairs[:3], item_pairs[3:]
    if sub > 1:
        final_other = half_plain(final_pairs, 1 - core, item, X_FIRST, ways).astype(BF)
        packed_other = half_plain(packed_pairs, 1 - core, item, Y_FIRST, ways).astype(BF)
    final_got = lax.ppermute(final_other, "lat", swap)
    packed_got = lax.ppermute(packed_other, "lat", swap)
    final_parts = half_grads(final_pairs, core, item, X_FIRST, ways, final_got)
    packed_parts = list(half_grads(packed_pairs, core, item, Y_FIRST, ways, packed_got, True))
    final_got, packed_got = [None, swap_items(final_parts[1], 1)], [None, swap_items(packed_parts[1], 2)]
    second_got, result_add, final_got[1], packed_got[1] = tie(
        (second_got, result_add, final_got[1], packed_got[1])
    )
    final_got[0], packed_got[0] = swap_items(final_parts[0], 1), swap_items(packed_parts[0], 2)
    packed_low = swap_items(packed_parts.pop(2), 2)
    final_kept, packed_kept = final_parts[2:], packed_parts[2:]
    result_got = reshare(result_add)

    back_args = (
        place, second_got, upstream, first_sum, slopes, cross_vectors, from_pixels, cross_up, cross_down,
        hats, normal, asks, mixed, kept, scores, top, cross_active, cross_normed, value_pad,
    )
    if block % 128 == 0:
        latent_side = (
            to_pixels, residual, latent_gain[None], out_weight, normed, latent_queries, item_sums
        )
        (
            parts_pix, grad_latents, small_mine, small_other, net_mine, net_other, out_mine, out_other
        ) = cross_back(*back_args, latent_side, groups)
    else:
        (
            grad_second_low, grad_cross_hidden, grad_first, grad_first_low, cross_sums, moves, parts_pix, pixel_sums,
            core_value, cross_mixed,
        ) = cross_back(*back_args, (), groups)
        cross_pairs = ((cross_active, grad_second_low), (cross_normed, grad_cross_hidden))
        net_mine, net_other, out_mine, out_other = [
            half_plain(pairs, half, item, order, ways).astype(BF)
            for pairs, order in ((cross_pairs, X_FIRST), (((cross_mixed, grad_first_low),), Y_FIRST))
            for half in (core, 1 - core)
        ]
        grad_latents, small_mine, small_other = last_block(
            core, item, ways, moves, to_pixels, residual, grad_first, latent_gain[None], core_value, out_weight,
            normed, latent_queries, jnp.concatenate([cross_sums, item_sums, jnp.zeros((2, width), F32)]), pixel_sums,
        )
    (
        parts_pix, grad_latents, small_mine, small_other, net_mine, net_other, out_mine, out_other,
        final_got[0], packed_got[0], packed_low, result_got,
    ) = tie(
        (
            parts_pix, grad_latents, small_mine, small_other, net_mine, net_other, out_mine, out_other,
            final_got[0], packed_got[0], packed_low, result_got,
        )
    )
    grad_pn = lax.psum_scatter(parts_pix, "lat", scatter_dimension=0, tiled=False)
    packed_got[1] = jnp.concatenate([packed_got[1], packed_low])
    net_got = lax.ppermute(net_other, "lat", swap)
    out_got = lax.ppermute(out_other, "lat", swap)
    final_two, packed_two = add(final_kept[1], final_got[1]), add(packed_kept[1], packed_got[1])
    final_two, packed_two = swap_items(final_two, 2), swap_items(packed_two, 1)
    small_got = lax.ppermute(small_other, "lat", swap)
    net_first, out_first = add(net_mine[:2], net_got[:2]), add(out_mine[:2], out_got[:2])
    small_first = add(small_mine[:2], small_got[:2])
    final_two, packed_two, net_first, out_first, small_first = tie(
        (final_two, packed_two, net_first, out_first, small_first)
    )
    first_got = [swap_items(net_first, 1), swap_items(out_first, 2), swap_items(small_first, 2)]
    item_here = jnp.concatenate(
        [
            total([final_kept[0], final_got[0], final_two]).astype(BF),
            total([packed_kept[0], packed_got[0], packed_two]).astype(BF),
        ],
        axis=1,
    )
    first_got = tie(tuple(first_got))
    item_part = over_chips_whole(item_here.reshape(chips, block, -1))
    flows = ((net_mine, net_got, 2), (out_mine, out_got, 1), (small_mine, small_got, 1))
    fast = block % 128 == 0 and chips == 4
    if fast:
        hops = second_hop(flows, first_got)
    else:
        hops = [
            total([mine[3], got[3], first[1]]).astype(BF)
            for (mine, got, hop), first in zip(flows, first_got)
        ]
    hops = [swap_items(part, hop) for part, (mine, got, hop) in zip(hops, flows)]
    if fast:
        pieces = pieces_of(chip, chips, block, flows, first_got, hops)
        item_part, grad_pn, *pieces = tie((item_part, grad_pn, *pieces))
        rest = [pieces[0]] + [
            lax.ppermute(
                pieces[m], "lat", [(i, ((i // 2) ^ m) * 2 + i % 2) for i in range(ways)]
            )
            for m in range(1, chips)
        ]
    else:
        item_part, grad_pn, *hops = tie((item_part, grad_pn, *hops))
        net_here, out_here, small_here = [
            total([mine[2], got[2], first[0], last]).astype(BF)
            for (mine, got, hop), first, last in zip(flows, first_got, hops)
        ]
        lines = small_here.shape[0] // (chips // 2)
        pieces = jnp.stack(
            [
                jnp.concatenate(
                    [
                        whole[z * block : (z + 1) * block, k * block : (k + 1) * block]
                        for whole in (net_here, out_here)
                        for k in range(whole.shape[1] // block)
                    ]
                    + [small_here[z // 2 * lines : (z // 2 + 1) * lines, z % 2 * block : (z % 2 + 1) * block]]
                )
                for z in range(chips)
            ]
        )
        rest = near_chips(lambda z: lax.dynamic_index_in_dim(pieces, z, 0, keepdims=False))
    item_parts = [item_part] + [swap_items(item_part, m) for m in range(1, groups - 1)]
    rest = list(rest)
    late_part, rest[1] = tie((item_part, rest[1]))
    tied = tie((*rest, *item_parts))
    item_parts = jnp.stack([*tied[len(rest) :], swap_items(late_part, groups - 1)])
    rest = total(tied[: len(rest)]).astype(BF)
    quarter = width // groups
    grad_latent_down, grad_latent_up, grad_self_out = [
        weight_of(item_parts[:, :, at * quarter : (at + 1) * quarter]) for at in range(3)
    ]
    grad_self_packed = weight_of(item_parts[:, :, 3 * quarter :])
    result = second_sum + result_got.astype(F32)
    grad_pn = grad_pn.astype(F32)[:cin]
    pix_hat, pix_inv = norm_parts(pixels[0].T.astype(F32), 0)
    scaled = grad_pn * pixel_gain[:, None]
    grad_pixels = pix_inv * (
        scaled
        - jnp.mean(scaled, axis=0, keepdims=True)
        - pix_hat * jnp.mean(scaled * pix_hat, axis=0, keepdims=True)
    )
    rest_parts = [rest] + [swap_items(rest, m) for m in range(1, groups)]
    if block % 128 == 0:
        (
            grad_cross_down, grad_cross_up, grad_out_weight, grad_query_weight, grad_key_weight, grad_value_weight,
            *vectors,
        ) = finish(item, rest_parts, key_pad, cin)
        grad_pixel_gain, grad_pixel_shift, *gains = [value.reshape(-1) for value in vectors]
    else:
        rest_parts = jnp.stack(rest_parts)
        tall = quarter // block * block
        grad_cross_down, grad_cross_up, grad_out_weight = [
            weight_of(
                rest_parts[:, at * tall : (at + 1) * tall]
                .reshape(groups, quarter // block, block, block)
                .transpose(0, 2, 1, 3)
                .reshape(groups, block, quarter)
            )
            for at in range(3)
        ]
        small = jnp.concatenate(by_item(rest_parts[:, 3 * tall :]), axis=0).astype(F32)
        grad_query_weight = dot_tn(small[channels : 2 * channels].astype(BF), key_pad) * score_scale
        grad_key_weight = small[2 * channels : 2 * channels + cin] * score_scale
        grad_value_weight = small[:cin]
        head = small[3 * channels : 3 * channels + 2]
        sums = small[3 * channels + 2 :]
        count = -(-channels // block)
        grad_pixel_gain = sums[:count].reshape(-1)[:cin]
        grad_pixel_shift = sums[count : 2 * count].reshape(-1)[:cin]
        gains = [head[0], head[1]] + [sums[2 * count + at] for at in range(6)]
    shape = (1, items, lat_rows, width)
    return (
        result.reshape(shape),
        grad_latents.reshape(shape),
        grad_pixels.T[None],
        gains[0],
        gains[1],
        grad_pixel_gain,
        grad_pixel_shift,
        grad_query_weight,
        grad_key_weight,
        grad_value_weight,
        grad_out_weight,
        gains[2],
        gains[3],
        grad_cross_up,
        grad_cross_down,
        gains[4],
        gains[5],
        grad_self_packed,
        grad_self_out,
        gains[6],
        gains[7],
        grad_latent_up,
        grad_latent_down,
    )


def solution(mesh):
    rows = P("items", None, "lat", None)
    in_specs = (rows, P("items", "lat", None), P("items", None), rows) + (P(),) * 20
    lane = P("lat")
    tall = P("lat", None)
    wide = P(None, "lat")
    out_specs = (
        rows,
        rows,
        P("items", "lat", None),
        lane,
        lane,
        P(),
        P(),
        tall,
        wide,
        wide,
        tall,
        lane,
        lane,
        tall,
        tall,
        lane,
        lane,
        tall,
        tall,
        lane,
        lane,
        tall,
        tall,
    )
    return jax.shard_map(
        on_device, mesh=mesh, in_specs=in_specs, out_specs=out_specs, check_vma=False
    )
```
